32 devices in a mesh: dp: 4 (over y, x), row: 2 (over core), col: 4 (over z).
Axes of the slice: x: 2, y: 2, z: 4, core: 2. Of those that a mesh axis runs over, the one named last changes fastest.
Arguments:
- tokens: bfloat16 [2048, 1024], P(('dp', 'row'), 'col'), may hold values from -6 to 6
- segment: int32 [2048], P('dp'), may hold values from -1 to 1, as said below
- ln_gain: float32 [2, 1024], P(None, 'col'), may hold values from 0.5 to 1.5
- ln_bias: float32 [2, 1024], P(None, 'col'), may hold values from -1.5 to 1.5
- w_qkv: bfloat16 [3, 1024, 1024], P(None, 'col', 'row'), may hold values from -0.1875 to 0.1875
- b_qv: float32 [2, 1024], P(None, ('row', 'col')), may hold values from -1.5 to 1.5
- w_out: bfloat16 [1024, 1024], P('row', 'col'), may hold values from -1.5 to 1.5
- b_out: float32 [1024], P('col'), may hold values from -1.5 to 1.5
- w_fc: bfloat16 [1024, 4096], P('col', 'row'), may hold values from -0.1875 to 0.1875
- b_fc: float32 [4096], P(('row', 'col')), may hold values from -1.5 to 1.5
- w_proj: bfloat16 [4096, 1024], P('row', 'col'), may hold values from -0.09375 to 0.09375
- b_proj: float32 [1024], P('col'), may hold values from -1.5 to 1.5
- cotangent: bfloat16 [2048, 1024], P(('dp', 'row'), 'col'), may hold values from -6 to 6
Outputs:
- mixed: bfloat16 [2048, 1024], P(('dp', 'row'), 'col')
- grad_tokens: float32 [2048, 1024], P(('dp', 'row'), 'col')
- grad_ln_gain: float32 [2, 1024], P(None, 'col')
- grad_ln_bias: float32 [2, 1024], P(None, 'col')
- grad_w_qkv: float32 [3, 1024, 1024], P(None, 'col', 'row')
- grad_b_qv: float32 [2, 1024], P(None, ('row', 'col'))
- grad_w_out: float32 [1024, 1024], P('row', 'col')
- grad_b_out: float32 [1024], P('col')
- grad_w_fc: float32 [1024, 4096], P('col', 'row')
- grad_b_fc: float32 [4096], P(('row', 'col'))
- grad_w_proj: float32 [4096, 1024], P('row', 'col')
- grad_b_proj: float32 [1024], P('col')
The draws below stay inside these ranges and needn't reach their ends.
Inputs may be any that keep to these rules, and one draw needn't show every extreme that they name: `segment`: in every group of 512 slots, sequence 0 starts at the group's first slot and covers more than half of it, sequence 1 follows it, and -1 marks the empty slots at the end. Some group is filled by one sequence of 512 slots; every other group holds two sequences and some empty slots.
All inputs are finite; a program needn't handle non-finite values.
Results may differ from the reference program's by a relative error of at most 0.014.
Values may be sent and summed in bfloat16 or wider, within the bound.
No kernel may reach another device: no remote copies, remote signals or barrier semaphores. Data moves between devices by JAX's collectives and lax.ppermute only.
A program may use at most 64 MiB of HBM per device.

```python
import math
import jax
import jax.numpy as jnp
from jax import lax

D = 1024
HEADS = 16
FF = 4096
GRP_TOK = 512
HEAD_DIM = 64
TOKENS = 2048


def draw_segment(key, part):
    key = jax.random.fold_in(key, 7)
    groups = TOKENS // GRP_TOK
    key_first, key_second, key_full = jax.random.split(key, 3)
    halfway = GRP_TOK // 2
    first_len = jax.random.randint(key_first, (groups,), halfway + 1, GRP_TOK - 1)
    room = GRP_TOK - 1 - first_len
    second_len = jax.random.randint(key_second, (groups,), 1, room + 1)
    full_group = jax.random.randint(key_full, (), 0, groups)
    is_full = jnp.arange(groups) == full_group
    first_len = jnp.where(is_full, GRP_TOK, first_len)
    second_len = jnp.where(is_full, 0, second_len)
    places = jnp.arange(GRP_TOK)[None, :]
    ends = (first_len + second_len)[:, None]
    ids = jnp.where(places < first_len[:, None], 0, jnp.where(places < ends, 1, -1))
    return ids.reshape(-1).astype(jnp.int32)


def steps_of(own_key, dims, pieces, smallest, top_value):
    level = 1.0
    for dim, blocks in pieces:
        draws = jax.random.uniform(jax.random.fold_in(jax.random.fold_in(own_key, 6), dim), (blocks,), jnp.float32, smallest / len(pieces), top_value / len(pieces))
        level = level * jnp.repeat(jnp.exp(draws), dims[dim] // blocks).reshape((-1,) + (1,) * (len(dims) - 1 - dim))
    return level


def centred(own_key, shape, deviation, bound, cuts=(), held_as=jnp.bfloat16):
    loudness = steps_of(own_key, shape, cuts, -0.22, 0.18) if cuts else 1.0
    drawn = jax.random.normal(own_key, shape, jnp.float32) * deviation * loudness
    return jnp.minimum(jnp.maximum(drawn, -bound), bound).astype(held_as)


def setup_inputs(seed: int = 0) -> dict:
    key_list = jax.random.split(jax.random.key(seed), 14)
    tokens = centred(key_list[0], (TOKENS, D), 1.0, 6.0, ((0, 8), (1, 4)))
    segment = draw_segment(jax.random.fold_in(key_list[13], 71), 0)
    ln_gain = jnp.clip(1.0 + 0.1 * jax.random.normal(key_list[2], (2, D), jnp.float32), 0.5, 1.5)
    ln_bias = centred(key_list[3], (2, D), 0.3, 1.5, ((1, 4),), jnp.float32)
    w_qkv = centred(key_list[4], (3, D, D), D ** -0.5, 0.1875, ((1, 4), (2, 2)))
    b_qv = centred(key_list[5], (2, D), 0.3, 1.5, ((1, 8),), jnp.float32)
    w_out = centred(key_list[6], (D, D), 16 ** -0.5, 1.5, ((0, 2), (1, 4)))
    b_out = centred(key_list[7], (D,), 0.3, 1.5, ((0, 4),), jnp.float32)
    w_fc = centred(key_list[8], (D, FF), D ** -0.5, 0.1875, ((0, 4), (1, 2)))
    b_fc = centred(key_list[9], (FF,), 0.3, 1.5, ((0, 8),), jnp.float32)
    w_proj = centred(key_list[10], (FF, D), FF ** -0.5, 0.09375, ((0, 2), (1, 4)))
    b_proj = centred(key_list[11], (D,), 0.3, 1.5, ((0, 4),), jnp.float32)
    cotangent = centred(key_list[12], (TOKENS, D), 1.0, 6.0, ((0, 8), (1, 4)))
    return dict(tokens=tokens, segment=segment, ln_gain=ln_gain, ln_bias=ln_bias, w_qkv=w_qkv, b_qv=b_qv, w_out=w_out, b_out=b_out, w_fc=w_fc, b_fc=b_fc, w_proj=w_proj, b_proj=b_proj, cotangent=cotangent)


@jax.custom_vjp
def low(v):
    return lax.optimization_barrier(v.astype(jnp.bfloat16)).astype(jnp.float32)

@jax.custom_vjp
def low_back(v):
    return v

def low_keep(v):
    return (low(v), None)

def low_pass(kept, grad):
    return (grad,)

def back_keep(v):
    return (v, None)

def back_low(kept, grad):
    return (low(grad),)
low.defvjp(low_keep, low_pass)
low_back.defvjp(back_keep, back_low)
EPS = 1e-05
HIGH = lax.Precision.HIGHEST

def norm(value, gain, shift):
    mean = lax.optimization_barrier(jnp.mean(value, -1, keepdims=True))
    squares = lax.optimization_barrier(jnp.mean(value * value, -1, keepdims=True))
    return (value - mean) * lax.rsqrt(squares - mean * mean + EPS) * gain + shift

def group_layer(inputs, segment, ln_gain, ln_bias, w_qkv, b_qv, w_out, b_out, w_fc, b_fc, w_proj, b_proj):
    total = inputs.shape[0]
    first = low(norm(inputs, ln_gain[0], ln_bias[0]))
    qkv = jnp.einsum('td,kdf->tkf', first, w_qkv, precision=HIGH)
    query = low(low_back(qkv[:, 0] + b_qv[0])).reshape(total, HEADS, HEAD_DIM)
    key_rows = low(low_back(qkv[:, 1])).reshape(total, HEADS, HEAD_DIM)
    value_rows = low(low_back(qkv[:, 2] + b_qv[1])).reshape(total, HEADS, HEAD_DIM)
    factor = 1.0 / math.sqrt(HEAD_DIM)
    score = low_back(jnp.einsum('qhd,khd->hqk', query, key_rows, precision=HIGH) * factor)
    places = jnp.arange(total)
    allowed = (segment[:, None] == segment[None, :]) & (places[:, None] >= places[None, :])
    probs = jax.nn.softmax(jnp.where(allowed[None], score, -1e+30), axis=-1)
    attended = jnp.einsum('hqk,khd->qhd', low(probs), value_rows, precision=HIGH).reshape(total, D)
    attended = low(low_back(attended))
    middle = inputs + low_back(jnp.dot(attended, w_out, precision=HIGH) + b_out)
    second = low(norm(middle, ln_gain[1], ln_bias[1]))
    hidden = low_back(jnp.dot(second, w_fc, precision=HIGH) + b_fc)
    active = low(jax.nn.gelu(hidden, approximate=True))
    return middle + jnp.dot(active, w_proj, precision=HIGH) + b_proj

def reference(tokens, segment, ln_gain, ln_bias, w_qkv, b_qv, w_out, b_out, w_fc, b_fc, w_proj, b_proj, cotangent):
    groups = tokens.shape[0] // GRP_TOK
    segments = segment.reshape(groups, GRP_TOK)

    def forward(inputs, *params):
        stepper = jax.checkpoint(lambda pair: group_layer(pair[0], pair[1], *params))
        result = lax.map(stepper, (inputs.reshape(groups, GRP_TOK, D), segments))
        return result.reshape(groups * GRP_TOK, D)
    params = (ln_gain.astype(jnp.float32), ln_bias.astype(jnp.float32), w_qkv.astype(jnp.float32), b_qv.astype(jnp.float32), w_out.astype(jnp.float32), b_out.astype(jnp.float32), w_fc.astype(jnp.float32), b_fc.astype(jnp.float32), w_proj.astype(jnp.float32), b_proj.astype(jnp.float32))
    mixed, pullback = jax.vjp(forward, tokens.astype(jnp.float32), *params)
    grads = pullback(cotangent.astype(jnp.float32))
    return (mixed.astype(jnp.bfloat16), grads[0], grads[1], grads[2], grads[3], grads[4], grads[5], grads[6], grads[7], grads[8], grads[9], grads[10])
```

```python
import math

import jax
import jax.numpy as jnp
from jax import lax
from jax.sharding import PartitionSpec as P

D = 1024
HEAD_DIM = 64
EPS = 1e-05
NEGATIVE = -1e30
LOW = jnp.bfloat16
F32 = jnp.float32


def swap(value, axis, k):
    return lax.ppermute(value, axis, [(i, i ^ k) for i in range(lax.axis_size(axis))])


def bits_of(axis):
    return range(int(math.log2(lax.axis_size(axis))))


def unxor(value, axis, index):
    size = value.shape[axis]
    for b in range(int(math.log2(size))):
        shape = value.shape
        split = value.reshape(shape[:axis] + (size >> (b + 1), 2, 1 << b) + shape[axis + 1 :])
        flipped = jnp.flip(split, axis + 1)
        value = jnp.where((index >> b) & 1 == 1, flipped, split).reshape(shape)
    return value


def col_gather(value):
    return [value] + [swap(value, "col", k) for k in range(1, lax.axis_size("col"))]


def col_exchange(blocks):
    return [blocks[0]] + [swap(blocks[k], "col", k) for k in range(1, len(blocks))]


def dp_scatter(blocks, order):
    n = blocks.shape[0]
    bits = int(math.log2(n))
    rest = blocks.shape[1:]
    value = blocks.reshape((2,) * bits + rest)
    alive = list(reversed(range(bits)))
    for b in order:
        axis = alive.index(b)
        keep = lax.index_in_dim(value, 0, axis, False)
        send = lax.index_in_dim(value, 1, axis, False)
        value = (keep.astype(F32) + swap(send, "dp", 1 << b).astype(F32)).astype(LOW)
        alive.remove(b)
    return value


def dp_gather(value, order):
    rest = value.shape
    bits = len(order)
    done = []
    for b in order:
        other = swap(value, "dp", 1 << b)
        place = len([x for x in done if x > b])
        value = jnp.stack([value, other], place)
        done = sorted(done + [b], reverse=True)
    return value.reshape((1 << bits,) + rest)


def row_scatter(value):
    half = value.shape[0] // 2
    return value[:half].astype(F32) + swap(value[half:].astype(LOW), "row", 1).astype(F32)


def shards(
    tokens,
    segment,
    ln_gain,
    ln_bias,
    w_qkv,
    b_qv,
    w_out,
    b_out,
    w_fc,
    b_fc,
    w_proj,
    b_proj,
    cotangent,
):
    cols = lax.axis_size("col")
    parts = lax.axis_size("dp")
    c = lax.axis_index("col")
    d = lax.axis_index("dp")
    r = lax.axis_index("row")
    half, width = tokens.shape
    group = 2 * half
    heads = w_qkv.shape[2] // cols
    units = w_fc.shape[1] // cols
    order_a = list(bits_of("dp"))
    order_b = order_a[1:] + order_a[:1]
    over_rows = (((0,), (0,)), ((), ()))
    over_cols = (((1,), (1,)), ((), ()))

    def dot(a, b, dims=(((1,), (0,)), ((), ()))):
        return lax.dot_general(a, b, dims, preferred_element_type=F32)

    piece = width // parts
    mine = lax.dynamic_slice_in_dim(w_qkv, d * piece, piece, 1)
    sent = [lax.dynamic_slice_in_dim(mine, (c ^ k) * heads, heads, 2) for k in range(cols)]
    quarter = jnp.stack(col_exchange(sent))
    params = jnp.concatenate([ln_gain, ln_bias])
    high = lax.reduce_precision(params, 8, 7)
    message = jnp.concatenate([tokens, high.astype(LOW), (params - high).astype(LOW)])
    got = jnp.stack(col_gather(message))
    qkv_rel = dp_gather(quarter, order_a)
    wq = unxor(qkv_rel, 0, d)
    wq = wq.transpose(1, 0, 3, 2, 4).reshape(cols * width, 3 * heads)
    x_blocks = got[:, :half]
    x_other = swap(x_blocks, "row", 1)
    x_all = jnp.concatenate([x_blocks, x_other], 1).transpose(1, 0, 2).reshape(group, D).astype(F32)
    full = (got[:, half : half + 4].astype(F32) + got[:, half + 4 :].astype(F32)).transpose(1, 0, 2)
    full = full.reshape(4, D)
    gains, shifts = full[:2], full[2:]

    unit = units // parts
    sent_fc = [
        lax.dynamic_slice_in_dim(w_fc, (c ^ k) * units + d * unit, unit, 1) for k in range(cols)
    ]
    sent_proj = [
        lax.dynamic_slice_in_dim(w_proj, (c ^ k) * units + d * unit, unit, 0) for k in range(cols)
    ]
    fc_rel = dp_gather(jnp.stack(col_exchange(sent_fc)), order_a)
    proj_rel = dp_gather(jnp.stack(col_exchange(sent_proj)), order_b)
    fc = fc_rel.transpose(1, 2, 0, 3).reshape(D, units)
    proj = proj_rel.transpose(0, 2, 1, 3).reshape(units, D)
    shift_fc = unxor(b_fc.reshape(parts, unit), 0, d).reshape(units)

    cot_blocks = jnp.stack(col_gather(cotangent))
    cot_other = swap(cot_blocks, "row", 1)
    cot_all = jnp.concatenate([cot_blocks, cot_other], 1).transpose(1, 0, 2).reshape(group, D)

    def norm(value, gain, shift):
        mean = jnp.mean(value, -1, keepdims=True)
        squares = jnp.mean(value * value, -1, keepdims=True)
        factor = lax.rsqrt(squares - mean * mean + EPS)
        normed = (value - mean) * factor
        return (normed * gain + shift).astype(LOW), normed, factor

    def norm_back(grad, normed, factor, gain):
        scaled = grad * gain
        first = jnp.mean(scaled, -1, keepdims=True)
        second = jnp.mean(scaled * normed, -1, keepdims=True)
        return factor * (scaled - first - normed * second)

    first, first_hat, first_factor = norm(x_all, gains[0], shifts[0])
    qkv = dot(first, wq)
    hd = HEAD_DIM
    per = heads // hd
    query = (qkv[:, :heads] + b_qv[0]).astype(LOW)
    keys = qkv[:, heads : 2 * heads].astype(LOW)
    values = (qkv[:, 2 * heads :] + b_qv[1]).astype(LOW)
    segs = jnp.concatenate([segment[half:], segment[:half]])
    segs = jnp.where(r == 0, segment, segs)
    places = (jnp.arange(group) + r * half) % group
    allowed = (segs[:, None] == segs[None, :]) & (places[:, None] >= places[None, :])
    factor = 1.0 / math.sqrt(hd)

    def split(value):
        return value.reshape(group, per, hd)

    score = jnp.einsum("qhd,khd->hqk", split(query), split(keys), preferred_element_type=F32)
    masked = jnp.where(allowed[None], score * factor, NEGATIVE)
    expo = jnp.exp(masked - jnp.max(masked, -1, keepdims=True))
    probs = expo / jnp.sum(expo, -1, keepdims=True)
    probs_low = probs.astype(LOW)
    attended = jnp.einsum("hqk,khd->qhd", probs_low, split(values), preferred_element_type=F32)
    attended = attended.reshape(group, heads).astype(LOW)
    attended_all = jnp.concatenate(col_gather(attended), 1)
    out_rel = unxor(w_out.reshape(cols, heads, width), 0, c).reshape(cols * heads, width)
    branch = dot(attended_all, out_rel)
    middle = (
        tokens.astype(F32) + (branch[:half] + swap(branch[half:], "row", 1)) + b_out
    )

    mid_blocks = jnp.stack(col_gather(middle.astype(LOW)))
    mid_other = swap(mid_blocks, "row", 1)
    mid_all = jnp.concatenate([mid_blocks, mid_other], 1).transpose(1, 0, 2).reshape(group, D)
    second, second_hat, second_factor = norm(mid_all.astype(F32), gains[1], shifts[1])
    hidden = dot(second, fc) + shift_fc
    active, pull = jax.vjp(lambda v: jax.nn.gelu(v, approximate=True), hidden)
    active = active.astype(LOW)
    grad_active = dot(cot_all, proj, over_cols)
    grad_hidden = pull(grad_active)[0].astype(LOW)
    grad_second = dot(grad_hidden, fc, over_cols)
    gain_second = jnp.sum(grad_second * second_hat, 0)
    shift_second = jnp.sum(grad_second, 0)
    back_second = row_scatter(norm_back(grad_second, second_hat, second_factor, gains[1]))

    def to_owner(value):
        low = value.astype(LOW)
        got = [low[:, k * width : (k + 1) * width] for k in range(cols)]
        got = col_exchange(got)
        return sum([g.astype(F32) for g in got[1:]], value[:, :width])

    grad_middle = cotangent.astype(F32) + to_owner(back_second)
    branch_low = grad_middle.astype(LOW)
    branch_all = jnp.concatenate([branch_low, swap(branch_low, "row", 1)])

    mixed_sum = to_owner(row_scatter(dot(active, proj)))
    mixed = (middle + mixed_sum + b_proj).astype(LOW)

    partial = dot(branch_all, out_rel, over_cols)
    got = col_exchange([partial[:, k * heads : (k + 1) * heads].astype(LOW) for k in range(cols)])
    grad_att = sum([g.astype(F32) for g in got[1:]], partial[:, :heads]).astype(LOW)
    grad_probs = jnp.einsum(
        "qhd,khd->hqk", split(grad_att), split(values), preferred_element_type=F32
    )
    grad_values = jnp.einsum(
        "hqk,qhd->khd", probs_low, split(grad_att), preferred_element_type=F32
    )
    centre = jnp.sum(probs * grad_probs, -1, keepdims=True)
    grad_score = (probs * (grad_probs - centre)).astype(LOW)
    grad_query = (
        jnp.einsum("hqk,khd->qhd", grad_score, split(keys), preferred_element_type=F32) * factor
    )
    grad_keys = (
        jnp.einsum("hqk,qhd->khd", grad_score, split(query), preferred_element_type=F32) * factor
    )
    grad_qkv = jnp.concatenate(
        [v.reshape(group, heads).astype(LOW) for v in (grad_query, grad_keys, grad_values)], 1
    )
    grad_first = dot(grad_qkv, wq, over_cols)
    gain_first = jnp.sum(grad_first * first_hat, 0)
    shift_first = jnp.sum(grad_first, 0)
    back_first = norm_back(grad_first, first_hat, first_factor, gains[0])
    sums = jnp.stack([gain_first, gain_second, shift_first, shift_second])
    sums_high = lax.reduce_precision(sums, 8, 7)
    low = back_first.astype(LOW)
    message = jnp.concatenate([low[half:], sums_high.astype(LOW), (sums - sums_high).astype(LOW)])
    got = swap(message, "row", 1).astype(F32)
    back_first = back_first[:half] + got[:half]
    sums = sums + got[half : half + 4] + got[half + 4 :]
    sums_high = lax.reduce_precision(sums, 8, 7)
    message = jnp.concatenate([back_first, sums_high, sums - sums_high]).astype(LOW)
    got = col_exchange([message[:, k * width : (k + 1) * width] for k in range(cols)])
    got = sum([g.astype(F32) for g in got[1:]])
    grad_tokens = grad_middle + back_first[:, :width] + got[:half]
    sums = sums[:, :width] + got[half : half + 4] + got[half + 4 :]

    fc_grad = dot(second, grad_hidden, over_rows).astype(LOW)
    fc_grad = fc_grad.reshape(cols, width, parts, unit).transpose(2, 0, 1, 3)
    proj_grad = dot(active, cot_all, over_rows).astype(LOW)
    proj_grad = proj_grad.reshape(parts, unit, cols, width).transpose(0, 2, 1, 3)
    fc_part = dp_scatter(fc_grad, order_a)
    proj_part = dp_scatter(proj_grad, order_b)
    fc_part = jnp.stack(col_exchange([fc_part[k] for k in range(cols)]))
    proj_part = jnp.stack(col_exchange([proj_part[k] for k in range(cols)]))
    fc_sum = dp_gather(fc_part, order_b)
    proj_sum = dp_gather(proj_part, order_a)
    fc_sum = unxor(unxor(fc_sum, 0, d), 1, c).transpose(2, 1, 0, 3).reshape(w_fc.shape)
    proj_sum = unxor(unxor(proj_sum, 0, d), 1, c).transpose(1, 0, 2, 3).reshape(w_proj.shape)

    out_grad = dot(attended_all, branch_all, over_rows)
    out_grad = lax.psum(out_grad.astype(LOW), "dp").astype(F32)
    out_grad = unxor(out_grad.reshape(cols, heads, width), 0, c).reshape(w_out.shape)

    qkv_grad = dot(first, grad_qkv, over_rows).astype(LOW)
    qkv_grad = qkv_grad.reshape(cols, parts, piece, 3, heads).transpose(1, 0, 3, 2, 4)
    qkv_grad = unxor(qkv_grad, 0, d)
    qkv_part = dp_scatter(qkv_grad, order_a)
    qkv_part = jnp.stack(col_exchange([qkv_part[k] for k in range(cols)]))
    qkv_sum = dp_gather(qkv_part, order_b)
    qkv_sum = unxor(unxor(qkv_sum, 0, d), 1, c)
    qkv_sum = qkv_sum.transpose(2, 0, 3, 1, 4).reshape(w_qkv.shape)

    fc_shift = jnp.sum(grad_hidden.astype(F32), 0).reshape(parts, unit)
    fc_shift = unxor(fc_shift, 0, d).reshape(-1, width)
    qv = grad_qkv.astype(F32)
    qv_shift = jnp.concatenate([jnp.sum(qv[:, :heads], 0), jnp.sum(qv[:, 2 * heads :], 0)])
    small = jnp.concatenate(
        [
            sums,
            jnp.sum(branch_all.astype(F32), 0)[None],
            jnp.sum(cot_all[:, :width].astype(F32), 0)[None],
            qv_shift.reshape(-1, width),
            fc_shift,
        ]
    )
    for b in order_a:
        small = small + swap(small, "dp", 1 << b)
    return (
        mixed,
        grad_tokens,
        small[0:2],
        small[2:4],
        qkv_sum.astype(F32),
        small[6].reshape(b_qv.shape),
        out_grad,
        small[4],
        fc_sum.astype(F32),
        small[7:].reshape(-1),
        proj_sum.astype(F32),
        small[5],
    )


def solution(mesh):
    in_specs = (
        P(("dp", "row"), "col"),
        P("dp"),
        P(None, "col"),
        P(None, "col"),
        P(None, "col", "row"),
        P(None, ("row", "col")),
        P("row", "col"),
        P("col"),
        P("col", "row"),
        P(("row", "col")),
        P("row", "col"),
        P("col"),
        P(("dp", "row"), "col"),
    )
    out_specs = (
        P(("dp", "row"), "col"),
        P(("dp", "row"), "col"),
        P(None, "col"),
        P(None, "col"),
        P(None, "col", "row"),
        P(None, ("row", "col")),
        P("row", "col"),
        P("col"),
        P("col", "row"),
        P(("row", "col")),
        P("row", "col"),
        P("col"),
    )
    return jax.shard_map(shards, mesh=mesh, in_specs=in_specs, out_specs=out_specs, check_vma=False)
```

```python
import math

import jax
import jax.numpy as jnp
from jax import lax
from jax.experimental import pallas as pl
from jax.experimental.pallas import tpu as pltpu
from jax.sharding import PartitionSpec as P

D = 1024
HEAD_DIM = 64
EPS = 1e-05
NEGATIVE = -1e30
LOW = jnp.bfloat16
F32 = jnp.float32
FACTOR = 1.0 / math.sqrt(HEAD_DIM)
ROOT = math.sqrt(2.0 / math.pi)
CUBE = 0.044715
COLS = 4
PARTS = 4
OVER_ROWS = (((0,), (0,)), ((), ()))
OVER_COLS = (((1,), (1,)), ((), ()))
PLAIN = (((1,), (0,)), ((), ()))


def swap(value, axis, k):
    return lax.ppermute(value, axis, [(i, i ^ k) for i in range(lax.axis_size(axis))])


def dot(a, b, dims=PLAIN):
    return lax.dot_general(a, b, dims, preferred_element_type=F32)


def arr(shape, dtype=LOW):
    return jax.ShapeDtypeStruct(shape, dtype)


def place():
    return lax.axis_index("col"), lax.rem(lax.axis_index("dp"), PARTS)


def call(body, outs, args, hbm=(), scratch=(), us=1.0, name=None):
    whole = pl.BlockSpec(memory_space=pltpu.VMEM)
    anywhere = pl.BlockSpec(memory_space=pl.ANY)
    held = sum(math.prod(a.shape) * a.dtype.itemsize for a in list(args) + list(outs))
    held += sum(math.prod(a.shape) * 4 for a in scratch if len(a.shape) > 1)
    return pl.pallas_call(
        body,
        out_shape=list(outs),
        in_specs=[anywhere if i in hbm else whole for i in range(len(args))],
        out_specs=[whole] * len(outs),
        scratch_shapes=list(scratch),
        compiler_params=pltpu.CompilerParams(vmem_limit_bytes=held + 3 * 1024 * 1024),
        cost_estimate=pl.CostEstimate(
            flops=int(us * 1.1e9), bytes_accessed=1024, transcendentals=0
        ),
        name=name,
    )(*args)


def pack_qkv(w, gain, shift, b_out, m0, m1, m2, m3, values, sems):
    c, d = place()
    small = [(gain, values.at[0:2]), (shift, values.at[2:4]), (b_out, values.at[4:5])]
    small = [pltpu.make_async_copy(a, b, sems.at[12 + i]) for i, (a, b) in enumerate(small)]
    values[...] = jnp.zeros_like(values)
    for copy in small:
        copy.start()
    copies = []
    for k, out in enumerate((m0, m1, m2, m3)):
        for j in range(3):
            piece = w.shape[1] // PARTS
            heads = w.shape[2] // COLS
            copies.append(
                pltpu.make_async_copy(
                    w.at[
                        j,
                        pl.ds(pl.multiple_of(d * piece, piece), piece),
                        pl.ds(pl.multiple_of((c ^ k) * heads, heads), heads),
                    ],
                    out.at[pl.ds(j * piece, piece)],
                    sems.at[k * 3 + j],
                )
            )
            copies[-1].start()
    for copy in small:
        copy.wait()
    full = values[...]
    high = full.astype(LOW)
    low = (full - high.astype(F32)).astype(LOW).astype(F32)
    high = high.astype(F32)
    rows = jnp.concatenate([high[:, :128], high[:, 128:], low[:, :128], low[:, 128:]], 0)
    rows = rows.astype(LOW)
    for out in (m0, m1, m2, m3):
        out[192:224, :] = rows
    for copy in copies:
        copy.wait()


def pack_mlp(w_fc, w_proj, w_out, f1, f2, f3, sems):
    c, d = place()
    units = w_fc.shape[1] // COLS
    unit = units // PARTS
    rows = w_out.shape[0] // PARTS
    copies = []
    for k, f in ((1, f1), (2, f2), (3, f3)):
        start = pl.ds(pl.multiple_of((c ^ k) * units + d * unit, unit), unit)
        mine = pl.ds(pl.multiple_of(d * rows, rows), rows)
        copies.append((w_fc.at[:, start], f.at[pl.ds(0, 256)]))
        for j in range(2):
            cols = pl.ds(j * 128, 128)
            copies.append((w_out.at[mine, cols], f.at[pl.ds(256 + j * 128, 128)]))
            copies.append((w_proj.at[start, cols], f.at[pl.ds(512 + j * 128, 128)]))
    copies = [pltpu.make_async_copy(a, b, sems.at[i]) for i, (a, b) in enumerate(copies)]
    for copy in copies:
        copy.start()
    for copy in copies:
        copy.wait()


def split_mlp(f1, f2, f3, wf, pr):
    for k, f in enumerate((f1, f2, f3)):
        wf[k] = f[0:512, :]
        pr[k] = f[512:768, :]


def stack(*refs):
    for i, ref in enumerate(refs[:-1]):
        refs[-1][i] = ref[...]


def norm_parts(blocks):
    total = sum(jnp.sum(b, -1, keepdims=True) for b in blocks)
    squares = sum(jnp.sum(b * b, -1, keepdims=True) for b in blocks)
    mean = total * (1.0 / D)
    factor = lax.rsqrt(squares * (1.0 / D) - mean * mean + EPS)
    return mean, factor


def head_lanes(shape):
    return lax.broadcasted_iota(jnp.int32, shape, 1) < HEAD_DIM


def attention(*refs):
    xo, xs = refs[0:4], refs[4:8]
    m0, st, r1, r2, r3, w, b_qv, segment = refs[8:16]
    first, x_all, wq, params, qkv, probs, attended, bias, sems = refs[16:25]
    c, d = place()
    piece = 64
    copies = []
    for j in range(3):
        copies.append(
            pltpu.make_async_copy(
                w.at[j, :, pl.ds(pl.multiple_of(c * 128, 128), 128)],
                wq.at[pl.ds(0, 256), pl.ds(j * 128, 128)],
                sems.at[j],
            )
        )
        copies[-1].start()
    for k in range(COLS):
        rows = (m0[192:224, :] if k == 0 else st[k - 1, 192:224, :]).astype(F32)
        full = rows[0:16] + rows[16:32]
        params[:, k * 256 : k * 256 + 128] = full[0:8]
        params[:, k * 256 + 128 : (k + 1) * 256] = full[8:16]
    for m, src in enumerate((st, r1, r2, r3)):
        for k in range(1, COLS):
            start = pl.multiple_of(k * 256 + (d ^ m) * piece, piece)
            for j in range(3):
                wq[pl.ds(start, piece), j * 128 : (j + 1) * 128] = src[
                    k - 1, j * piece : (j + 1) * piece, :
                ]
    for half, srcs in enumerate((xo, xs)):

        @pl.loop(0, 8)
        def _(i):
            rows = pl.ds(pl.multiple_of(i * 32, 32), 32)
            into = pl.ds(pl.multiple_of(half * 256 + i * 32, 32), 32)
            low = [src[rows, :] for src in srcs]
            blocks = [b.astype(F32) for b in low]
            mean, factor = norm_parts(blocks)
            for k in range(COLS):
                cols = slice(k * 256, (k + 1) * 256)
                out = (blocks[k] - mean) * factor * params[0:1, cols] + params[2:3, cols]
                first[into, cols] = out.astype(LOW)
                x_all[into, cols] = low[k]

    r = lax.axis_index("row")
    ids = segment[...].astype(F32)
    ids = jnp.where(r == 0, ids, jnp.concatenate([ids[:, 256:512], ids[:, 0:256]], 1))
    spot = lax.rem(lax.broadcasted_iota(jnp.int32, (1, 512), 1) + r * 256, 512).astype(F32)
    for i in range(4):
        cols = slice(i * 128, (i + 1) * 128)
        there = [
            jnp.concatenate([jnp.broadcast_to(v[:, cols], (128, 128)).T] * 4, 1)
            for v in (ids, spot)
        ]
        allowed = (there[0] == ids) & (there[1] >= spot)
        bias[cols, :] = jnp.where(allowed, 0.0, NEGATIVE)
    for copy in copies:
        copy.wait()
    added = jnp.concatenate([b_qv[0:1, :], jnp.zeros((1, 128), F32), b_qv[1:2, :]], 1)

    @pl.loop(0, 4)
    def _(i):
        rows = pl.ds(pl.multiple_of(i * 128, 128), 128)
        qkv[rows, :] = (dot(first[rows, :], wq[...]) + added).astype(LOW)

    @pl.loop(0, 4)
    def _(i):
        rows = pl.ds(pl.multiple_of(i * 128, 128), 128)
        lanes = head_lanes((128, 128))
        query = qkv[rows, 0:128]
        keys = qkv[:, 128:256]
        values = qkv[:, 256:384]
        outs = []
        for h in range(2):
            mine = jnp.where(lanes == (h == 0), query, jnp.zeros_like(query))
            score = dot(mine, keys, OVER_COLS) * FACTOR + bias[rows, :]
            expo = jnp.exp(score - jnp.max(score, -1, keepdims=True))
            weights = expo / jnp.sum(expo, -1, keepdims=True)
            probs[h, rows, :] = weights
            outs.append(dot(weights.astype(LOW), values))
        attended[rows, :] = jnp.where(lanes, outs[0], outs[1]).astype(LOW)


def join_fc(w_out, w_fc, st, r1, r2, r3, out, fc, sems):
    c, d = place()
    copies = [(w_out, out.at[:, pl.ds(0, 256)])]
    for m in range(PARTS):
        start = pl.ds(pl.multiple_of(c * 512 + (d ^ m) * 128, 128), 128)
        copies.append((w_fc.at[:, start], fc.at[pl.ds(0, 256), pl.ds(m * 128, 128)]))
    copies = [pltpu.make_async_copy(a, b, sems.at[i]) for i, (a, b) in enumerate(copies)]
    for copy in copies:
        copy.start()
    for m, src in enumerate((st, r1, r2, r3)):
        rows = pl.ds(pl.multiple_of((d ^ m) * 128, 128), 128)
        for k in range(1, COLS):
            out[rows, k * 256 : k * 256 + 128] = src[k - 1, 256:384, :]
            out[rows, k * 256 + 128 : (k + 1) * 256] = src[k - 1, 384:512, :]
            fc[k * 256 : (k + 1) * 256, m * 128 : (m + 1) * 128] = src[k - 1, 0:256, :]
    for copy in copies:
        copy.wait()


def join_proj(w_proj, st, r1, r2, r3, proj, sems):
    c, d = place()
    copies = []
    for m in range(PARTS):
        start = pl.ds(pl.multiple_of(c * 512 + (d ^ m) * 128, 128), 128)
        copies.append((w_proj.at[start], proj.at[pl.ds(m * 128, 128), pl.ds(0, 256)]))
    copies = [pltpu.make_async_copy(a, b, sems.at[i]) for i, (a, b) in enumerate(copies)]
    for copy in copies:
        copy.start()
    for m, src in enumerate((st, r1, r2, r3)):
        rows = slice(m * 128, (m + 1) * 128)
        for k in range(1, COLS):
            proj[rows, k * 256 : k * 256 + 128] = src[k - 1, 0:128, :]
            proj[rows, k * 256 + 128 : (k + 1) * 256] = src[k - 1, 128:256, :]
    for copy in copies:
        copy.wait()


def forward(*refs):
    mine, theirs = refs[0:4], refs[4:8]
    w_own, w_sib, x_all, params, fc, b_fc = refs[8:14]
    att_own, middle, second, hidden, mid_own, att_sib, shift = refs[14:21]
    c, d = place()
    for m in range(PARTS):
        here = pl.ds(pl.multiple_of((d ^ m) * 128, 128), 128)
        shift[0:1, m * 128 : (m + 1) * 128] = b_fc[0:1, here]
    for k in range(COLS):
        cols = pl.ds(pl.multiple_of((c ^ k) * 128, 128), 128)
        att_own[:, cols] = mine[k][...]
        att_sib[0:256, cols] = theirs[k][256:512, :]
        att_sib[256:512, cols] = theirs[k][0:256, :]

    @pl.loop(0, 4)
    def _(i):
        rows = pl.ds(pl.multiple_of(i * 128, 128), 128)
        value = dot(att_own[rows, :], w_own[...]) + dot(att_sib[rows, :], w_sib[...])
        value = value + x_all[rows, :].astype(F32) + params[4:5, :]
        middle[rows, :] = value
        mean, factor = norm_parts([value])
        out = (value - mean) * factor * params[1:2, :] + params[3:4, :]
        second[rows, :] = out.astype(LOW)
        hidden[rows, :] = dot(second[rows, :], fc[...]) + shift[0:1, :]

    mid_own[...] = middle[0:256, 0:256]


def backward(*refs):
    co, cs = refs[0:4], refs[4:8]
    middle, hidden, fc, proj, params = refs[8:13]
    cot, active, grad_hidden, back, send, sums, fc_shift, cot_shift, shift = refs[13:22]
    for k in range(COLS):
        cols = slice(k * 256, (k + 1) * 256)
        cot[0:256, cols] = co[k][...]
        cot[256:512, cols] = cs[k][...]
    sums[...] = jnp.zeros_like(sums)
    shift[...] = jnp.zeros_like(shift)
    cot_shift[...] = jnp.sum(cot[:, 0:256].astype(F32), 0, keepdims=True)

    def step(start):
        rows = pl.ds(pl.multiple_of(start, 128), 128)
        v = hidden[rows, :]
        t = jnp.tanh(ROOT * (v + CUBE * (v * v * v)))
        active[rows, :] = (0.5 * v * (1.0 + t)).astype(LOW)
        slope = 0.5 * (1.0 + t) + 0.5 * v * (1.0 - t * t) * (ROOT * (1.0 + 3.0 * CUBE * (v * v)))
        low = (dot(cot[rows, :], proj[...], OVER_COLS) * slope).astype(LOW)
        grad_hidden[rows, :] = low
        shift[0:1, :] += jnp.sum(low.astype(F32), 0, keepdims=True)
        grad = dot(low, fc[...], OVER_COLS)
        mean, factor = norm_parts([middle[rows, :]])
        normed = (middle[rows, :] - mean) * factor
        sums[0:1, :] += jnp.sum(grad * normed, 0, keepdims=True)
        sums[1:2, :] += jnp.sum(grad, 0, keepdims=True)
        scaled = grad * params[1:2, :]
        one = jnp.mean(scaled, -1, keepdims=True)
        two = jnp.mean(scaled * normed, -1, keepdims=True)
        return factor * (scaled - one - normed * two)

    @pl.loop(0, 2)
    def _(i):
        send[pl.ds(pl.multiple_of(i * 128, 128), 128), :] = step(256 + i * 128).astype(LOW)

    @pl.loop(0, 2)
    def _(i):
        back[pl.ds(pl.multiple_of(i * 128, 128), 128), :] = step(i * 128)

    c, d = place()
    for m in range(PARTS):
        here = pl.ds(pl.multiple_of((d ^ m) * 128, 128), 128)
        fc_shift[0:1, here] = shift[0:1, m * 128 : (m + 1) * 128]


def mlp_grads(second, grad_hidden, active, cot, proj, fk, fs, pk, ps, mine, send):
    @pl.loop(0, 4)
    def _(k):
        cols = pl.ds(pl.multiple_of(k * 256, 256), 256)
        value = dot(second[:, cols], grad_hidden[...], OVER_ROWS).astype(LOW)
        for m in range(PARTS):
            (fs if m % 2 else fk)[m // 2, k] = value[:, m * 128 : (m + 1) * 128]

    for m in range(PARTS):
        value = dot(active[:, m * 128 : (m + 1) * 128], cot[...], OVER_ROWS).astype(LOW)
        for k in range(COLS):
            (ps if m // 2 else pk)[m % 2, k] = value[:, k * 256 : (k + 1) * 256]
    mine[...] = dot(active[0:256, :], proj[...])
    send[...] = dot(active[256:512, :], proj[...]).astype(LOW)


def split_sum(back, got, o0, o1, o2, o3):
    for k, out in enumerate((o0, o1, o2, o3)):
        cols = slice(k * 256, (k + 1) * 256)
        out[...] = (back[:, cols] + got[:, cols].astype(F32)).astype(out.dtype)


def middle_sum(cot, o0, g1, g2, g3, out, low):
    value = cot[...].astype(F32) + (
        o0[...] + g1[...].astype(F32) + g2[...].astype(F32) + g3[...].astype(F32)
    )
    out[...] = value
    low[...] = value.astype(LOW)


def mixed_sum(middle, o0, g1, g2, g3, b_proj, out):
    value = o0[...] + g1[...].astype(F32) + g2[...].astype(F32) + g3[...].astype(F32)
    out[...] = (middle[...] + value + b_proj[...]).astype(LOW)


def grad_out(own, other, w_out, o0, o1, o2, o3):
    c, d = place()
    for k, out in enumerate((o0, o1, o2, o3)):
        rows = pl.ds(pl.multiple_of((c ^ k) * 128, 128), 128)
        w = w_out[rows, :]
        out[0:256, :] = dot(own[...], w, OVER_COLS).astype(out.dtype)
        out[256:512, :] = dot(other[...], w, OVER_COLS).astype(out.dtype)


def out_weight(att, own, other, out, shift):
    out[...] = (
        dot(att[0:256, :], own[...], OVER_ROWS) + dot(att[256:512, :], other[...], OVER_ROWS)
    ).astype(LOW)
    shift[...] = jnp.sum(own[...].astype(F32), 0, keepdims=True) + jnp.sum(
        other[...].astype(F32), 0, keepdims=True
    )


def attention_back(*refs):
    d0, d1, d2, d3, qkv, probs, wq, x_all, params, sums2 = refs[0:10]
    dqkv, back, send, qv_shift = refs[10:14]
    datt, scores, lows, sums = refs[14:18]
    datt[...] = (
        d0[...] + d1[...].astype(F32) + d2[...].astype(F32) + d3[...].astype(F32)
    ).astype(LOW)

    @pl.loop(0, 4)
    def _(i):
        rows = pl.ds(pl.multiple_of(i * 128, 128), 128)
        lanes = head_lanes((128, 128))
        keys = qkv[:, 128:256]
        values = qkv[:, 256:384]
        grad = datt[rows, :]
        outs = []
        for h in range(2):
            mine = jnp.where(lanes == (h == 0), grad, jnp.zeros_like(grad))
            gp = dot(mine, values, OVER_COLS)
            weights = probs[h, rows, :]
            centre = jnp.sum(weights * gp, -1, keepdims=True)
            score = (weights * (gp - centre)).astype(LOW)
            scores[h, rows, :] = score
            lows[h, rows, :] = weights.astype(LOW)
            outs.append(dot(score, keys))
        dqkv[rows, 0:128] = (jnp.where(lanes, outs[0], outs[1]) * FACTOR).astype(LOW)

    lanes = head_lanes((512, 128))
    gk = [dot(scores[h], qkv[:, 0:128], OVER_ROWS) for h in range(2)]
    dqkv[:, 128:256] = (jnp.where(lanes, gk[0], gk[1]) * FACTOR).astype(LOW)
    gv = [dot(lows[h], datt[...], OVER_ROWS) for h in range(2)]
    dqkv[:, 256:384] = jnp.where(lanes, gv[0], gv[1]).astype(LOW)
    qv_shift[...] = jnp.sum(dqkv[...].astype(F32), 0, keepdims=True)
    sums[...] = jnp.zeros_like(sums)

    def step(start):
        rows = pl.ds(pl.multiple_of(start, 128), 128)
        grad = dot(dqkv[rows, :], wq[...], OVER_COLS)
        x = x_all[rows, :].astype(F32)
        mean, factor = norm_parts([x])
        normed = (x - mean) * factor
        sums[0:1, :] += jnp.sum(grad * normed, 0, keepdims=True)
        sums[1:2, :] += jnp.sum(grad, 0, keepdims=True)
        scaled = grad * params[0:1, :]
        one = jnp.mean(scaled, -1, keepdims=True)
        two = jnp.mean(scaled * normed, -1, keepdims=True)
        return factor * (scaled - one - normed * two)

    @pl.loop(0, 2)
    def _(i):
        send[pl.ds(pl.multiple_of(i * 128, 128), 128), :] = step(256 + i * 128).astype(LOW)

    @pl.loop(0, 2)
    def _(i):
        back[pl.ds(pl.multiple_of(i * 128, 128), 128), :] = step(i * 128)

    rows = jnp.concatenate(
        [sums[0:1, :], sums2[0:1, :], sums[1:2, :], sums2[1:2, :], jnp.zeros((4, D), F32)], 0
    )
    back[256:264, :] = rows
    high = rows.astype(LOW).astype(F32)
    send[256:272, :] = jnp.concatenate([high, rows - high], 0).astype(LOW)


def split_last(back, got, o0, s0, o1, o2, o3):
    more = got[256:272, :].astype(F32)
    sums = back[256:264, :] + more[0:8] + more[8:16]
    high = sums.astype(LOW).astype(F32)
    both = jnp.concatenate([high, sums - high], 0).astype(LOW)
    o0[...] = back[0:256, 0:256] + got[0:256, 0:256].astype(F32)
    s0[...] = sums[:, 0:256]
    for k, out in ((1, o1), (2, o2), (3, o3)):
        cols = slice(k * 256, (k + 1) * 256)
        out[0:256, :] = (back[0:256, cols] + got[0:256, cols].astype(F32)).astype(LOW)
        out[256:272, :] = both[:, cols]


def last_sum(o0, s0, g1, g2, g3, middle, out, sums):
    out[...] = middle[...] + (
        o0[...]
        + g1[0:256, :].astype(F32)
        + g2[0:256, :].astype(F32)
        + g3[0:256, :].astype(F32)
    )
    value = s0[...]
    for g in (g1, g2, g3):
        more = g[256:272, :].astype(F32)
        value = value + more[0:8] + more[8:16]
    sums[...] = value


def qkv_weight(first, dqkv, w_out, ak, as_, bk, bs, full):
    c, d = place()

    @pl.loop(0, 4)
    def _(k):
        cols = pl.ds(pl.multiple_of(k * 256, 256), 256)
        full[cols, :] = dot(first[:, cols], dqkv[...], OVER_ROWS)

    for m in range(PARTS):
        outs = ((as_ if m % 2 else ak, m // 2), (bs if m // 2 else bk, m % 2))
        rows = pl.ds(pl.multiple_of((d ^ m) * 128, 128), 128)
        for j, (out, index) in enumerate(outs):
            out[index, 384:512, :] = w_out[rows, j * 128 : (j + 1) * 128]
        for k in range(COLS):
            out, index = outs[k // 2]
            start = pl.ds(pl.multiple_of(k * 256 + (d ^ m) * 64, 64), 64)
            for j in range(3):
                row = (k % 2) * 192 + j * 64
                out[index, row : row + 64, :] = full[start, j * 128 : (j + 1) * 128].astype(LOW)


def unpack_qkv(st, r1, r2, r3, out, w_out):
    c, d = place()
    for m, src in enumerate((st, r1, r2, r3)):
        rows = pl.ds(pl.multiple_of((d ^ m) * 64, 64), 64)
        for k in range(COLS):
            cols = pl.ds(pl.multiple_of((c ^ k) * 128, 128), 128)
            for j in range(3):
                start = k * 192 + j * 64
                out[j, rows, cols] = src[start : start + 64, :].astype(F32)
        rows = pl.ds(pl.multiple_of((d ^ m) * 128, 128), 128)
        w_out[rows, 0:128] = src[768:896, :].astype(F32)
        w_out[rows, 128:256] = src[896:1024, :].astype(F32)


def unpack_mlp(st, r1, r2, r3, fc, proj):
    c, d = place()
    for m, src in enumerate((st, r1, r2, r3)):
        for k in range(COLS):
            here = pl.ds(pl.multiple_of((c ^ k) * 512 + (d ^ m) * 128, 128), 128)
            fc[:, here] = src[k, 0:256, :].astype(F32)
            proj[here, 0:128] = src[k, 256:384, :].astype(F32)
            proj[here, 128:256] = src[k, 384:512, :].astype(F32)


def first_add_mlp(ka, ra, kb, rb, ha, sa, hb, sb):
    for keep, got, have, send in ((ka, ra, ha, sa), (kb, rb, hb, sb)):
        for k in range(COLS):
            have[k] = keep[0, k].astype(F32) + got[0, k].astype(F32)
            send[k] = (keep[1, k].astype(F32) + got[1, k].astype(F32)).astype(LOW)


def first_add_qkv(ka, ra, kb, rb, ha, sa, hb, sb):
    for keep, got, have, send in ((ka, ra, ha, sa), (kb, rb, hb, sb)):
        have[...] = keep[0].astype(F32) + got[0].astype(F32)
        send[...] = (keep[1].astype(F32) + got[1].astype(F32)).astype(LOW)


def second_add_mlp(ha, ra, hb, rb, *outs):
    for k, out in enumerate(outs):
        out[0:256, :] = (ha[k] + ra[k].astype(F32)).astype(LOW)
        proj = (hb[k] + rb[k].astype(F32)).astype(LOW)
        out[256:384, :] = proj[:, 0:128]
        out[384:512, :] = proj[:, 128:256]


def second_add_qkv(ha, ra, hb, rb, *outs):
    for k, out in enumerate(outs[:-1]):
        have, got = (ha, ra) if k < 2 else (hb, rb)
        rows = slice((k % 2) * 192, (k % 2) * 192 + 192)
        out[...] = (have[rows, :] + got[rows, :].astype(F32)).astype(LOW)
    for j, (have, got) in enumerate(((ha, ra), (hb, rb))):
        value = have[384:512, :] + got[384:512, :].astype(F32)
        outs[-1][j * 128 : (j + 1) * 128, :] = value.astype(LOW)


def stack_qkv(o0, o1, o2, o3, w_out, out):
    for k, part in enumerate((o0, o1, o2, o3)):
        out[k * 192 : (k + 1) * 192, :] = part[...]
    out[768:1024, :] = w_out[...]


def small_pack(sums, out_shift, cot_shift, qv, fc_shift, out):
    out[0:4, :] = sums[0:4, :]
    out[4:5, :] = out_shift[...]
    out[5:6, :] = cot_shift[...]
    out[6:7, 0:128] = qv[0:1, 0:128]
    out[6:7, 128:256] = qv[0:1, 256:384]
    out[7:8, :] = fc_shift[0:1, 0:256]
    out[8:9, :] = fc_shift[0:1, 256:512]
    out[9:16, :] = jnp.zeros((7, 256), F32)


def small_add(a, b, out):
    out[...] = a[...] + b[...]


def small_unpack(a, b, gain, shift, b_qv, b_out, b_fc, b_proj):
    total = a[...] + b[...]
    gain[...] = total[0:2]
    shift[...] = total[2:4]
    b_out[...] = total[4:5]
    b_proj[...] = total[5:6]
    b_qv[0:1, :] = total[6:7, 0:128]
    b_qv[1:2, :] = total[6:7, 128:256]
    b_fc[0:1, 0:256] = total[7:8]
    b_fc[0:1, 256:512] = total[8:9]


def after(value, *others):
    return lax.optimization_barrier((value, others))[0]


def high_bits():
    return [1 << b for b in range(2, int(math.log2(lax.axis_size("dp"))))]


def dp_gather(value):
    return [swap(value, "dp", k) for k in (1, 2, 3)]


def dp_first(ka, sa, kb, sb):
    return [ka, swap(sa, "dp", 1), kb, swap(sb, "dp", 2)]


def dp_second(sums, body, shapes, name):
    ha, sa, hb, sb = sums
    got = [ha, swap(sa, "dp", 2), hb, swap(sb, "dp", 1)]
    outs = call(body, [arr(shape) for shape in shapes], got, name=name)
    for k in high_bits():
        outs = [(o.astype(F32) + swap(o, "dp", k).astype(F32)).astype(LOW) for o in outs]
    return outs


def shards(
    tokens,
    segment,
    ln_gain,
    ln_bias,
    w_qkv,
    b_qv,
    w_out,
    b_out,
    w_fc,
    b_fc,
    w_proj,
    b_proj,
    cotangent,
):
    half, width = tokens.shape
    group = 2 * half
    dma = pltpu.SemaphoreType.DMA

    sent = call(
        pack_qkv,
        [arr((224, 128))] * 4,
        [w_qkv, ln_gain, ln_bias, b_out.reshape(1, width)],
        hbm=(0, 1, 2, 3),
        scratch=[pltpu.VMEM((8, width), F32), dma((15,))],
        name="pack_qkv",
    )
    q_got = [swap(sent[k], "col", k) for k in (1, 2, 3)]
    tokens = after(tokens, sent)
    x_own = [tokens] + [swap(tokens, "col", k) for k in (1, 2, 3)]
    x_sib = [swap(x, "row", 1) for x in x_own]
    q_st = call(stack, [arr((3, 224, 128))], q_got, name="stack_qkv")[0]
    q_dp = dp_gather(q_st)
    packed = call(
        pack_mlp,
        [arr((768, 128))] * 3,
        [w_fc, w_proj, w_out],
        hbm=(0, 1, 2),
        scratch=[dma((15,))],
        name="pack_mlp",
    )
    packed = after(packed, x_own)
    packed = [swap(packed[k - 1], "col", k) for k in (1, 2, 3)]

    first, x_all, wq, params, qkv, probs, attended = call(
        attention,
        [
            arr((group, D)),
            arr((group, D)),
            arr((D, 384)),
            arr((8, D), F32),
            arr((group, 384)),
            arr((2, group, group), F32),
            arr((group, 128)),
        ],
        [*x_own, *x_sib, sent[0], q_st, *q_dp, w_qkv, b_qv, segment.reshape(1, group)],
        hbm=(13,),
        scratch=[pltpu.VMEM((group, group), F32), dma((3,))],
        us=9.3,
        name="attention",
    )
    a_own = [attended] + [swap(attended, "col", k) for k in (1, 2, 3)]
    a_sib = [swap(a, "row", 1) for a in a_own]

    wf_st, pr_st = call(
        split_mlp,
        [arr((3, 512, 128)), arr((3, 256, 128))],
        after(packed, a_own[1]),
        name="split_mlp",
    )
    wf_dp = dp_gather(wf_st)
    w_own, fc = call(
        join_fc,
        [arr((512, D)), arr((D, 512))],
        [w_out, w_fc, wf_st, *wf_dp],
        hbm=(0, 1),
        scratch=[dma((5,))],
        us=1.6,
        name="join_fc",
    )
    w_sib = swap(w_own, "row", 1)
    pr_st = after(pr_st, a_own, a_sib)
    pr_dp = dp_gather(pr_st)
    att_own, middle, second, hidden, mid_own = call(
        forward,
        [
            arr((group, 512)),
            arr((group, D), F32),
            arr((group, D)),
            arr((group, 512), F32),
            arr((half, width), F32),
        ],
        [*a_own, *a_sib, w_own, w_sib, x_all, params, fc, b_fc.reshape(1, 512)],
        scratch=[pltpu.VMEM((group, 512), LOW), pltpu.VMEM((8, 512), F32)],
        us=6.6,
        name="forward",
    )

    proj = call(
        join_proj,
        [arr((512, D))],
        [w_proj, pr_st, *pr_dp],
        hbm=(0,),
        scratch=[dma((4,))],
        name="join_proj",
    )[0]
    cot = after(cotangent, a_own, a_sib)
    c_own = [cot] + [swap(cot, "col", k) for k in (1, 2, 3)]
    c_sib = [swap(x, "row", 1) for x in c_own]
    cot_all, active, grad_hidden, back, send, sums2, fc_shift, cot_shift = call(
        backward,
        [
            arr((group, D)),
            arr((group, 512)),
            arr((group, 512)),
            arr((half, D), F32),
            arr((half, D)),
            arr((2, D), F32),
            arr((1, 512), F32),
            arr((1, width), F32),
        ],
        [*c_own, *c_sib, middle, hidden, fc, proj, params],
        scratch=[pltpu.VMEM((8, 512), F32)],
        us=6.5,
        name="backward",
    )
    got = swap(send, "row", 1)
    parts = call(
        split_sum,
        [arr((half, width), F32)] + [arr((half, width))] * 3,
        [back, got],
        name="split_second",
    )
    got = [swap(parts[k], "col", k) for k in (1, 2, 3)]
    mid_parts = [parts[0], *got]
    fk, fs, pk, ps, mix, mix_send = call(
        mlp_grads,
        [
            arr((2, 4, 256, 128)),
            arr((2, 4, 256, 128)),
            arr((2, 4, 128, 256)),
            arr((2, 4, 128, 256)),
            arr((half, D), F32),
            arr((half, D)),
        ],
        [after(second, parts), grad_hidden, active, cot_all, proj],
        us=5.4,
        name="mlp_grads",
    )
    mlp_got = dp_first(fk, fs, pk, ps)
    grad_middle, branch = call(
        middle_sum,
        [arr((half, width), F32), arr((half, width))],
        after([cotangent, *mid_parts], fk),
        name="middle_sum",
    )
    other = swap(branch, "row", 1)
    parts = call(
        grad_out,
        [arr((group, 128), F32)] + [arr((group, 128))] * 3,
        [branch, other, w_out],
        us=0.5,
        name="grad_out",
    )
    out_grad, out_shift = call(
        out_weight,
        [arr(w_out.shape), arr((1, width), F32)],
        [att_own, branch, other],
        us=1.0,
        name="out_weight",
    )
    datt = [after(parts[0], out_grad)] + [swap(parts[k], "col", k) for k in (1, 2, 3)]
    m_sums = call(
        first_add_mlp,
        [
            arr((4, 256, 128), F32),
            arr((4, 256, 128)),
            arr((4, 128, 256), F32),
            arr((4, 128, 256)),
        ],
        after(mlp_got, parts),
        name="first_add_mlp",
    )
    ms = dp_second(m_sums, second_add_mlp, [(512, 128)] * 4, "second_add_mlp")
    datt = after(datt, ms)
    ms = [ms[0]] + [swap(ms[k], "col", k) for k in (1, 2, 3)]
    dqkv, back, send, qv_shift = call(
        attention_back,
        [
            arr((group, 384)),
            arr((half + 8, D), F32),
            arr((half + 16, D)),
            arr((1, 384), F32),
        ],
        [*datt, qkv, probs, wq, x_all, params, sums2],
        scratch=[
            pltpu.VMEM((group, 128), LOW),
            pltpu.VMEM((2, group, group), LOW),
            pltpu.VMEM((2, group, group), LOW),
            pltpu.VMEM((8, D), F32),
        ],
        us=7.4,
        name="attention_back",
    )
    ak, as_, bk, bs = call(
        qkv_weight,
        [arr((2, 512, 128))] * 4,
        [first, dqkv, out_grad],
        scratch=[pltpu.VMEM((D, 384), F32)],
        us=1.5,
        name="qkv_weight",
    )
    q_got = dp_first(ak, as_, bk, bs)
    got = swap(send, "row", 1)
    own, sums_own, *parts = call(
        split_last,
        [arr((half, width), F32), arr((8, width), F32)] + [arr((half + 16, width))] * 3,
        [back, got],
        name="split_last",
    )
    got = [swap(parts[k - 1], "col", k) for k in (1, 2, 3)]
    grad_tokens, sums = call(
        last_sum,
        [arr((half, width), F32), arr((8, width), F32)],
        [own, sums_own, *got, grad_middle],
        name="last_sum",
    )

    q_sums = call(
        first_add_qkv,
        [arr((512, 128), F32), arr((512, 128)), arr((512, 128), F32), arr((512, 128))],
        q_got,
        name="first_add_qkv",
    )
    *qs, out_part = dp_second(q_sums, second_add_qkv, [(192, 128)] * 4 + [(256, 128)], "second_add_qkv")
    qs = [qs[0]] + [swap(qs[k], "col", k) for k in (1, 2, 3)]
    qs = call(stack_qkv, [arr((1024, 128))], [*qs, out_part], name="stack_qkv_grad")[0]
    q_all = dp_gather(qs)
    ms = call(stack, [arr((4, 512, 128))], ms, name="stack_mlp_grad")[0]
    m_all = dp_gather(ms)

    mix_send = after(mix_send, grad_tokens)
    got = swap(mix_send, "row", 1)
    parts = call(
        split_sum,
        [arr((half, width), F32)] + [arr((half, width))] * 3,
        [mix, got],
        name="split_mixed",
    )
    got = [swap(parts[k], "col", k) for k in (1, 2, 3)]
    mixed = call(
        mixed_sum,
        [arr((half, width))],
        [mid_own, parts[0], *got, b_proj.reshape(1, width)],
        name="mixed_sum",
    )[0]

    qkv_sum, out_sum = call(
        unpack_qkv,
        [arr(w_qkv.shape, F32), arr(w_out.shape, F32)],
        [qs, *q_all],
        us=2.0,
        name="unpack_qkv",
    )
    fc_sum, proj_sum = call(
        unpack_mlp,
        [arr(w_fc.shape, F32), arr(w_proj.shape, F32)],
        [ms, *m_all],
        us=3.0,
        name="unpack_mlp",
    )

    small = call(
        small_pack,
        [arr((16, width), F32)],
        [sums, out_shift, cot_shift, qv_shift, fc_shift],
        name="small_pack",
    )[0]
    for b in range(int(math.log2(lax.axis_size("dp"))) - 1):
        small = call(
            small_add, [arr((16, width), F32)], [small, swap(small, "dp", 2 << b)], name="small_add"
        )[0]
    gain, shift, qv, out_shift, fc_shift, proj_shift = call(
        small_unpack,
        [
            arr((2, width), F32),
            arr((2, width), F32),
            arr(b_qv.shape, F32),
            arr((1, width), F32),
            arr((1, 512), F32),
            arr((1, width), F32),
        ],
        [small, swap(small, "dp", 1)],
        name="small_unpack",
    )
    return (
        mixed,
        grad_tokens,
        gain,
        shift,
        qkv_sum,
        qv,
        out_sum,
        out_shift.reshape(b_out.shape),
        fc_sum,
        fc_shift.reshape(b_fc.shape),
        proj_sum,
        proj_shift.reshape(b_proj.shape),
    )


def solution(mesh):
    in_specs = (
        P(("dp", "row"), "col"),
        P("dp"),
        P(None, "col"),
        P(None, "col"),
        P(None, "col", "row"),
        P(None, ("row", "col")),
        P("row", "col"),
        P("col"),
        P("col", "row"),
        P(("row", "col")),
        P("row", "col"),
        P("col"),
        P(("dp", "row"), "col"),
    )
    out_specs = (
        P(("dp", "row"), "col"),
        P(("dp", "row"), "col"),
        P(None, "col"),
        P(None, "col"),
        P(None, "col", "row"),
        P(None, ("row", "col")),
        P("row", "col"),
        P("col"),
        P("col", "row"),
        P(("row", "col")),
        P("row", "col"),
        P("col"),
    )
    return jax.shard_map(shards, mesh=mesh, in_specs=in_specs, out_specs=out_specs, check_vma=False)
```

```python
import math

import jax
import jax.numpy as jnp
from jax import lax
from jax.experimental import pallas as pl
from jax.experimental.pallas import tpu as pltpu
from jax.sharding import PartitionSpec as P

D = 1024
HEAD_DIM = 64
EPS = 1e-05
NEGATIVE = -1e30
LOW = jnp.bfloat16
F32 = jnp.float32
FACTOR = 1.0 / math.sqrt(HEAD_DIM)
ROOT = math.sqrt(2.0 / math.pi)
CUBE = 0.044715
COLS = 4
PARTS = 4
OVER_ROWS = (((0,), (0,)), ((), ()))
OVER_COLS = (((1,), (1,)), ((), ()))
PLAIN = (((1,), (0,)), ((), ()))
ORDER = (
    "pack_all",
    "send_weights",
    "split_qkv",
    "split_weights",
    "send_tokens",
    "send_qkv_one",
    "pair_qkv",
    "send_qkv_two",
    "stack_tokens",
    "swap_tokens",
    "send_cotangent",
    "send_weights_one",
    "attend",
    "pair_weights",
    "stack_cotangent",
    "send_attended",
    "swap_cotangent",
    "send_weights_two",
    "stack_attended",
    "swap_attended",
    "join_all",
    "swap_w_out",
    "feed_forward",
    "feed_back",
    "swap_second",
    "mlp_weights",
    "send_mlp_one",
    "split_second",
    "send_second",
    "sum_second",
    "swap_branch",
    "swap_mixed",
    "back_out",
    "send_back_out",
    "weigh_out",
    "add_mlp_one",
    "send_mlp_two",
    "sum_attended",
    "add_mlp_two",
    "send_mlp_cols",
    "attend_back",
    "swap_first",
    "qkv_weights",
    "send_grad_one",
    "join_mlp_cols",
    "split_first",
    "send_first",
    "add_grad_one",
    "send_grad_two",
    "add_grad_two",
    "send_mlp_three",
    "sum_first",
    "send_grad_cols",
    "pack_small",
    "pair_mlp",
    "send_mlp_four",
    "join_grad",
    "send_grad_three",
    "send_mixed_two",
    "pair_grad",
    "send_grad_four",
    "send_mixed_three",
    "send_mixed_one",
    "unpack_mlp_all",
    "unpack_grad",
    "sum_mixed",
)
COST = {
    "stack_tokens": 50.0,
    "attend": 50.0,
    "attend_back": 50.0,
    "join_mlp_cols": 50.0,
    "sum_first": 50.0,
    "sum_attended": 2.0,
}


def swap(value, axis, k):
    return lax.ppermute(value, axis, [(i, i ^ k) for i in range(lax.axis_size(axis))])


def dot(a, b, dims=PLAIN):
    return lax.dot_general(a, b, dims, preferred_element_type=F32)


def arr(shape, dtype=LOW):
    return jax.ShapeDtypeStruct(shape, dtype)


def place():
    return lax.axis_index("col"), lax.rem(lax.axis_index("dp"), PARTS)


def call(body, outs, args, hbm=(), scratch=(), name=None, room=None):
    whole = pl.BlockSpec(memory_space=pltpu.VMEM)
    anywhere = pl.BlockSpec(memory_space=pl.ANY)
    held = sum(math.prod(a.shape) * a.dtype.itemsize for a in list(args) + list(outs))
    held += sum(math.prod(a.shape) * 4 for a in scratch if len(a.shape) > 1)
    return pl.pallas_call(
        body,
        out_shape=list(outs),
        in_specs=[anywhere if i in hbm else whole for i in range(len(args))],
        out_specs=[whole] * len(outs),
        scratch_shapes=list(scratch),
        compiler_params=pltpu.CompilerParams(vmem_limit_bytes=room or held + 3 * 1024 * 1024),
        cost_estimate=pl.CostEstimate(
            flops=int(COST.get(name, 0.001) * 1e9), bytes_accessed=1024, transcendentals=0
        ),
        name=name,
    )(*args)


def run_copies(copies, sems):
    copies = [pltpu.make_async_copy(a, b, sems.at[i]) for i, (a, b) in enumerate(copies)]
    for copy in copies:
        copy.start()
    for copy in copies:
        copy.wait()


def pack(w_qkv, w_fc, w_proj, w_out, gain, shift, b_out, f1, f2, f3, p0, full, sems):
    c, d = place()
    units = w_fc.shape[1] // COLS
    unit = units // PARTS
    quarter = w_out.shape[0] // PARTS
    piece = w_qkv.shape[1] // PARTS
    heads = w_qkv.shape[2] // COLS
    full[...] = jnp.zeros_like(full)
    copies = [(gain, full.at[0:2]), (shift, full.at[2:4]), (b_out, full.at[4:5])]
    for k, f in ((1, f1), (2, f2), (3, f3)):
        rows = pl.ds(pl.multiple_of(d * piece, piece), piece)
        cols = pl.ds(pl.multiple_of((c ^ k) * heads, heads), heads)
        for j in range(3):
            copies.append((w_qkv.at[j, rows, cols], f.at[pl.ds(j * piece, piece)]))
        start = pl.ds(pl.multiple_of((c ^ k) * units + d * unit, unit), unit)
        mine = pl.ds(pl.multiple_of(d * quarter, quarter), quarter)
        copies.append((w_fc.at[:, start], f.at[pl.ds(192, 256)]))
        for j in range(2):
            cols = pl.ds(j * 128, 128)
            copies.append((w_out.at[mine, cols], f.at[pl.ds(448 + j * 128, 128)]))
            copies.append((w_proj.at[start, cols], f.at[pl.ds(704 + j * 128, 128)]))
    run_copies(copies, sems)
    value = full[...]
    high = value.astype(LOW)
    low = (value - high.astype(F32)).astype(LOW).astype(F32)
    high = high.astype(F32)
    rows = jnp.concatenate([high[:, :128], high[:, 128:], low[:, :128], low[:, 128:]], 0)
    rows = rows.astype(LOW)
    p0[...] = rows
    for f in (f1, f2, f3):
        f[960:992, :] = rows


def split_q(f1, f2, f3, qa, qb):
    for k, f in enumerate((f1, f2, f3)):
        qa[k] = f[0:96, :]
        qb[k] = f[96:192, :]


def split_rest(f1, f2, f3, left, right):
    for k, f in enumerate((f1, f2, f3)):
        right[k, 0:256, :] = f[192:448, :]
        left[k, 0:256, :] = f[448:704, :]
        left[k, 256:384, :] = f[704:832, :]
        right[k, 256:384, :] = f[832:960, :]


def pair(a, b, c, d, left, right):
    left[0] = a[...]
    left[1] = b[...]
    right[0] = c[...]
    right[1] = d[...]


def stack(*refs):
    for i, ref in enumerate(refs[:-1]):
        refs[-1][i] = ref[...]


def norm_parts(blocks):
    total = sum(jnp.sum(b, -1, keepdims=True) for b in blocks)
    squares = sum(jnp.sum(b * b, -1, keepdims=True) for b in blocks)
    mean = total * (1.0 / D)
    factor = lax.rsqrt(squares * (1.0 / D) - mean * mean + EPS)
    return mean, factor


def head_lanes(shape):
    return lax.broadcasted_iota(jnp.int32, shape, 1) < HEAD_DIM


def attention(*refs):
    xo, xs = refs[0], refs[1]
    heads, (qa0, qa1, qb0, qb1, w, b_qv, segment) = refs[2:6], refs[6:13]
    first, x_all, wq, params, qkv, probs, attended, bias, sems = refs[13:22]
    c, d = place()
    piece = 64
    copies = []
    for j in range(3):
        copies.append(
            pltpu.make_async_copy(
                w.at[j, :, pl.ds(pl.multiple_of(c * 128, 128), 128)],
                wq.at[pl.ds(0, 256), pl.ds(j * 128, 128)],
                sems.at[j],
            )
        )
        copies[-1].start()
    for k in range(COLS):
        rows = (heads[k][...] if k == 0 else heads[k][960:992, :]).astype(F32)
        full = rows[0:16] + rows[16:32]
        params[:, k * 256 : k * 256 + 128] = full[0:8]
        params[:, k * 256 + 128 : (k + 1) * 256] = full[8:16]
    lefts = (qa0.at[0], qa0.at[1], qa1.at[0], qa1.at[1])
    rights = (qb0.at[0], qb1.at[0], qb0.at[1], qb1.at[1])
    for m in range(PARTS):
        for k in range(1, COLS):
            start = pl.multiple_of(k * 256 + (d ^ m) * piece, piece)
            both = jnp.concatenate([lefts[m][k - 1], rights[m][k - 1]], 0)
            for j in range(3):
                wq[pl.ds(start, piece), j * 128 : (j + 1) * 128] = both[
                    j * piece : (j + 1) * piece, :
                ]
    for half, srcs in enumerate((xo, xs)):

        @pl.loop(0, 8)
        def _(i):
            rows = pl.ds(pl.multiple_of(i * 32, 32), 32)
            into = pl.ds(pl.multiple_of(half * 256 + i * 32, 32), 32)
            low = [srcs[k, rows, :] for k in range(COLS)]
            blocks = [b.astype(F32) for b in low]
            mean, factor = norm_parts(blocks)
            for k in range(COLS):
                cols = slice(k * 256, (k + 1) * 256)
                out = (blocks[k] - mean) * factor * params[0:1, cols] + params[2:3, cols]
                first[into, cols] = out.astype(LOW)
                x_all[into, cols] = low[k]

    r = lax.axis_index("row")
    ids = segment[...].astype(F32)
    ids = jnp.where(r == 0, ids, jnp.concatenate([ids[:, 256:512], ids[:, 0:256]], 1))
    spot = lax.rem(lax.broadcasted_iota(jnp.int32, (1, 512), 1) + r * 256, 512).astype(F32)
    for i in range(4):
        cols = slice(i * 128, (i + 1) * 128)
        there = [
            jnp.concatenate([jnp.broadcast_to(v[:, cols], (128, 128)).T] * 4, 1)
            for v in (ids, spot)
        ]
        allowed = (there[0] == ids) & (there[1] >= spot)
        bias[cols, :] = jnp.where(allowed, 0.0, NEGATIVE)
    for copy in copies:
        copy.wait()
    added = jnp.concatenate([b_qv[0:1, :], jnp.zeros((1, 128), F32), b_qv[1:2, :]], 1)

    @pl.loop(0, 4)
    def _(i):
        rows = pl.ds(pl.multiple_of(i * 128, 128), 128)
        qkv[rows, :] = (dot(first[rows, :], wq[...]) + added).astype(LOW)

    @pl.loop(0, 4)
    def _(i):
        rows = pl.ds(pl.multiple_of(i * 128, 128), 128)
        lanes = head_lanes((128, 128))
        query = qkv[rows, 0:128]
        keys = qkv[:, 128:256]
        values = qkv[:, 256:384]
        outs = []
        for h in range(2):
            mine = jnp.where(lanes == (h == 0), query, jnp.zeros_like(query))
            score = dot(mine, keys, OVER_COLS) * FACTOR + bias[rows, :]
            expo = jnp.exp(score - jnp.max(score, -1, keepdims=True))
            weights = expo / jnp.sum(expo, -1, keepdims=True)
            probs[h, rows, :] = weights
            outs.append(dot(weights.astype(LOW), values))
        attended[rows, :] = jnp.where(lanes, outs[0], outs[1]).astype(LOW)


def by_part(a0, a1, b0, b1):
    return (
        (a0.at[0], a0.at[1], a1.at[0], a1.at[1]),
        (b0.at[0], b1.at[0], b0.at[1], b1.at[1]),
    )


def join_weights(w_out, w_fc, w_proj, a0, a1, b0, b1, out, fc, proj, sems):
    c, d = place()
    copies = [(w_out, out.at[:, pl.ds(0, 256)])]
    for m in range(PARTS):
        start = pl.ds(pl.multiple_of(c * 512 + (d ^ m) * 128, 128), 128)
        copies.append((w_fc.at[:, start], fc.at[pl.ds(0, 256), pl.ds(m * 128, 128)]))
        copies.append((w_proj.at[start], proj.at[pl.ds(m * 128, 128), pl.ds(0, 256)]))
    copies = [pltpu.make_async_copy(a, b, sems.at[i]) for i, (a, b) in enumerate(copies)]
    for copy in copies:
        copy.start()
    lefts, rights = by_part(a0, a1, b0, b1)
    for m in range(PARTS):
        rows = pl.ds(pl.multiple_of((d ^ m) * 128, 128), 128)
        mine = slice(m * 128, (m + 1) * 128)
        for k in range(1, COLS):
            one, two = slice(k * 256, k * 256 + 128), slice(k * 256 + 128, (k + 1) * 256)
            out[rows, one] = lefts[m][k - 1, 0:128, :]
            out[rows, two] = lefts[m][k - 1, 128:256, :]
            fc[k * 256 : (k + 1) * 256, mine] = rights[m][k - 1, 0:256, :]
            proj[mine, one] = lefts[m][k - 1, 256:384, :]
            proj[mine, two] = rights[m][k - 1, 256:384, :]
    for copy in copies:
        copy.wait()


def forward(*refs):
    mine, theirs = refs[0:2]
    w_own, w_sib, x_all, params, fc, b_fc = refs[2:8]
    att_own, middle, second, hidden, mid_own, att_sib, shift = refs[8:15]
    c, d = place()
    for m in range(PARTS):
        here = pl.ds(pl.multiple_of((d ^ m) * 128, 128), 128)
        shift[0:1, m * 128 : (m + 1) * 128] = b_fc[0:1, here]
    for k in range(COLS):
        cols = pl.ds(pl.multiple_of((c ^ k) * 128, 128), 128)
        att_own[:, cols] = mine[k]
        att_sib[0:256, cols] = theirs[k, 256:512, :]
        att_sib[256:512, cols] = theirs[k, 0:256, :]

    @pl.loop(0, 4)
    def _(i):
        rows = pl.ds(pl.multiple_of(i * 128, 128), 128)
        value = dot(att_own[rows, :], w_own[...]) + dot(att_sib[rows, :], w_sib[...])
        value = value + x_all[rows, :].astype(F32) + params[4:5, :]
        middle[rows, :] = value
        mean, factor = norm_parts([value])
        out = (value - mean) * factor * params[1:2, :] + params[3:4, :]
        second[rows, :] = out.astype(LOW)
        hidden[rows, :] = dot(second[rows, :], fc[...]) + shift[0:1, :]

    mid_own[...] = middle[0:256, 0:256]


def backward(*refs):
    co, cs = refs[0:2]
    middle, hidden, fc, proj, params = refs[2:7]
    cot, active, grad_hidden, back, send, sums, fc_shift, cot_shift, shift = refs[7:16]
    for k in range(COLS):
        cols = slice(k * 256, (k + 1) * 256)
        cot[0:256, cols] = co[k]
        cot[256:512, cols] = cs[k]
    sums[...] = jnp.zeros_like(sums)
    shift[...] = jnp.zeros_like(shift)
    cot_shift[...] = jnp.sum(cot[:, 0:256].astype(F32), 0, keepdims=True)

    def step(start):
        rows = pl.ds(pl.multiple_of(start, 128), 128)
        v = hidden[rows, :]
        t = jnp.tanh(ROOT * (v + CUBE * (v * v * v)))
        active[rows, :] = (0.5 * v * (1.0 + t)).astype(LOW)
        slope = 0.5 * (1.0 + t) + 0.5 * v * (1.0 - t * t) * (ROOT * (1.0 + 3.0 * CUBE * (v * v)))
        low = (dot(cot[rows, :], proj[...], OVER_COLS) * slope).astype(LOW)
        grad_hidden[rows, :] = low
        shift[0:1, :] += jnp.sum(low.astype(F32), 0, keepdims=True)
        grad = dot(low, fc[...], OVER_COLS)
        mean, factor = norm_parts([middle[rows, :]])
        normed = (middle[rows, :] - mean) * factor
        sums[0:1, :] += jnp.sum(grad * normed, 0, keepdims=True)
        sums[1:2, :] += jnp.sum(grad, 0, keepdims=True)
        scaled = grad * params[1:2, :]
        one = jnp.mean(scaled, -1, keepdims=True)
        two = jnp.mean(scaled * normed, -1, keepdims=True)
        return factor * (scaled - one - normed * two)

    @pl.loop(0, 2)
    def _(i):
        send[pl.ds(pl.multiple_of(i * 128, 128), 128), :] = step(256 + i * 128).astype(LOW)

    @pl.loop(0, 2)
    def _(i):
        back[pl.ds(pl.multiple_of(i * 128, 128), 128), :] = step(i * 128)

    c, d = place()
    for m in range(PARTS):
        here = pl.ds(pl.multiple_of((d ^ m) * 128, 128), 128)
        fc_shift[0:1, here] = shift[0:1, m * 128 : (m + 1) * 128]


def mlp_grads(second, grad_hidden, active, cot, proj, fk, fs, pk, ps, mine, left, right):
    for k in range(COLS):
        cols = slice(k * 256, (k + 1) * 256)
        value = dot(second[:, cols], grad_hidden[...], OVER_ROWS).astype(LOW)
        for m in range(PARTS):
            (fs if m % 2 else fk)[m // 2, cols, :] = value[:, m * 128 : (m + 1) * 128]
    for m in range(PARTS):
        value = dot(active[:, m * 128 : (m + 1) * 128], cot[...], OVER_ROWS).astype(LOW)
        for i in range(2 * COLS):
            rows = slice(i * 128, (i + 1) * 128)
            (ps if m // 2 else pk)[m % 2, rows, :] = value[:, rows]
    mine[...] = dot(active[0:256, :], proj[...])
    theirs = dot(active[256:512, :], proj[...]).astype(LOW)
    left[...] = theirs[:, 0:512]
    right[...] = theirs[:, 512:1024]


def first_add(ka, ra, kb, rb, ha, sa, hb, sb):
    for keep, got, have, send in ((ka, ra, ha, sa), (kb, rb, hb, sb)):
        have[...] = keep[0].astype(F32) + got[0].astype(F32)
        send[...] = (keep[1].astype(F32) + got[1].astype(F32)).astype(LOW)


def second_add_mlp(ha, ra, hb, rb, *outs):
    for k, out in enumerate(outs):
        rows = slice(k * 256, (k + 1) * 256)
        out[0:256, :] = (ha[rows, :] + ra[rows, :].astype(F32)).astype(LOW)
        out[256:512, :] = (hb[rows, :] + rb[rows, :].astype(F32)).astype(LOW)


def second_add_qkv(ha, ra, hb, rb, *outs):
    for k, out in enumerate(outs[:-1]):
        have, got = (ha, ra) if k < 2 else (hb, rb)
        rows = slice((k % 2) * 192, (k % 2) * 192 + 192)
        out[...] = (have[rows, :] + got[rows, :].astype(F32)).astype(LOW)
    for j, (have, got) in enumerate(((ha, ra), (hb, rb))):
        value = have[384:512, :] + got[384:512, :].astype(F32)
        outs[-1][j * 128 : (j + 1) * 128, :] = value.astype(LOW)


def split_sum(back, got, o0, o1, o2, o3):
    for k, out in enumerate((o0, o1, o2, o3)):
        cols = slice(k * 256, (k + 1) * 256)
        out[...] = (back[:, cols] + got[:, cols].astype(F32)).astype(out.dtype)


def middle_sum(cot, o0, g1, g2, g3, out, low):
    value = cot[...].astype(F32) + (
        o0[...] + g1[...].astype(F32) + g2[...].astype(F32) + g3[...].astype(F32)
    )
    out[...] = value
    low[...] = value.astype(LOW)


def mixed_sum(middle, o0, g1, g2, g3, b_proj, out):
    value = o0[...] + g1[...].astype(F32) + g2[...].astype(F32) + g3[...].astype(F32)
    out[...] = (middle[...] + value + b_proj[...]).astype(LOW)


def grad_out(own, other, w_out, o0, o1, o2, o3):
    c, d = place()
    for k, out in enumerate((o0, o1, o2, o3)):
        rows = pl.ds(pl.multiple_of((c ^ k) * 128, 128), 128)
        w = w_out[rows, :]
        out[0:256, :] = dot(own[...], w, OVER_COLS).astype(out.dtype)
        out[256:512, :] = dot(other[...], w, OVER_COLS).astype(out.dtype)


def out_weight(att, own, other, mix, left, right, out, shift, o0, o1, o2, o3):
    for k, part in enumerate((o0, o1, o2, o3)):
        cols = slice((k % 2) * 256, (k % 2 + 1) * 256)
        total = mix[:, k * 256 : (k + 1) * 256] + (left, right)[k // 2][:, cols].astype(F32)
        part[...] = total.astype(part.dtype)
    out[...] = (
        dot(att[0:256, :], own[...], OVER_ROWS) + dot(att[256:512, :], other[...], OVER_ROWS)
    ).astype(LOW)
    shift[...] = jnp.sum(own[...].astype(F32), 0, keepdims=True) + jnp.sum(
        other[...].astype(F32), 0, keepdims=True
    )


def sum_datt(o0, g1, g2, g3, out):
    value = o0[...] + g1[...].astype(F32) + g2[...].astype(F32) + g3[...].astype(F32)
    out[...] = value.astype(LOW)


def attention_back(*refs):
    datt, qkv, probs, wq, x_all, params, sums2 = refs[0:7]
    dqkv, back, send, qv_shift = refs[7:11]
    scores, lows, sums = refs[11:14]

    @pl.loop(0, 4)
    def _(i):
        rows = pl.ds(pl.multiple_of(i * 128, 128), 128)
        lanes = head_lanes((128, 128))
        keys = qkv[:, 128:256]
        values = qkv[:, 256:384]
        grad = datt[rows, :]
        outs = []
        for h in range(2):
            mine = jnp.where(lanes == (h == 0), grad, jnp.zeros_like(grad))
            gp = dot(mine, values, OVER_COLS)
            weights = probs[h, rows, :]
            centre = jnp.sum(weights * gp, -1, keepdims=True)
            score = (weights * (gp - centre)).astype(LOW)
            scores[h, rows, :] = score
            lows[h, rows, :] = weights.astype(LOW)
            outs.append(dot(score, keys))
        dqkv[rows, 0:128] = (jnp.where(lanes, outs[0], outs[1]) * FACTOR).astype(LOW)

    lanes = head_lanes((512, 128))
    gk = [dot(scores[h], qkv[:, 0:128], OVER_ROWS) for h in range(2)]
    dqkv[:, 128:256] = (jnp.where(lanes, gk[0], gk[1]) * FACTOR).astype(LOW)
    gv = [dot(lows[h], datt[...], OVER_ROWS) for h in range(2)]
    dqkv[:, 256:384] = jnp.where(lanes, gv[0], gv[1]).astype(LOW)
    qv_shift[...] = jnp.sum(dqkv[...].astype(F32), 0, keepdims=True)
    sums[...] = jnp.zeros_like(sums)

    def step(start):
        rows = pl.ds(pl.multiple_of(start, 128), 128)
        grad = dot(dqkv[rows, :], wq[...], OVER_COLS)
        x = x_all[rows, :].astype(F32)
        mean, factor = norm_parts([x])
        normed = (x - mean) * factor
        sums[0:1, :] += jnp.sum(grad * normed, 0, keepdims=True)
        sums[1:2, :] += jnp.sum(grad, 0, keepdims=True)
        scaled = grad * params[0:1, :]
        one = jnp.mean(scaled, -1, keepdims=True)
        two = jnp.mean(scaled * normed, -1, keepdims=True)
        return factor * (scaled - one - normed * two)

    @pl.loop(0, 2)
    def _(i):
        send[pl.ds(pl.multiple_of(i * 128, 128), 128), :] = step(256 + i * 128).astype(LOW)

    @pl.loop(0, 2)
    def _(i):
        back[pl.ds(pl.multiple_of(i * 128, 128), 128), :] = step(i * 128)

    rows = jnp.concatenate(
        [sums[0:1, :], sums2[0:1, :], sums[1:2, :], sums2[1:2, :], jnp.zeros((4, D), F32)], 0
    )
    back[256:264, :] = rows
    high = rows.astype(LOW).astype(F32)
    send[256:272, :] = jnp.concatenate([high, rows - high], 0).astype(LOW)


def split_last(back, got, o0, s0, o1, o2, o3):
    more = got[256:272, :].astype(F32)
    sums = back[256:264, :] + more[0:8] + more[8:16]
    high = sums.astype(LOW).astype(F32)
    both = jnp.concatenate([high, sums - high], 0).astype(LOW)
    o0[...] = back[0:256, 0:256] + got[0:256, 0:256].astype(F32)
    s0[...] = sums[:, 0:256]
    for k, out in ((1, o1), (2, o2), (3, o3)):
        cols = slice(k * 256, (k + 1) * 256)
        out[0:256, :] = (back[0:256, cols] + got[0:256, cols].astype(F32)).astype(LOW)
        out[256:272, :] = both[:, cols]


def last_sum(o0, s0, g1, g2, g3, middle, out, sums):
    out[...] = middle[...] + (
        o0[...]
        + g1[0:256, :].astype(F32)
        + g2[0:256, :].astype(F32)
        + g3[0:256, :].astype(F32)
    )
    value = s0[...]
    for g in (g1, g2, g3):
        more = g[256:272, :].astype(F32)
        value = value + more[0:8] + more[8:16]
    sums[...] = value


def qkv_weight(first, dqkv, w_out, ak, as_, bk, bs, full):
    c, d = place()

    @pl.loop(0, 4)
    def _(k):
        cols = pl.ds(pl.multiple_of(k * 256, 256), 256)
        full[cols, :] = dot(first[:, cols], dqkv[...], OVER_ROWS)

    for m in range(PARTS):
        outs = ((as_ if m % 2 else ak, m // 2), (bs if m // 2 else bk, m % 2))
        rows = pl.ds(pl.multiple_of((d ^ m) * 128, 128), 128)
        for j, (out, index) in enumerate(outs):
            out[index, 384:512, :] = w_out[rows, j * 128 : (j + 1) * 128]
        for k in range(COLS):
            out, index = outs[k // 2]
            start = pl.ds(pl.multiple_of(k * 256 + (d ^ m) * 64, 64), 64)
            for j in range(3):
                row = (k % 2) * 192 + j * 64
                out[index, row : row + 64, :] = full[start, j * 128 : (j + 1) * 128].astype(LOW)


def unpack_qkv(a0, a1, b0, b1, out, w_out, gain, shift, b_qv, b_out, b_fc, b_proj):
    c, d = place()
    lefts, rights = by_part(a0, a1, b0, b1)
    for m in range(PARTS):
        rows = pl.ds(pl.multiple_of((d ^ m) * 64, 64), 64)
        for k in range(COLS):
            src = (lefts if k < 2 else rights)[m]
            cols = pl.ds(pl.multiple_of((c ^ k) * 128, 128), 128)
            for j in range(3):
                start = (k % 2) * 192 + j * 64
                out[j, rows, cols] = src[start : start + 64, :].astype(F32)
        rows = pl.ds(pl.multiple_of((d ^ m) * 128, 128), 128)
        w_out[rows, 0:128] = lefts[m][384:512, :].astype(F32)
        w_out[rows, 128:256] = rights[m][384:512, :].astype(F32)
    total = sum(left[512:576, :].astype(F32) for left in lefts)
    total = total[0:32] + total[32:64]
    for j, rows in enumerate((total[0:16], total[16:32])):
        cols = slice(j * 128, (j + 1) * 128)
        gain[:, cols] = rows[0:2]
        shift[:, cols] = rows[2:4]
        b_out[:, cols] = rows[4:5]
        b_proj[:, cols] = rows[5:6]
        b_qv[j : j + 1, :] = rows[6:7]
        b_fc[0:1, j * 128 : (j + 1) * 128] = rows[7:8]
        b_fc[0:1, 256 + j * 128 : 256 + (j + 1) * 128] = rows[8:9]


def unpack_mlp(a0, a1, b0, b1, fc, proj):
    c, d = place()
    lefts, rights = by_part(a0, a1, b0, b1)
    for m in range(PARTS):
        for k in range(COLS):
            here = pl.ds(pl.multiple_of((c ^ k) * 512 + (d ^ m) * 128, 128), 128)
            fc[:, here] = lefts[m][k * 256 : (k + 1) * 256, :].astype(F32)
            for j in range(2):
                row = k * 256 + j * 128
                cols = slice(j * 128, (j + 1) * 128)
                proj[here, cols] = rights[m][row : row + 128, :].astype(F32)


def join_mlp(m0, m1, m2, m3, left, right):
    for k, part in enumerate((m0, m1, m2, m3)):
        rows = slice(k * 256, (k + 1) * 256)
        left[rows, :] = part[0:256, :]
        right[rows, :] = part[256:512, :]


def join_qkv(q0, q1, q2, q3, w_out, small, left, right):
    for j, (out, one, two) in enumerate(((left, q0, q1), (right, q2, q3))):
        out[0:192, :] = one[...]
        out[192:384, :] = two[...]
        out[384:512, :] = w_out[j * 128 : (j + 1) * 128, :]
    full = small[...]
    high = full.astype(LOW).astype(F32)
    low = full - high
    rows = [high[:, 0:128], high[:, 128:256], low[:, 0:128], low[:, 128:256]]
    left[512:576, :] = jnp.concatenate(rows, 0).astype(LOW)


def small_pack(sums, out_shift, cot_shift, qv, fc_shift, out):
    out[0:4, :] = sums[0:4, :]
    out[4:5, :] = out_shift[...]
    out[5:6, :] = cot_shift[...]
    out[6:7, 0:128] = qv[0:1, 0:128]
    out[6:7, 128:256] = qv[0:1, 256:384]
    out[7:8, :] = fc_shift[0:1, 0:256]
    out[8:9, :] = fc_shift[0:1, 256:512]
    out[9:16, :] = jnp.zeros((7, 256), F32)


def after(value, *others):
    return lax.optimization_barrier((value, others))[0]


def high_bits():
    return [1 << b for b in range(2, int(math.log2(lax.axis_size("dp"))))]


def over_high(parts):
    for k in high_bits():
        parts = [(o.astype(F32) + swap(o, "dp", k).astype(F32)).astype(LOW) for o in parts]
    return parts


def three(parts, axis="col"):
    return [swap(part, axis, k + 1) for k, part in enumerate(parts)]


def pair_arrays(left, right):
    return [arr((2,) + left.shape), arr((2,) + right.shape)]


def shards(
    tokens,
    segment,
    ln_gain,
    ln_bias,
    w_qkv,
    b_qv,
    w_out,
    b_out,
    w_fc,
    b_fc,
    w_proj,
    b_proj,
    cotangent,
):
    half, width = tokens.shape
    group = 2 * half
    dma = pltpu.SemaphoreType.DMA
    last = []
    v = {}
    steps = {}

    def run(body, outs, args, **keys):
        results = call(body, outs, after(list(args), last), **keys)
        last[:] = results[:1]
        return results

    def now(value):
        return after(value, last)

    def step(function):
        steps[function.__name__] = function
        return function

    def send_pair(left, right, one, two):
        left, right = now([left, right])
        return swap(left, "dp", one), swap(right, "dp", two)

    def join_pair(name, left, one, right, two):
        return run(pair, pair_arrays(left, right), [left, one, right, two], name=name)

    def first_sum(name, ka, kb, got):
        rows = ka.shape[1]
        outs = [arr((rows, 128), F32), arr((rows, 128))] * 2
        return run(first_add, outs, [ka, got[0], kb, got[1]], name=name)

    def split(name, back, got):
        outs = [arr((half, width), F32)] + [arr((half, width))] * 3
        return run(split_sum, outs, [back, got], name=name)

    @step
    def pack_all():
        *v["sent"], v["head"] = run(
            pack,
            [arr((992, 128))] * 3 + [arr((32, 128))],
            [w_qkv, w_fc, w_proj, w_out, ln_gain, ln_bias, b_out.reshape(1, width)],
            hbm=range(7),
            scratch=[pltpu.VMEM((8, width), F32), dma((27,))],
            name="pack_all",
            room=56 * 1024 * 1024,
        )

    @step
    def send_weights():
        v["f"] = three(now(v["sent"]))

    @step
    def split_qkv():
        v["qa"], v["qb"] = run(split_q, [arr((3, 96, 128))] * 2, v["f"], name="split_qkv")

    @step
    def split_weights():
        outs = [arr((3, 384, 128))] * 2
        v["wa"], v["wb"] = run(split_rest, outs, v["f"], name="split_weights")

    @step
    def send_tokens():
        v["x"] = three([now(tokens)] * 3)

    @step
    def send_qkv_one():
        v["q1"] = send_pair(v["qa"], v["qb"], 1, 2)

    @step
    def pair_qkv():
        v["qa"], v["qb"] = join_pair("pair_qkv", v["qa"], v["q1"][0], v["qb"], v["q1"][1])

    @step
    def send_qkv_two():
        v["q2"] = send_pair(v["qa"], v["qb"], 2, 1)

    @step
    def stack_tokens():
        outs = [arr((4, half, width))]
        v["x_own"] = run(stack, outs, [tokens, *v["x"]], name="stack_tokens")[0]

    @step
    def swap_tokens():
        v["x_sib"] = swap(now(v["x_own"]), "row", 1)

    @step
    def send_cotangent():
        v["cot"] = three([now(cotangent)] * 3)

    @step
    def send_weights_one():
        v["w1"] = send_pair(v["wa"], v["wb"], 1, 2)

    @step
    def attend():
        (
            v["first"],
            v["x_all"],
            v["wq"],
            v["params"],
            v["qkv"],
            v["probs"],
            v["attended"],
        ) = run(
            attention,
            [
                arr((group, D)),
                arr((group, D)),
                arr((D, 384)),
                arr((8, D), F32),
                arr((group, 384)),
                arr((2, group, group), F32),
                arr((group, 128)),
            ],
            [
                v["x_own"],
                v["x_sib"],
                v["head"],
                *v["f"],
                v["qa"],
                v["q2"][0],
                v["qb"],
                v["q2"][1],
                w_qkv,
                b_qv,
                segment.reshape(1, group),
            ],
            hbm=(10,),
            scratch=[pltpu.VMEM((group, group), F32), dma((3,))],
            name="attend",
        )

    @step
    def pair_weights():
        v["wa"], v["wb"] = join_pair("pair_weights", v["wa"], v["w1"][0], v["wb"], v["w1"][1])

    @step
    def send_weights_two():
        v["w2"] = send_pair(v["wa"], v["wb"], 2, 1)

    @step
    def stack_cotangent():
        outs = [arr((4, half, width))]
        v["cot_own"] = run(stack, outs, [cotangent, *v["cot"]], name="stack_cotangent")[0]

    @step
    def swap_cotangent():
        v["cot_sib"] = swap(now(v["cot_own"]), "row", 1)

    @step
    def send_attended():
        v["att"] = three([now(v["attended"])] * 3)

    @step
    def stack_attended():
        outs = [arr((4, group, 128))]
        v["att_four"] = run(stack, outs, [v["attended"], *v["att"]], name="stack_attended")[0]

    @step
    def swap_attended():
        v["att_sib"] = swap(now(v["att_four"]), "row", 1)

    @step
    def join_all():
        v["w_own"], v["fc"], v["proj"] = run(
            join_weights,
            [arr((512, D)), arr((D, 512)), arr((512, D))],
            [w_out, w_fc, w_proj, v["wa"], v["w2"][0], v["wb"], v["w2"][1]],
            hbm=(0, 1, 2),
            scratch=[dma((9,))],
            name="join_all",
        )

    @step
    def swap_w_out():
        v["w_sib"] = swap(now(v["w_own"]), "row", 1)

    @step
    def feed_forward():
        v["att_own"], v["middle"], v["second"], v["hidden"], v["mid_own"] = run(
            forward,
            [
                arr((group, 512)),
                arr((group, D), F32),
                arr((group, D)),
                arr((group, 512), F32),
                arr((half, width), F32),
            ],
            [
                v["att_four"],
                v["att_sib"],
                v["w_own"],
                v["w_sib"],
                v["x_all"],
                v["params"],
                v["fc"],
                b_fc.reshape(1, 512),
            ],
            scratch=[pltpu.VMEM((group, 512), LOW), pltpu.VMEM((8, 512), F32)],
            name="feed_forward",
        )

    @step
    def feed_back():
        (
            v["cot_all"],
            v["active"],
            v["grad_hidden"],
            v["back"],
            v["send"],
            v["sums2"],
            v["fc_shift"],
            v["cot_shift"],
        ) = run(
            backward,
            [
                arr((group, D)),
                arr((group, 512)),
                arr((group, 512)),
                arr((half, D), F32),
                arr((half, D)),
                arr((2, D), F32),
                arr((1, 512), F32),
                arr((1, width), F32),
            ],
            [v["cot_own"], v["cot_sib"], v["middle"], v["hidden"], v["fc"], v["proj"], v["params"]],
            scratch=[pltpu.VMEM((8, 512), F32)],
            name="feed_back",
        )

    @step
    def swap_second():
        v["got"] = swap(now(v["send"]), "row", 1)

    @step
    def mlp_weights():
        v["fk"], v["fs"], v["pk"], v["ps"], v["mix"], *v["mix_send"] = run(
            mlp_grads,
            [arr((2, 1024, 128))] * 4 + [arr((half, D), F32)] + [arr((half, D // 2))] * 2,
            [v["second"], v["grad_hidden"], v["active"], v["cot_all"], v["proj"]],
            name="mlp_weights",
        )

    @step
    def send_mlp_one():
        v["m1"] = send_pair(v["fs"], v["ps"], 1, 2)

    @step
    def split_second():
        v["own"], *v["parts"] = split("split_second", v["back"], v["got"])

    @step
    def send_second():
        v["mid"] = three(now(v["parts"]))

    @step
    def sum_second():
        v["grad_middle"], v["branch"] = run(
            middle_sum,
            [arr((half, width), F32), arr((half, width))],
            [cotangent, v["own"], *v["mid"]],
            name="sum_second",
        )

    @step
    def swap_branch():
        v["other"] = swap(now(v["branch"]), "row", 1)

    @step
    def swap_mixed():
        v["mix_got"] = [swap(part, "row", 1) for part in now(v["mix_send"])]

    @step
    def back_out():
        v["att_sum"], *v["att_parts"] = run(
            grad_out,
            [arr((group, 128), F32)] + [arr((group, 128))] * 3,
            [v["branch"], v["other"], w_out],
            name="back_out",
        )

    @step
    def send_back_out():
        v["datt"] = three(now(v["att_parts"]))

    @step
    def weigh_out():
        v["out_grad"], v["out_shift"], v["mix"], *v["mix_parts"] = run(
            out_weight,
            [arr(w_out.shape), arr((1, width), F32), arr((half, width), F32)]
            + [arr((half, width))] * 3,
            [v["att_own"], v["branch"], v["other"], v["mix"], *v["mix_got"]],
            name="weigh_out",
        )

    @step
    def add_mlp_one():
        v["ha"], v["sa"], v["hb"], v["sb"] = first_sum("add_mlp_one", v["fk"], v["pk"], v["m1"])

    @step
    def send_mlp_two():
        v["m2"] = send_pair(v["sa"], v["sb"], 2, 1)

    @step
    def sum_attended():
        v["att_sum"] = run(
            sum_datt, [arr((group, 128))], [v["att_sum"], *v["datt"]], name="sum_attended"
        )[0]

    @step
    def add_mlp_two():
        ms = run(
            second_add_mlp,
            [arr((512, 128))] * 4,
            [v["ha"], v["m2"][0], v["hb"], v["m2"][1]],
            name="add_mlp_two",
        )
        v["ms"] = over_high(ms)

    @step
    def send_mlp_cols():
        v["mz"] = three(now(v["ms"][1:]))

    @step
    def attend_back():
        v["dqkv"], v["back"], v["send"], v["qv_shift"] = run(
            attention_back,
            [
                arr((group, 384)),
                arr((half + 8, D), F32),
                arr((half + 16, D)),
                arr((1, 384), F32),
            ],
            [v["att_sum"], v["qkv"], v["probs"], v["wq"], v["x_all"], v["params"], v["sums2"]],
            scratch=[
                pltpu.VMEM((2, group, group), LOW),
                pltpu.VMEM((2, group, group), LOW),
                pltpu.VMEM((8, D), F32),
            ],
            name="attend_back",
        )

    @step
    def swap_first():
        v["got"] = swap(now(v["send"]), "row", 1)

    @step
    def qkv_weights():
        v["ak"], v["as"], v["bk"], v["bs"] = run(
            qkv_weight,
            [arr((2, 512, 128))] * 4,
            [v["first"], v["dqkv"], v["out_grad"]],
            scratch=[pltpu.VMEM((D, 384), F32)],
            name="qkv_weights",
        )

    @step
    def send_grad_one():
        v["g1"] = send_pair(v["as"], v["bs"], 1, 2)

    @step
    def add_grad_one():
        v["ga"], v["gs"], v["gb"], v["gt"] = first_sum("add_grad_one", v["ak"], v["bk"], v["g1"])

    @step
    def send_grad_two():
        v["g2"] = send_pair(v["gs"], v["gt"], 2, 1)

    @step
    def add_grad_two():
        outs = run(
            second_add_qkv,
            [arr((192, 128))] * 4 + [arr((256, 128))],
            [v["ga"], v["g2"][0], v["gb"], v["g2"][1]],
            name="add_grad_two",
        )
        *v["qs"], v["out_part"] = over_high(outs)

    @step
    def send_grad_cols():
        v["qz"] = three(now(v["qs"][1:]))

    @step
    def join_grad():
        v["ga"], v["gb"] = run(
            join_qkv,
            [arr((576, 128)), arr((512, 128))],
            [v["qs"][0], *v["qz"], v["out_part"], v["small"]],
            name="join_grad",
        )

    @step
    def send_grad_three():
        v["g3"] = send_pair(v["ga"], v["gb"], 1, 2)

    @step
    def pair_grad():
        v["ga"], v["gb"] = join_pair("pair_grad", v["ga"], v["g3"][0], v["gb"], v["g3"][1])

    @step
    def send_grad_four():
        v["g4"] = send_pair(v["ga"], v["gb"], 2, 1)

    @step
    def join_mlp_cols():
        v["ma"], v["mb"] = run(
            join_mlp, [arr((1024, 128))] * 2, [v["ms"][0], *v["mz"]], name="join_mlp_cols"
        )

    @step
    def send_mlp_three():
        v["m3"] = send_pair(v["ma"], v["mb"], 1, 2)

    @step
    def pair_mlp():
        v["ma"], v["mb"] = join_pair("pair_mlp", v["ma"], v["m3"][0], v["mb"], v["m3"][1])

    @step
    def send_mlp_four():
        v["m4"] = send_pair(v["ma"], v["mb"], 2, 1)

    @step
    def split_first():
        v["last_own"], v["last_sums"], *v["last_parts"] = run(
            split_last,
            [arr((half, width), F32), arr((8, width), F32)] + [arr((half + 16, width))] * 3,
            [v["back"], v["got"]],
            name="split_first",
        )

    @step
    def send_first():
        v["last"] = three(now(v["last_parts"]))

    @step
    def sum_first():
        v["grad_tokens"], v["sums"] = run(
            last_sum,
            [arr((half, width), F32), arr((8, width), F32)],
            [v["last_own"], v["last_sums"], *v["last"], v["grad_middle"]],
            name="sum_first",
        )

    def send_mixed(k):
        part = now(v["mix_parts"][k - 1])
        v["mixed"] = v.get("mixed", []) + [swap(part, "col", k)]

    @step
    def send_mixed_one():
        send_mixed(1)

    @step
    def send_mixed_two():
        send_mixed(2)

    @step
    def send_mixed_three():
        send_mixed(3)

    @step
    def sum_mixed():
        v["mixed"] = run(
            mixed_sum,
            [arr((half, width))],
            [v["mid_own"], v["mix"], *v["mixed"], b_proj.reshape(1, width)],
            name="sum_mixed",
        )[0]

    @step
    def pack_small():
        v["small"] = run(
            small_pack,
            [arr((16, width), F32)],
            [v["sums"], v["out_shift"], v["cot_shift"], v["qv_shift"], v["fc_shift"]],
            name="pack_small",
        )[0]
        for k in high_bits():
            v["small"] = v["small"] + swap(v["small"], "dp", k)

    @step
    def unpack_mlp_all():
        v["fc_sum"], v["proj_sum"] = run(
            unpack_mlp,
            [arr(w_fc.shape, F32), arr(w_proj.shape, F32)],
            [v["ma"], v["m4"][0], v["mb"], v["m4"][1]],
            name="unpack_mlp_all",
        )

    @step
    def unpack_grad():
        v["qkv_sum"], v["out_sum"], *v["outs"] = run(
            unpack_qkv,
            [
                arr(w_qkv.shape, F32),
                arr(w_out.shape, F32),
                arr((2, width), F32),
                arr((2, width), F32),
                arr(b_qv.shape, F32),
                arr((1, width), F32),
                arr((1, 512), F32),
                arr((1, width), F32),
            ],
            [v["ga"], v["g4"][0], v["gb"], v["g4"][1]],
            name="unpack_grad",
        )

    for name in ORDER:
        steps[name]()
    gain, shift, qv, out_shift, fc_shift, proj_shift = v["outs"]
    return (
        v["mixed"],
        v["grad_tokens"],
        gain,
        shift,
        v["qkv_sum"],
        qv,
        v["out_sum"],
        out_shift.reshape(b_out.shape),
        v["fc_sum"],
        fc_shift.reshape(b_fc.shape),
        v["proj_sum"],
        proj_shift.reshape(b_proj.shape),
    )


def solution(mesh):
    in_specs = (
        P(("dp", "row"), "col"),
        P("dp"),
        P(None, "col"),
        P(None, "col"),
        P(None, "col", "row"),
        P(None, ("row", "col")),
        P("row", "col"),
        P("col"),
        P("col", "row"),
        P(("row", "col")),
        P("row", "col"),
        P("col"),
        P(("dp", "row"), "col"),
    )
    out_specs = (
        P(("dp", "row"), "col"),
        P(("dp", "row"), "col"),
        P(None, "col"),
        P(None, "col"),
        P(None, "col", "row"),
        P(None, ("row", "col")),
        P("row", "col"),
        P("col"),
        P("col", "row"),
        P(("row", "col")),
        P("row", "col"),
        P("col"),
    )
    return jax.shard_map(shards, mesh=mesh, in_specs=in_specs, out_specs=out_specs, check_vma=False)
```

```python
import math
import types

import jax
import jax.numpy as jnp
from jax import lax
from jax.experimental import pallas as pl
from jax.experimental.pallas import tpu as pltpu
from jax.sharding import PartitionSpec as P

D = 1024
HEAD_DIM = 64
EPS = 1e-05
NEGATIVE = -1e30
LOW = jnp.bfloat16
F32 = jnp.float32
FACTOR = 1.0 / math.sqrt(HEAD_DIM)
ROOT = math.sqrt(2.0 / math.pi)
CUBE = 0.044715
COLS = 4
PARTS = 4
OVER_ROWS = (((0,), (0,)), ((), ()))
OVER_COLS = (((1,), (1,)), ((), ()))
PLAIN = (((1,), (0,)), ((), ()))


def swap(value, axis, k):
    return lax.ppermute(value, axis, [(i, i ^ k) for i in range(lax.axis_size(axis))])


def dot(a, b, dims=PLAIN):
    return lax.dot_general(a, b, dims, preferred_element_type=F32)


def arr(shape, dtype=LOW):
    return jax.ShapeDtypeStruct(shape, dtype)


def place():
    return lax.axis_index("col"), lax.rem(lax.axis_index("dp"), PARTS)


def call(body, outs, args, hbm=(), scratch=(), room=None, us=0.001):
    whole = pl.BlockSpec(memory_space=pltpu.VMEM)
    anywhere = pl.BlockSpec(memory_space=pl.ANY)
    held = sum(math.prod(a.shape) * a.dtype.itemsize for a in list(args) + list(outs))
    held += sum(math.prod(a.shape) * 4 for a in scratch if len(a.shape) > 1)
    return pl.pallas_call(
        body,
        out_shape=list(outs),
        in_specs=[anywhere if i in hbm else whole for i in range(len(args))],
        out_specs=[whole] * len(outs),
        scratch_shapes=list(scratch),
        compiler_params=pltpu.CompilerParams(vmem_limit_bytes=room or held + 3 * 1024 * 1024),
        cost_estimate=pl.CostEstimate(
            flops=int(us * 1e9), bytes_accessed=1024, transcendentals=0
        ),
    )(*args)


def run_copies(copies, sems):
    copies = [pltpu.make_async_copy(a, b, sems.at[i]) for i, (a, b) in enumerate(copies)]
    for copy in copies:
        copy.start()
    for copy in copies:
        copy.wait()


def pack(w_qkv, w_fc, w_proj, w_out, gain, shift, b_out, f1, f2, f3, p0, full, sems):
    c, d = place()
    units = w_fc.shape[1] // COLS
    unit = units // PARTS
    quarter = w_out.shape[0] // PARTS
    piece = w_qkv.shape[1] // PARTS
    heads = w_qkv.shape[2] // COLS
    full[...] = jnp.zeros_like(full)
    copies = [(gain, full.at[0:2]), (shift, full.at[2:4]), (b_out, full.at[4:5])]
    for k, f in ((1, f1), (2, f2), (3, f3)):
        rows = pl.ds(pl.multiple_of(d * piece, piece), piece)
        cols = pl.ds(pl.multiple_of((c ^ k) * heads, heads), heads)
        for j in range(3):
            copies.append((w_qkv.at[j, rows, cols], f.at[pl.ds(j * piece, piece)]))
        start = pl.ds(pl.multiple_of((c ^ k) * units + d * unit, unit), unit)
        mine = pl.ds(pl.multiple_of(d * quarter, quarter), quarter)
        copies.append((w_fc.at[:, start], f.at[pl.ds(192, 256)]))
        for j in range(2):
            cols = pl.ds(j * 128, 128)
            copies.append((w_out.at[mine, cols], f.at[pl.ds(448 + j * 128, 128)]))
            copies.append((w_proj.at[start, cols], f.at[pl.ds(704 + j * 128, 128)]))
    run_copies(copies, sems)
    value = full[...]
    high = value.astype(LOW)
    low = (value - high.astype(F32)).astype(LOW).astype(F32)
    high = high.astype(F32)
    rows = jnp.concatenate([high[:, :128], high[:, 128:], low[:, :128], low[:, 128:]], 0)
    rows = rows.astype(LOW)
    p0[...] = rows
    for f in (f1, f2, f3):
        f[960:992, :] = rows


def split_pack(f1, f2, f3, left, right):
    for k, f in enumerate((f1, f2, f3)):
        left[k, 0:96, :] = f[0:96, :]
        right[k, 0:96, :] = f[96:192, :]
        right[k, 96:352, :] = f[192:448, :]
        left[k, 96:352, :] = f[448:704, :]
        left[k, 352:480, :] = f[704:832, :]
        right[k, 352:480, :] = f[832:960, :]


def pair_first(a, b, c, d, qa, wa, qb, wb):
    for i, ref in enumerate((a, b)):
        qa[i] = ref[:, 0:96, :]
        wa[i] = ref[:, 96:480, :]
    for i, ref in enumerate((c, d)):
        qb[i] = ref[:, 0:96, :]
        wb[i] = ref[:, 96:480, :]


def pair(a, b, c, d, left, right):
    left[0] = a[...]
    left[1] = b[...]
    right[0] = c[...]
    right[1] = d[...]


def stack(*refs):
    for i, ref in enumerate(refs[:-1]):
        refs[-1][i] = ref[...]


def norm_parts(blocks):
    total = sum(jnp.sum(b, -1, keepdims=True) for b in blocks)
    squares = sum(jnp.sum(b * b, -1, keepdims=True) for b in blocks)
    mean = total * (1.0 / D)
    factor = lax.rsqrt(squares * (1.0 / D) - mean * mean + EPS)
    return mean, factor


def head_lanes(shape):
    return lax.broadcasted_iota(jnp.int32, shape, 1) < HEAD_DIM


def attention(*refs):
    xo, xs = refs[0], refs[1]
    heads, (qa0, qa1, qb0, qb1, w, b_qv, segment) = refs[2:6], refs[6:13]
    first, x_all, wq, params, qkv, probs, attended, bias, sems = refs[13:22]
    c, d = place()
    piece = 64
    copies = []
    for j in range(3):
        copies.append(
            pltpu.make_async_copy(
                w.at[j, :, pl.ds(pl.multiple_of(c * 128, 128), 128)],
                wq.at[pl.ds(0, 256), pl.ds(j * 128, 128)],
                sems.at[j],
            )
        )
        copies[-1].start()
    for k in range(COLS):
        rows = (heads[k][...] if k == 0 else heads[k][960:992, :]).astype(F32)
        full = rows[0:16] + rows[16:32]
        params[:, k * 256 : k * 256 + 128] = full[0:8]
        params[:, k * 256 + 128 : (k + 1) * 256] = full[8:16]
    lefts = (qa0.at[0], qa0.at[1], qa1.at[0], qa1.at[1])
    rights = (qb0.at[0], qb1.at[0], qb0.at[1], qb1.at[1])
    for m in range(PARTS):
        for k in range(1, COLS):
            start = pl.multiple_of(k * 256 + (d ^ m) * piece, piece)
            both = jnp.concatenate([lefts[m][k - 1], rights[m][k - 1]], 0)
            for j in range(3):
                wq[pl.ds(start, piece), j * 128 : (j + 1) * 128] = both[
                    j * piece : (j + 1) * piece, :
                ]
    for half, srcs in enumerate((xo, xs)):

        @pl.loop(0, 8)
        def _(i):
            rows = pl.ds(pl.multiple_of(i * 32, 32), 32)
            into = pl.ds(pl.multiple_of(half * 256 + i * 32, 32), 32)
            low = [srcs[k, rows, :] for k in range(COLS)]
            blocks = [b.astype(F32) for b in low]
            mean, factor = norm_parts(blocks)
            for k in range(COLS):
                cols = slice(k * 256, (k + 1) * 256)
                out = (blocks[k] - mean) * factor * params[0:1, cols] + params[2:3, cols]
                first[into, cols] = out.astype(LOW)
                x_all[into, cols] = low[k]

    r = lax.axis_index("row")
    ids = segment[...].astype(F32)
    ids = jnp.where(r == 0, ids, jnp.concatenate([ids[:, 256:512], ids[:, 0:256]], 1))
    spot = lax.rem(lax.broadcasted_iota(jnp.int32, (1, 512), 1) + r * 256, 512).astype(F32)
    for i in range(4):
        cols = slice(i * 128, (i + 1) * 128)
        there = [
            jnp.concatenate([jnp.broadcast_to(v[:, cols], (128, 128)).T] * 4, 1)
            for v in (ids, spot)
        ]
        allowed = (there[0] == ids) & (there[1] >= spot)
        bias[cols, :] = jnp.where(allowed, 0.0, NEGATIVE)
    for copy in copies:
        copy.wait()
    added = jnp.concatenate([b_qv[0:1, :], jnp.zeros((1, 128), F32), b_qv[1:2, :]], 1)

    @pl.loop(0, 4)
    def _(i):
        rows = pl.ds(pl.multiple_of(i * 128, 128), 128)
        qkv[rows, :] = (dot(first[rows, :], wq[...]) + added).astype(LOW)

    @pl.loop(0, 4)
    def _(i):
        rows = pl.ds(pl.multiple_of(i * 128, 128), 128)
        lanes = head_lanes((128, 128))
        query = qkv[rows, 0:128]
        keys = qkv[:, 128:256]
        values = qkv[:, 256:384]
        outs = []
        for h in range(2):
            mine = jnp.where(lanes == (h == 0), query, jnp.zeros_like(query))
            score = dot(mine, keys, OVER_COLS) * FACTOR + bias[rows, :]
            expo = jnp.exp(score - jnp.max(score, -1, keepdims=True))
            weights = expo / jnp.sum(expo, -1, keepdims=True)
            probs[h, rows, :] = weights
            outs.append(dot(weights.astype(LOW), values))
        attended[rows, :] = jnp.where(lanes, outs[0], outs[1]).astype(LOW)


def by_part(a0, a1, b0, b1):
    return (
        (a0.at[0], a0.at[1], a1.at[0], a1.at[1]),
        (b0.at[0], b1.at[0], b0.at[1], b1.at[1]),
    )


def join_weights(w_out, w_fc, w_proj, a0, a1, b0, b1, out, fc, proj, sems):
    c, d = place()
    copies = [(w_out, out.at[:, pl.ds(0, 256)])]
    for m in range(PARTS):
        start = pl.ds(pl.multiple_of(c * 512 + (d ^ m) * 128, 128), 128)
        copies.append((w_fc.at[:, start], fc.at[pl.ds(0, 256), pl.ds(m * 128, 128)]))
        copies.append((w_proj.at[start], proj.at[pl.ds(m * 128, 128), pl.ds(0, 256)]))
    copies = [pltpu.make_async_copy(a, b, sems.at[i]) for i, (a, b) in enumerate(copies)]
    for copy in copies:
        copy.start()
    lefts, rights = by_part(a0, a1, b0, b1)
    for m in range(PARTS):
        rows = pl.ds(pl.multiple_of((d ^ m) * 128, 128), 128)
        mine = slice(m * 128, (m + 1) * 128)
        for k in range(1, COLS):
            one, two = slice(k * 256, k * 256 + 128), slice(k * 256 + 128, (k + 1) * 256)
            out[rows, one] = lefts[m][k - 1, 0:128, :]
            out[rows, two] = lefts[m][k - 1, 128:256, :]
            fc[k * 256 : (k + 1) * 256, mine] = rights[m][k - 1, 0:256, :]
            proj[mine, one] = lefts[m][k - 1, 256:384, :]
            proj[mine, two] = rights[m][k - 1, 256:384, :]
    for copy in copies:
        copy.wait()


def forward(*refs):
    mine, theirs = refs[0:2]
    w_own, w_sib, x_all, params, fc, b_fc = refs[2:8]
    att_own, middle, second, hidden, mid_own, att_sib, shift = refs[8:15]
    c, d = place()
    for m in range(PARTS):
        here = pl.ds(pl.multiple_of((d ^ m) * 128, 128), 128)
        shift[0:1, m * 128 : (m + 1) * 128] = b_fc[0:1, here]
    for k in range(COLS):
        cols = pl.ds(pl.multiple_of((c ^ k) * 128, 128), 128)
        att_own[:, cols] = mine[k]
        att_sib[0:256, cols] = theirs[k, 256:512, :]
        att_sib[256:512, cols] = theirs[k, 0:256, :]

    @pl.loop(0, 4)
    def _(i):
        rows = pl.ds(pl.multiple_of(i * 128, 128), 128)
        value = dot(att_own[rows, :], w_own[...]) + dot(att_sib[rows, :], w_sib[...])
        value = value + x_all[rows, :].astype(F32) + params[4:5, :]
        middle[rows, :] = value
        mean, factor = norm_parts([value])
        out = (value - mean) * factor * params[1:2, :] + params[3:4, :]
        second[rows, :] = out.astype(LOW)
        hidden[rows, :] = dot(second[rows, :], fc[...]) + shift[0:1, :]

    mid_own[...] = middle[0:256, 0:256]


def backward(*refs):
    co, cs = refs[0:2]
    middle, hidden, fc, proj, params = refs[2:7]
    cot, active, grad_hidden, back, send, sums, fc_shift, cot_shift, shift = refs[7:16]
    for k in range(COLS):
        cols = slice(k * 256, (k + 1) * 256)
        cot[0:256, cols] = co[k]
        cot[256:512, cols] = cs[k]
    sums[...] = jnp.zeros_like(sums)
    shift[...] = jnp.zeros_like(shift)
    cot_shift[...] = jnp.sum(cot[:, 0:256].astype(F32), 0, keepdims=True)

    def step(start):
        rows = pl.ds(pl.multiple_of(start, 128), 128)
        v = hidden[rows, :]
        t = jnp.tanh(ROOT * (v + CUBE * (v * v * v)))
        active[rows, :] = (0.5 * v * (1.0 + t)).astype(LOW)
        slope = 0.5 * (1.0 + t) + 0.5 * v * (1.0 - t * t) * (ROOT * (1.0 + 3.0 * CUBE * (v * v)))
        low = (dot(cot[rows, :], proj[...], OVER_COLS) * slope).astype(LOW)
        grad_hidden[rows, :] = low
        shift[0:1, :] += jnp.sum(low.astype(F32), 0, keepdims=True)
        grad = dot(low, fc[...], OVER_COLS)
        mean, factor = norm_parts([middle[rows, :]])
        normed = (middle[rows, :] - mean) * factor
        sums[0:1, :] += jnp.sum(grad * normed, 0, keepdims=True)
        sums[1:2, :] += jnp.sum(grad, 0, keepdims=True)
        scaled = grad * params[1:2, :]
        one = jnp.mean(scaled, -1, keepdims=True)
        two = jnp.mean(scaled * normed, -1, keepdims=True)
        return factor * (scaled - one - normed * two)

    @pl.loop(0, 2)
    def _(i):
        send[pl.ds(pl.multiple_of(i * 128, 128), 128), :] = step(256 + i * 128).astype(LOW)

    @pl.loop(0, 2)
    def _(i):
        back[pl.ds(pl.multiple_of(i * 128, 128), 128), :] = step(i * 128)

    c, d = place()
    for m in range(PARTS):
        here = pl.ds(pl.multiple_of((d ^ m) * 128, 128), 128)
        fc_shift[0:1, here] = shift[0:1, m * 128 : (m + 1) * 128]


def mlp_grads(second, grad_hidden, active, cot, proj, fk, fs, pk, ps, mine, left, right):
    for k in range(COLS):
        cols = slice(k * 256, (k + 1) * 256)
        value = dot(second[:, cols], grad_hidden[...], OVER_ROWS).astype(LOW)
        for m in range(PARTS):
            (fs if m % 2 else fk)[m // 2, cols, :] = value[:, m * 128 : (m + 1) * 128]
    for m in range(PARTS):
        value = dot(active[:, m * 128 : (m + 1) * 128], cot[...], OVER_ROWS).astype(LOW)
        for i in range(2 * COLS):
            rows = slice(i * 128, (i + 1) * 128)
            (ps if m // 2 else pk)[m % 2, rows, :] = value[:, rows]
    mine[...] = dot(active[0:256, :], proj[...])
    theirs = dot(active[256:512, :], proj[...]).astype(LOW)
    left[...] = theirs[:, 0:512]
    right[...] = theirs[:, 512:1024]


def first_add(ka, ra, kb, rb, ha, sa, hb, sb):
    for keep, got, have, send in ((ka, ra, ha, sa), (kb, rb, hb, sb)):
        have[...] = keep[0].astype(F32) + got[0].astype(F32)
        send[...] = (keep[1].astype(F32) + got[1].astype(F32)).astype(LOW)


def second_add_mlp(ha, ra, hb, rb, *outs):
    for k, out in enumerate(outs):
        rows = slice(k * 256, (k + 1) * 256)
        out[0:256, :] = (ha[rows, :] + ra[rows, :].astype(F32)).astype(LOW)
        out[256:512, :] = (hb[rows, :] + rb[rows, :].astype(F32)).astype(LOW)


def second_add_qkv(ha, ra, hb, rb, *outs):
    for k, out in enumerate(outs[:-1]):
        have, got = (ha, ra) if k < 2 else (hb, rb)
        rows = slice((k % 2) * 192, (k % 2) * 192 + 192)
        out[...] = (have[rows, :] + got[rows, :].astype(F32)).astype(LOW)
    for j, (have, got) in enumerate(((ha, ra), (hb, rb))):
        value = have[384:512, :] + got[384:512, :].astype(F32)
        outs[-1][j * 128 : (j + 1) * 128, :] = value.astype(LOW)


def split_sum(back, got, o0, o1, o2, o3):
    for k, out in enumerate((o0, o1, o2, o3)):
        cols = slice(k * 256, (k + 1) * 256)
        out[...] = (back[:, cols] + got[:, cols].astype(F32)).astype(out.dtype)


def middle_sum(cot, o0, g1, g2, g3, out, low):
    value = cot[...].astype(F32) + (
        o0[...] + g1[...].astype(F32) + g2[...].astype(F32) + g3[...].astype(F32)
    )
    out[...] = value
    low[...] = value.astype(LOW)


def mixed_sum(middle, o0, g1, g2, g3, b_proj, out):
    value = o0[...] + g1[...].astype(F32) + g2[...].astype(F32) + g3[...].astype(F32)
    out[...] = (middle[...] + value + b_proj[...]).astype(LOW)


def grad_out(own, other, w_out, o0, o1, o2, o3):
    c, d = place()
    for k, out in enumerate((o0, o1, o2, o3)):
        rows = pl.ds(pl.multiple_of((c ^ k) * 128, 128), 128)
        w = w_out[rows, :]
        out[0:256, :] = dot(own[...], w, OVER_COLS).astype(out.dtype)
        out[256:512, :] = dot(other[...], w, OVER_COLS).astype(out.dtype)


def out_weight(att, own, other, mix, left, right, out, shift, o0, o1, o2, o3):
    for k, part in enumerate((o0, o1, o2, o3)):
        cols = slice((k % 2) * 256, (k % 2 + 1) * 256)
        total = mix[:, k * 256 : (k + 1) * 256] + (left, right)[k // 2][:, cols].astype(F32)
        part[...] = total.astype(part.dtype)
    out[...] = (
        dot(att[0:256, :], own[...], OVER_ROWS) + dot(att[256:512, :], other[...], OVER_ROWS)
    ).astype(LOW)
    shift[...] = jnp.sum(own[...].astype(F32), 0, keepdims=True) + jnp.sum(
        other[...].astype(F32), 0, keepdims=True
    )


def sum_datt(o0, g1, g2, g3, out):
    value = o0[...] + g1[...].astype(F32) + g2[...].astype(F32) + g3[...].astype(F32)
    out[...] = value.astype(LOW)


def attention_back(*refs):
    datt, qkv, probs, wq, x_all, params, sums2 = refs[0:7]
    dqkv, back, send, qv_shift = refs[7:11]
    scores, lows, sums = refs[11:14]

    @pl.loop(0, 4)
    def _(i):
        rows = pl.ds(pl.multiple_of(i * 128, 128), 128)
        lanes = head_lanes((128, 128))
        keys = qkv[:, 128:256]
        values = qkv[:, 256:384]
        grad = datt[rows, :]
        outs = []
        for h in range(2):
            mine = jnp.where(lanes == (h == 0), grad, jnp.zeros_like(grad))
            gp = dot(mine, values, OVER_COLS)
            weights = probs[h, rows, :]
            centre = jnp.sum(weights * gp, -1, keepdims=True)
            score = (weights * (gp - centre)).astype(LOW)
            scores[h, rows, :] = score
            lows[h, rows, :] = weights.astype(LOW)
            outs.append(dot(score, keys))
        dqkv[rows, 0:128] = (jnp.where(lanes, outs[0], outs[1]) * FACTOR).astype(LOW)

    lanes = head_lanes((512, 128))
    gk = [dot(scores[h], qkv[:, 0:128], OVER_ROWS) for h in range(2)]
    dqkv[:, 128:256] = (jnp.where(lanes, gk[0], gk[1]) * FACTOR).astype(LOW)
    gv = [dot(lows[h], datt[...], OVER_ROWS) for h in range(2)]
    dqkv[:, 256:384] = jnp.where(lanes, gv[0], gv[1]).astype(LOW)
    qv_shift[...] = jnp.sum(dqkv[...].astype(F32), 0, keepdims=True)
    sums[...] = jnp.zeros_like(sums)

    def step(start):
        rows = pl.ds(pl.multiple_of(start, 128), 128)
        grad = dot(dqkv[rows, :], wq[...], OVER_COLS)
        x = x_all[rows, :].astype(F32)
        mean, factor = norm_parts([x])
        normed = (x - mean) * factor
        sums[0:1, :] += jnp.sum(grad * normed, 0, keepdims=True)
        sums[1:2, :] += jnp.sum(grad, 0, keepdims=True)
        scaled = grad * params[0:1, :]
        one = jnp.mean(scaled, -1, keepdims=True)
        two = jnp.mean(scaled * normed, -1, keepdims=True)
        return factor * (scaled - one - normed * two)

    @pl.loop(0, 2)
    def _(i):
        send[pl.ds(pl.multiple_of(i * 128, 128), 128), :] = step(256 + i * 128).astype(LOW)

    @pl.loop(0, 2)
    def _(i):
        back[pl.ds(pl.multiple_of(i * 128, 128), 128), :] = step(i * 128)

    rows = jnp.concatenate(
        [sums[0:1, :], sums2[0:1, :], sums[1:2, :], sums2[1:2, :], jnp.zeros((4, D), F32)], 0
    )
    back[256:264, :] = rows
    high = rows.astype(LOW).astype(F32)
    send[256:272, :] = jnp.concatenate([high, rows - high], 0).astype(LOW)


def split_last(back, got, o0, s0, o1, o2, o3):
    more = got[256:272, :].astype(F32)
    sums = back[256:264, :] + more[0:8] + more[8:16]
    high = sums.astype(LOW).astype(F32)
    both = jnp.concatenate([high, sums - high], 0).astype(LOW)
    o0[...] = back[0:256, 0:256] + got[0:256, 0:256].astype(F32)
    s0[...] = sums[:, 0:256]
    for k, out in ((1, o1), (2, o2), (3, o3)):
        cols = slice(k * 256, (k + 1) * 256)
        out[0:256, :] = (back[0:256, cols] + got[0:256, cols].astype(F32)).astype(LOW)
        out[256:272, :] = both[:, cols]


def last_sum(o0, s0, g1, g2, g3, middle, out, sums):
    out[...] = middle[...] + (
        o0[...]
        + g1[0:256, :].astype(F32)
        + g2[0:256, :].astype(F32)
        + g3[0:256, :].astype(F32)
    )
    value = s0[...]
    for g in (g1, g2, g3):
        more = g[256:272, :].astype(F32)
        value = value + more[0:8] + more[8:16]
    sums[...] = value


def qkv_weight(first, dqkv, w_out, ak, as_, bk, bs, full):
    c, d = place()

    @pl.loop(0, 4)
    def _(k):
        cols = pl.ds(pl.multiple_of(k * 256, 256), 256)
        full[cols, :] = dot(first[:, cols], dqkv[...], OVER_ROWS)

    for m in range(PARTS):
        outs = ((as_ if m % 2 else ak, m // 2), (bs if m // 2 else bk, m % 2))
        rows = pl.ds(pl.multiple_of((d ^ m) * 128, 128), 128)
        for j, (out, index) in enumerate(outs):
            out[index, 384:512, :] = w_out[rows, j * 128 : (j + 1) * 128]
        for k in range(COLS):
            out, index = outs[k // 2]
            start = pl.ds(pl.multiple_of(k * 256 + (d ^ m) * 64, 64), 64)
            for j in range(3):
                row = (k % 2) * 192 + j * 64
                out[index, row : row + 64, :] = full[start, j * 128 : (j + 1) * 128].astype(LOW)


def unpack_qkv(a0, a1, b0, b1, out, w_out, gain, shift, b_qv, b_out, b_fc, b_proj):
    c, d = place()
    lefts, rights = by_part(a0, a1, b0, b1)
    for m in range(PARTS):
        rows = pl.ds(pl.multiple_of((d ^ m) * 64, 64), 64)
        for k in range(COLS):
            src = (lefts if k < 2 else rights)[m]
            cols = pl.ds(pl.multiple_of((c ^ k) * 128, 128), 128)
            for j in range(3):
                start = (k % 2) * 192 + j * 64
                out[j, rows, cols] = src[start : start + 64, :].astype(F32)
        rows = pl.ds(pl.multiple_of((d ^ m) * 128, 128), 128)
        w_out[rows, 0:128] = lefts[m][384:512, :].astype(F32)
        w_out[rows, 128:256] = rights[m][384:512, :].astype(F32)
    total = sum(left[512:576, :].astype(F32) for left in lefts)
    total = total[0:32] + total[32:64]
    for j, rows in enumerate((total[0:16], total[16:32])):
        cols = slice(j * 128, (j + 1) * 128)
        gain[:, cols] = rows[0:2]
        shift[:, cols] = rows[2:4]
        b_out[:, cols] = rows[4:5]
        b_proj[:, cols] = rows[5:6]
        b_qv[j : j + 1, :] = rows[6:7]
        b_fc[0:1, j * 128 : (j + 1) * 128] = rows[7:8]
        b_fc[0:1, 256 + j * 128 : 256 + (j + 1) * 128] = rows[8:9]


def unpack_mlp(a0, a1, b0, b1, fc, proj):
    c, d = place()
    lefts, rights = by_part(a0, a1, b0, b1)
    for m in range(PARTS):
        for k in range(COLS):
            here = pl.ds(pl.multiple_of((c ^ k) * 512 + (d ^ m) * 128, 128), 128)
            fc[:, here] = lefts[m][k * 256 : (k + 1) * 256, :].astype(F32)
            for j in range(2):
                row = k * 256 + j * 128
                cols = slice(j * 128, (j + 1) * 128)
                proj[here, cols] = rights[m][row : row + 128, :].astype(F32)


def join_mlp(m0, m1, m2, m3, left, right):
    for k, part in enumerate((m0, m1, m2, m3)):
        rows = slice(k * 256, (k + 1) * 256)
        left[rows, :] = part[0:256, :]
        right[rows, :] = part[256:512, :]


def join_qkv(q0, q1, q2, q3, w_out, small, left, right):
    for j, (out, one, two) in enumerate(((left, q0, q1), (right, q2, q3))):
        out[0:192, :] = one[...]
        out[192:384, :] = two[...]
        out[384:512, :] = w_out[j * 128 : (j + 1) * 128, :]
    full = small[...]
    high = full.astype(LOW).astype(F32)
    low = full - high
    rows = [high[:, 0:128], high[:, 128:256], low[:, 0:128], low[:, 128:256]]
    left[512:576, :] = jnp.concatenate(rows, 0).astype(LOW)


def small_pack(sums, out_shift, cot_shift, qv, fc_shift, out):
    out[0:4, :] = sums[0:4, :]
    out[4:5, :] = out_shift[...]
    out[5:6, :] = cot_shift[...]
    out[6:7, 0:128] = qv[0:1, 0:128]
    out[6:7, 128:256] = qv[0:1, 256:384]
    out[7:8, :] = fc_shift[0:1, 0:256]
    out[8:9, :] = fc_shift[0:1, 256:512]
    out[9:16, :] = jnp.zeros((7, 256), F32)


def after(value, *others):
    return lax.optimization_barrier((value, others))[0]


def high_bits():
    return [1 << b for b in range(2, int(math.log2(lax.axis_size("dp"))))]


def over_high(parts):
    for k in high_bits():
        parts = [(o.astype(F32) + swap(o, "dp", k).astype(F32)).astype(LOW) for o in parts]
    return parts


def three(parts, axis="col"):
    return [swap(part, axis, k + 1) for k, part in enumerate(parts)]


def pair_arrays(left, right):
    return [arr((2,) + left.shape), arr((2,) + right.shape)]


def shards(
    tokens,
    segment,
    ln_gain,
    ln_bias,
    w_qkv,
    b_qv,
    w_out,
    b_out,
    w_fc,
    b_fc,
    w_proj,
    b_proj,
    cotangent,
):
    half, width = tokens.shape
    group = 2 * half
    dma = pltpu.SemaphoreType.DMA
    last = []
    v = types.SimpleNamespace(mixed=[])

    def run(body, outs, args, **keys):
        results = call(body, outs, after(list(args), last), **keys)
        last[:] = results[:1]
        return results

    def now(value):
        return after(value, last)

    def send_pair(left, right, one, two):
        left, right = now([left, right])
        return swap(left, "dp", one), swap(right, "dp", two)

    def join_pair(left, one, right, two):
        return run(pair, pair_arrays(left, right), [left, one, right, two])

    def first_sum(ka, kb, got):
        rows = ka.shape[1]
        outs = [arr((rows, 128), F32), arr((rows, 128))] * 2
        return run(first_add, outs, [ka, got[0], kb, got[1]])

    def split(back, got):
        outs = [arr((half, width), F32)] + [arr((half, width))] * 3
        return run(split_sum, outs, [back, got])

    def pack_all():
        *v.sent, v.head = run(
            pack,
            [arr((992, 128))] * 3 + [arr((32, 128))],
            [w_qkv, w_fc, w_proj, w_out, ln_gain, ln_bias, b_out.reshape(1, width)],
            hbm=range(7),
            scratch=[pltpu.VMEM((8, width), F32), dma((27,))],
            room=56 * 1024 * 1024,
        )

    def send_weights():
        v.f = three(now(v.sent))

    def split_weights():
        v.wa, v.wb = run(split_pack, [arr((3, 480, 128))] * 2, v.f)

    def send_tokens():
        v.x = three([now(tokens)] * 3)

    def send_weights_first():
        v.w1 = send_pair(v.wa, v.wb, 1, 2)

    def pair_weights_first():
        v.qa, v.wa, v.qb, v.wb = run(
            pair_first,
            [arr((2, 3, 96, 128)), arr((2, 3, 384, 128))] * 2,
            [v.wa, v.w1[0], v.wb, v.w1[1]],
        )

    def send_qkv_two():
        v.q2 = send_pair(v.qa, v.qb, 2, 1)

    def stack_tokens():
        outs = [arr((4, half, width))]
        v.x_own = run(stack, outs, [tokens, *v.x], us=50.0)[0]

    def swap_tokens():
        v.x_sib = swap(now(v.x_own), "row", 1)

    def send_cotangent():
        v.cot = three([now(cotangent)] * 3)

    def attend():
        (
            v.first,
            v.x_all,
            v.wq,
            v.params,
            v.qkv,
            v.probs,
            v.attended,
        ) = run(
            attention,
            [
                arr((group, D)),
                arr((group, D)),
                arr((D, 384)),
                arr((8, D), F32),
                arr((group, 384)),
                arr((2, group, group), F32),
                arr((group, 128)),
            ],
            [
                v.x_own,
                v.x_sib,
                v.head,
                *v.f,
                v.qa,
                v.q2[0],
                v.qb,
                v.q2[1],
                w_qkv,
                b_qv,
                segment.reshape(1, group),
            ],
            hbm=(10,),
            scratch=[pltpu.VMEM((group, group), F32), dma((3,))],
            us=50.0,
        )

    def send_weights_two():
        v.w2 = send_pair(v.wa, v.wb, 2, 1)

    def stack_cotangent():
        outs = [arr((4, half, width))]
        v.cot_own = run(stack, outs, [cotangent, *v.cot])[0]

    def swap_cotangent():
        v.cot_sib = swap(now(v.cot_own), "row", 1)

    def send_attended():
        v.att = three([now(v.attended)] * 3)

    def stack_attended():
        outs = [arr((4, group, 128))]
        v.att_four = run(stack, outs, [v.attended, *v.att])[0]

    def swap_attended():
        v.att_sib = swap(now(v.att_four), "row", 1)

    def join_all():
        v.w_own, v.fc, v.proj = run(
            join_weights,
            [arr((512, D)), arr((D, 512)), arr((512, D))],
            [w_out, w_fc, w_proj, v.wa, v.w2[0], v.wb, v.w2[1]],
            hbm=(0, 1, 2),
            scratch=[dma((9,))],
        )

    def swap_w_out():
        v.w_sib = swap(now(v.w_own), "row", 1)

    def feed_forward():
        v.att_own, v.middle, v.second, v.hidden, v.mid_own = run(
            forward,
            [
                arr((group, 512)),
                arr((group, D), F32),
                arr((group, D)),
                arr((group, 512), F32),
                arr((half, width), F32),
            ],
            [
                v.att_four,
                v.att_sib,
                v.w_own,
                v.w_sib,
                v.x_all,
                v.params,
                v.fc,
                b_fc.reshape(1, 512),
            ],
            scratch=[pltpu.VMEM((group, 512), LOW), pltpu.VMEM((8, 512), F32)],
        )

    def feed_back():
        (
            v.cot_all,
            v.active,
            v.grad_hidden,
            v.back,
            v.send,
            v.sums2,
            v.fc_shift,
            v.cot_shift,
        ) = run(
            backward,
            [
                arr((group, D)),
                arr((group, 512)),
                arr((group, 512)),
                arr((half, D), F32),
                arr((half, D)),
                arr((2, D), F32),
                arr((1, 512), F32),
                arr((1, width), F32),
            ],
            [v.cot_own, v.cot_sib, v.middle, v.hidden, v.fc, v.proj, v.params],
            scratch=[pltpu.VMEM((8, 512), F32)],
        )

    def swap_second():
        v.got = swap(now(v.send), "row", 1)

    def mlp_weights():
        v.fk, v.fs, v.pk, v.ps, v.mix, *v.mix_send = run(
            mlp_grads,
            [arr((2, 1024, 128))] * 4 + [arr((half, D), F32)] + [arr((half, D // 2))] * 2,
            [v.second, v.grad_hidden, v.active, v.cot_all, v.proj],
        )

    def send_mlp_one():
        v.m1 = send_pair(v.fs, v.ps, 1, 2)

    def split_second():
        v.own, *v.parts = split(v.back, v.got)

    def send_second():
        v.mid = three(now(v.parts))

    def sum_second():
        v.grad_middle, v.branch = run(
            middle_sum,
            [arr((half, width), F32), arr((half, width))],
            [cotangent, v.own, *v.mid],
        )

    def swap_branch():
        v.other = swap(now(v.branch), "row", 1)

    def swap_mixed():
        v.mix_got = [swap(part, "row", 1) for part in now(v.mix_send)]

    def back_out():
        v.att_sum, *v.att_parts = run(
            grad_out,
            [arr((group, 128), F32)] + [arr((group, 128))] * 3,
            [v.branch, v.other, w_out],
        )

    def send_back_out():
        v.datt = three(now(v.att_parts))

    def weigh_out():
        v.out_grad, v.out_shift, v.mix, *v.mix_parts = run(
            out_weight,
            [arr(w_out.shape), arr((1, width), F32), arr((half, width), F32)]
            + [arr((half, width))] * 3,
            [v.att_own, v.branch, v.other, v.mix, *v.mix_got],
        )

    def add_mlp_one():
        v.ha, v.sa, v.hb, v.sb = first_sum(v.fk, v.pk, v.m1)

    def send_mlp_two():
        v.m2 = send_pair(v.sa, v.sb, 2, 1)

    def sum_attended():
        v.att_sum = run(
            sum_datt, [arr((group, 128))], [v.att_sum, *v.datt], us=2.0
        )[0]

    def add_mlp_two():
        ms = run(
            second_add_mlp,
            [arr((512, 128))] * 4,
            [v.ha, v.m2[0], v.hb, v.m2[1]],
        )
        v.ms = over_high(ms)

    def send_mlp_cols():
        v.mz = three(now(v.ms[1:]))

    def attend_back():
        v.dqkv, v.back, v.send, v.qv_shift = run(
            attention_back,
            [
                arr((group, 384)),
                arr((half + 8, D), F32),
                arr((half + 16, D)),
                arr((1, 384), F32),
            ],
            [v.att_sum, v.qkv, v.probs, v.wq, v.x_all, v.params, v.sums2],
            scratch=[
                pltpu.VMEM((2, group, group), LOW),
                pltpu.VMEM((2, group, group), LOW),
                pltpu.VMEM((8, D), F32),
            ],
            us=50.0,
        )

    def swap_first():
        v.got = swap(now(v.send), "row", 1)

    def qkv_weights():
        v.ak, v.as_, v.bk, v.bs = run(
            qkv_weight,
            [arr((2, 512, 128))] * 4,
            [v.first, v.dqkv, v.out_grad],
            scratch=[pltpu.VMEM((D, 384), F32)],
        )

    def send_grad_one():
        v.g1 = send_pair(v.as_, v.bs, 1, 2)

    def add_grad_one():
        v.ga, v.gs, v.gb, v.gt = first_sum(v.ak, v.bk, v.g1)

    def send_grad_two():
        v.g2 = send_pair(v.gs, v.gt, 2, 1)

    def add_grad_two():
        outs = run(
            second_add_qkv,
            [arr((192, 128))] * 4 + [arr((256, 128))],
            [v.ga, v.g2[0], v.gb, v.g2[1]],
        )
        *v.qs, v.out_part = over_high(outs)

    def send_grad_cols():
        v.qz = three(now(v.qs[1:]))

    def join_grad():
        v.ga, v.gb = run(
            join_qkv,
            [arr((576, 128)), arr((512, 128))],
            [v.qs[0], *v.qz, v.out_part, v.small],
        )

    def send_grad_three():
        v.g3 = send_pair(v.ga, v.gb, 1, 2)

    def pair_grad():
        v.ga, v.gb = join_pair(v.ga, v.g3[0], v.gb, v.g3[1])

    def send_grad_four():
        v.g4 = send_pair(v.ga, v.gb, 2, 1)

    def join_mlp_cols():
        v.ma, v.mb = run(
            join_mlp, [arr((1024, 128))] * 2, [v.ms[0], *v.mz], us=50.0
        )

    def send_mlp_three():
        v.m3 = send_pair(v.ma, v.mb, 1, 2)

    def pair_mlp():
        v.ma, v.mb = join_pair(v.ma, v.m3[0], v.mb, v.m3[1])

    def send_mlp_four():
        v.m4 = send_pair(v.ma, v.mb, 2, 1)

    def split_first():
        v.last_own, v.last_sums, *v.last_parts = run(
            split_last,
            [arr((half, width), F32), arr((8, width), F32)] + [arr((half + 16, width))] * 3,
            [v.back, v.got],
        )

    def send_first():
        v.last = three(now(v.last_parts))

    def sum_first():
        v.grad_tokens, v.sums = run(
            last_sum,
            [arr((half, width), F32), arr((8, width), F32)],
            [v.last_own, v.last_sums, *v.last, v.grad_middle],
            us=50.0,
        )

    def send_mixed(k):
        part = now(v.mix_parts[k - 1])
        v.mixed = v.mixed + [swap(part, "col", k)]

    def send_mixed_one():
        send_mixed(1)

    def send_mixed_two():
        send_mixed(2)

    def send_mixed_three():
        send_mixed(3)

    def sum_mixed():
        v.mixed_out = run(
            mixed_sum,
            [arr((half, width))],
            [v.mid_own, v.mix, *v.mixed, b_proj.reshape(1, width)],
        )[0]

    def pack_small():
        v.small = run(
            small_pack,
            [arr((16, width), F32)],
            [v.sums, v.out_shift, v.cot_shift, v.qv_shift, v.fc_shift],
        )[0]
        for k in high_bits():
            v.small = v.small + swap(v.small, "dp", k)

    def unpack_mlp_all():
        v.fc_sum, v.proj_sum = run(
            unpack_mlp,
            [arr(w_fc.shape, F32), arr(w_proj.shape, F32)],
            [v.ma, v.m4[0], v.mb, v.m4[1]],
        )

    def unpack_grad():
        v.qkv_sum, v.out_sum, *v.outs = run(
            unpack_qkv,
            [
                arr(w_qkv.shape, F32),
                arr(w_out.shape, F32),
                arr((2, width), F32),
                arr((2, width), F32),
                arr(b_qv.shape, F32),
                arr((1, width), F32),
                arr((1, 512), F32),
                arr((1, width), F32),
            ],
            [v.ga, v.g4[0], v.gb, v.g4[1]],
        )

    order = (
        pack_all,
        send_weights,
        split_weights,
        send_tokens,
        send_weights_first,
        pair_weights_first,
        send_qkv_two,
        stack_tokens,
        swap_tokens,
        send_cotangent,
        send_weights_two,
        attend,
        stack_cotangent,
        send_attended,
        swap_cotangent,
        stack_attended,
        swap_attended,
        join_all,
        swap_w_out,
        feed_forward,
        feed_back,
        swap_second,
        mlp_weights,
        send_mlp_one,
        split_second,
        send_second,
        sum_second,
        swap_branch,
        swap_mixed,
        back_out,
        send_back_out,
        weigh_out,
        add_mlp_one,
        send_mlp_two,
        sum_attended,
        add_mlp_two,
        send_mlp_cols,
        attend_back,
        swap_first,
        qkv_weights,
        send_grad_one,
        join_mlp_cols,
        split_first,
        send_first,
        add_grad_one,
        send_grad_two,
        add_grad_two,
        send_mlp_three,
        sum_first,
        send_grad_cols,
        pack_small,
        pair_mlp,
        send_mlp_four,
        join_grad,
        send_grad_three,
        send_mixed_two,
        unpack_mlp_all,
        send_mixed_three,
        send_mixed_one,
        pair_grad,
        send_grad_four,
        unpack_grad,
        sum_mixed,
    )
    for step in order:
        step()
    gain, shift, qv, out_shift, fc_shift, proj_shift = v.outs
    return (
        v.mixed_out,
        v.grad_tokens,
        gain,
        shift,
        v.qkv_sum,
        qv,
        v.out_sum,
        out_shift.reshape(b_out.shape),
        v.fc_sum,
        fc_shift.reshape(b_fc.shape),
        v.proj_sum,
        proj_shift.reshape(b_proj.shape),
    )


def solution(mesh):
    in_specs = (
        P(("dp", "row"), "col"),
        P("dp"),
        P(None, "col"),
        P(None, "col"),
        P(None, "col", "row"),
        P(None, ("row", "col")),
        P("row", "col"),
        P("col"),
        P("col", "row"),
        P(("row", "col")),
        P("row", "col"),
        P("col"),
        P(("dp", "row"), "col"),
    )
    out_specs = (
        P(("dp", "row"), "col"),
        P(("dp", "row"), "col"),
        P(None, "col"),
        P(None, "col"),
        P(None, "col", "row"),
        P(None, ("row", "col")),
        P("row", "col"),
        P("col"),
        P("col", "row"),
        P(("row", "col")),
        P("row", "col"),
        P("col"),
    )
    return jax.shard_map(shards, mesh=mesh, in_specs=in_specs, out_specs=out_specs, check_vma=False)
```

```python
import math
import types

import jax
import jax.numpy as jnp
from jax import lax
from jax.experimental import pallas as pl
from jax.experimental.pallas import tpu as pltpu
from jax.sharding import PartitionSpec as P

D = 1024
HEAD_DIM = 64
EPS = 1e-05
NEGATIVE = -1e30
LOW = jnp.bfloat16
F32 = jnp.float32
FACTOR = 1.0 / math.sqrt(HEAD_DIM)
ROOT = math.sqrt(2.0 / math.pi)
CUBE = 0.044715
COLS = 4
PARTS = 4
OVER_ROWS = (((0,), (0,)), ((), ()))
OVER_COLS = (((1,), (1,)), ((), ()))
PLAIN = (((1,), (0,)), ((), ()))


def swap(value, axis, k):
    return lax.ppermute(value, axis, [(i, i ^ k) for i in range(lax.axis_size(axis))])


def dot(a, b, dims=PLAIN):
    return lax.dot_general(a, b, dims, preferred_element_type=F32)


def arr(shape, dtype=LOW):
    return jax.ShapeDtypeStruct(shape, dtype)


def place():
    return lax.axis_index("col"), lax.rem(lax.axis_index("dp"), PARTS)


def call(body, outs, args, hbm=(), scratch=(), room=None, us=0.001):
    whole = pl.BlockSpec(memory_space=pltpu.VMEM)
    anywhere = pl.BlockSpec(memory_space=pl.ANY)
    held = sum(math.prod(a.shape) * a.dtype.itemsize for a in list(args) + list(outs))
    held += sum(math.prod(a.shape) * 4 for a in scratch if len(a.shape) > 1)
    return pl.pallas_call(
        body,
        out_shape=list(outs),
        in_specs=[anywhere if i in hbm else whole for i in range(len(args))],
        out_specs=[whole] * len(outs),
        scratch_shapes=list(scratch),
        compiler_params=pltpu.CompilerParams(vmem_limit_bytes=room or held + 3 * 1024 * 1024),
        cost_estimate=pl.CostEstimate(
            flops=int(us * 1e9), bytes_accessed=1024, transcendentals=0
        ),
    )(*args)


def run_copies(copies, sems):
    copies = [pltpu.make_async_copy(a, b, sems.at[i]) for i, (a, b) in enumerate(copies)]
    for copy in copies:
        copy.start()
    for copy in copies:
        copy.wait()


def pack(w_qkv, w_fc, w_proj, w_out, gain, shift, b_out, f1, f2, f3, p0, full, sems):
    c, d = place()
    units = w_fc.shape[1] // COLS
    unit = units // PARTS
    quarter = w_out.shape[0] // PARTS
    piece = w_qkv.shape[1] // PARTS
    heads = w_qkv.shape[2] // COLS
    full[...] = jnp.zeros_like(full)
    copies = [(gain, full.at[0:2]), (shift, full.at[2:4]), (b_out, full.at[4:5])]
    for k, f in ((1, f1), (2, f2), (3, f3)):
        rows = pl.ds(pl.multiple_of(d * piece, piece), piece)
        cols = pl.ds(pl.multiple_of((c ^ k) * heads, heads), heads)
        for j in range(3):
            copies.append((w_qkv.at[j, rows, cols], f.at[pl.ds(j * piece, piece)]))
        start = pl.ds(pl.multiple_of((c ^ k) * units + d * unit, unit), unit)
        mine = pl.ds(pl.multiple_of(d * quarter, quarter), quarter)
        copies.append((w_fc.at[:, start], f.at[pl.ds(192, 256)]))
        for j in range(2):
            cols = pl.ds(j * 128, 128)
            copies.append((w_out.at[mine, cols], f.at[pl.ds(448 + j * 128, 128)]))
            copies.append((w_proj.at[start, cols], f.at[pl.ds(704 + j * 128, 128)]))
    run_copies(copies, sems)
    value = full[...]
    high = value.astype(LOW)
    low = (value - high.astype(F32)).astype(LOW).astype(F32)
    high = high.astype(F32)
    rows = jnp.concatenate([high[:, :128], high[:, 128:], low[:, :128], low[:, 128:]], 0)
    rows = rows.astype(LOW)
    p0[...] = rows
    for f in (f1, f2, f3):
        f[960:992, :] = rows


def split_pack(f1, f2, f3, left, right):
    for k, f in enumerate((f1, f2, f3)):
        left[k, 0:96, :] = f[0:96, :]
        right[k, 0:96, :] = f[96:192, :]
        right[k, 96:352, :] = f[192:448, :]
        left[k, 96:352, :] = f[448:704, :]
        left[k, 352:480, :] = f[704:832, :]
        right[k, 352:480, :] = f[832:960, :]


def pair_first(a, b, c, d, qa, wa, qb, wb):
    for i, ref in enumerate((a, b)):
        qa[i] = ref[:, 0:96, :]
        wa[i] = ref[:, 96:480, :]
    for i, ref in enumerate((c, d)):
        qb[i] = ref[:, 0:96, :]
        wb[i] = ref[:, 96:480, :]


def pair(a, b, c, d, left, right):
    left[0] = a[...]
    left[1] = b[...]
    right[0] = c[...]
    right[1] = d[...]


def stack(*refs):
    for i, ref in enumerate(refs[:-1]):
        refs[-1][i] = ref[...]


def norm_parts(blocks):
    total = sum(jnp.sum(b, -1, keepdims=True) for b in blocks)
    squares = sum(jnp.sum(b * b, -1, keepdims=True) for b in blocks)
    mean = total * (1.0 / D)
    factor = lax.rsqrt(squares * (1.0 / D) - mean * mean + EPS)
    return mean, factor


def head_lanes(shape):
    return lax.broadcasted_iota(jnp.int32, shape, 1) < HEAD_DIM


def attention(*refs):
    xo, xs = refs[0], refs[1]
    heads, (qa0, qa1, qb0, qb1, w, b_qv, segment) = refs[2:6], refs[6:13]
    first, x_all, wq, params, qkv, probs, attended, bias, sems = refs[13:22]
    c, d = place()
    piece = 64
    copies = []
    for j in range(3):
        copies.append(
            pltpu.make_async_copy(
                w.at[j, :, pl.ds(pl.multiple_of(c * 128, 128), 128)],
                wq.at[pl.ds(0, 256), pl.ds(j * 128, 128)],
                sems.at[j],
            )
        )
        copies[-1].start()
    for k in range(COLS):
        rows = (heads[k][...] if k == 0 else heads[k][960:992, :]).astype(F32)
        full = rows[0:16] + rows[16:32]
        params[:, k * 256 : k * 256 + 128] = full[0:8]
        params[:, k * 256 + 128 : (k + 1) * 256] = full[8:16]
    lefts = (qa0.at[0], qa0.at[1], qa1.at[0], qa1.at[1])
    rights = (qb0.at[0], qb1.at[0], qb0.at[1], qb1.at[1])
    for m in range(PARTS):
        for k in range(1, COLS):
            start = pl.multiple_of(k * 256 + (d ^ m) * piece, piece)
            both = jnp.concatenate([lefts[m][k - 1], rights[m][k - 1]], 0)
            for j in range(3):
                wq[pl.ds(start, piece), j * 128 : (j + 1) * 128] = both[
                    j * piece : (j + 1) * piece, :
                ]
    for half, srcs in enumerate((xo, xs)):

        @pl.loop(0, 8)
        def _(i):
            rows = pl.ds(pl.multiple_of(i * 32, 32), 32)
            into = pl.ds(pl.multiple_of(half * 256 + i * 32, 32), 32)
            low = [srcs[k, rows, :] for k in range(COLS)]
            blocks = [b.astype(F32) for b in low]
            mean, factor = norm_parts(blocks)
            for k in range(COLS):
                cols = slice(k * 256, (k + 1) * 256)
                out = (blocks[k] - mean) * factor * params[0:1, cols] + params[2:3, cols]
                first[into, cols] = out.astype(LOW)
                x_all[into, cols] = low[k]

    r = lax.axis_index("row")
    ids = segment[...].astype(F32)
    ids = jnp.where(r == 0, ids, jnp.concatenate([ids[:, 256:512], ids[:, 0:256]], 1))
    spot = lax.rem(lax.broadcasted_iota(jnp.int32, (1, 512), 1) + r * 256, 512).astype(F32)
    for i in range(4):
        cols = slice(i * 128, (i + 1) * 128)
        there = [
            jnp.concatenate([jnp.broadcast_to(v[:, cols], (128, 128)).T] * 4, 1)
            for v in (ids, spot)
        ]
        allowed = (there[0] == ids) & (there[1] >= spot)
        bias[cols, :] = jnp.where(allowed, 0.0, NEGATIVE)
    for copy in copies:
        copy.wait()
    added = jnp.concatenate([b_qv[0:1, :], jnp.zeros((1, 128), F32), b_qv[1:2, :]], 1)

    @pl.loop(0, 4)
    def _(i):
        rows = pl.ds(pl.multiple_of(i * 128, 128), 128)
        qkv[rows, :] = (dot(first[rows, :], wq[...]) + added).astype(LOW)

    @pl.loop(0, 4)
    def _(i):
        rows = pl.ds(pl.multiple_of(i * 128, 128), 128)
        lanes = head_lanes((128, 128))
        query = qkv[rows, 0:128]
        keys = qkv[:, 128:256]
        values = qkv[:, 256:384]
        outs = []
        for h in range(2):
            mine = jnp.where(lanes == (h == 0), query, jnp.zeros_like(query))
            score = dot(mine, keys, OVER_COLS) * FACTOR + bias[rows, :]
            expo = jnp.exp(score - jnp.max(score, -1, keepdims=True))
            weights = expo / jnp.sum(expo, -1, keepdims=True)
            probs[h, rows, :] = weights
            outs.append(dot(weights.astype(LOW), values))
        attended[rows, :] = jnp.where(lanes, outs[0], outs[1]).astype(LOW)


def by_part(a0, a1, b0, b1):
    return (
        (a0.at[0], a0.at[1], a1.at[0], a1.at[1]),
        (b0.at[0], b1.at[0], b0.at[1], b1.at[1]),
    )


def join_weights(w_out, w_fc, w_proj, a0, a1, b0, b1, out, fc, proj, sems):
    c, d = place()
    copies = [(w_out, out.at[:, pl.ds(0, 256)])]
    for m in range(PARTS):
        start = pl.ds(pl.multiple_of(c * 512 + (d ^ m) * 128, 128), 128)
        copies.append((w_fc.at[:, start], fc.at[pl.ds(0, 256), pl.ds(m * 128, 128)]))
        copies.append((w_proj.at[start], proj.at[pl.ds(m * 128, 128), pl.ds(0, 256)]))
    copies = [pltpu.make_async_copy(a, b, sems.at[i]) for i, (a, b) in enumerate(copies)]
    for copy in copies:
        copy.start()
    lefts, rights = by_part(a0, a1, b0, b1)
    for m in range(PARTS):
        rows = pl.ds(pl.multiple_of((d ^ m) * 128, 128), 128)
        mine = slice(m * 128, (m + 1) * 128)
        for k in range(1, COLS):
            one, two = slice(k * 256, k * 256 + 128), slice(k * 256 + 128, (k + 1) * 256)
            out[rows, one] = lefts[m][k - 1, 0:128, :]
            out[rows, two] = lefts[m][k - 1, 128:256, :]
            fc[k * 256 : (k + 1) * 256, mine] = rights[m][k - 1, 0:256, :]
            proj[mine, one] = lefts[m][k - 1, 256:384, :]
            proj[mine, two] = rights[m][k - 1, 256:384, :]
    for copy in copies:
        copy.wait()


def forward(*refs):
    mine, theirs = refs[0:2]
    w_own, w_sib, x_all, params, fc, b_fc = refs[2:8]
    att_own, middle, second, hidden, mid_own, att_sib, shift = refs[8:15]
    c, d = place()
    for m in range(PARTS):
        here = pl.ds(pl.multiple_of((d ^ m) * 128, 128), 128)
        shift[0:1, m * 128 : (m + 1) * 128] = b_fc[0:1, here]
    for k in range(COLS):
        cols = pl.ds(pl.multiple_of((c ^ k) * 128, 128), 128)
        att_own[:, cols] = mine[k]
        att_sib[0:256, cols] = theirs[k, 256:512, :]
        att_sib[256:512, cols] = theirs[k, 0:256, :]

    @pl.loop(0, 4)
    def _(i):
        rows = pl.ds(pl.multiple_of(i * 128, 128), 128)
        value = dot(att_own[rows, :], w_own[...]) + dot(att_sib[rows, :], w_sib[...])
        value = value + x_all[rows, :].astype(F32) + params[4:5, :]
        middle[rows, :] = value
        mean, factor = norm_parts([value])
        out = (value - mean) * factor * params[1:2, :] + params[3:4, :]
        second[rows, :] = out.astype(LOW)
        hidden[rows, :] = dot(second[rows, :], fc[...]) + shift[0:1, :]

    mid_own[...] = middle[0:256, 0:256]


def backward(*refs):
    co, cs = refs[0:2]
    middle, hidden, fc, proj, params = refs[2:7]
    cot, active, grad_hidden, back, send, sums, fc_shift, cot_shift, shift = refs[7:16]
    for k in range(COLS):
        cols = slice(k * 256, (k + 1) * 256)
        cot[0:256, cols] = co[k]
        cot[256:512, cols] = cs[k]
    sums[...] = jnp.zeros_like(sums)
    shift[...] = jnp.zeros_like(shift)
    cot_shift[...] = jnp.sum(cot[:, 0:256].astype(F32), 0, keepdims=True)

    def step(start):
        rows = pl.ds(pl.multiple_of(start, 128), 128)
        v = hidden[rows, :]
        t = jnp.tanh(ROOT * (v + CUBE * (v * v * v)))
        active[rows, :] = (0.5 * v * (1.0 + t)).astype(LOW)
        slope = 0.5 * (1.0 + t) + 0.5 * v * (1.0 - t * t) * (ROOT * (1.0 + 3.0 * CUBE * (v * v)))
        low = (dot(cot[rows, :], proj[...], OVER_COLS) * slope).astype(LOW)
        grad_hidden[rows, :] = low
        shift[0:1, :] += jnp.sum(low.astype(F32), 0, keepdims=True)
        grad = dot(low, fc[...], OVER_COLS)
        mean, factor = norm_parts([middle[rows, :]])
        normed = (middle[rows, :] - mean) * factor
        sums[0:1, :] += jnp.sum(grad * normed, 0, keepdims=True)
        sums[1:2, :] += jnp.sum(grad, 0, keepdims=True)
        scaled = grad * params[1:2, :]
        one = jnp.mean(scaled, -1, keepdims=True)
        two = jnp.mean(scaled * normed, -1, keepdims=True)
        return factor * (scaled - one - normed * two)

    @pl.loop(0, 2)
    def _(i):
        send[pl.ds(pl.multiple_of(i * 128, 128), 128), :] = step(256 + i * 128).astype(LOW)

    @pl.loop(0, 2)
    def _(i):
        back[pl.ds(pl.multiple_of(i * 128, 128), 128), :] = step(i * 128)

    c, d = place()
    for m in range(PARTS):
        here = pl.ds(pl.multiple_of((d ^ m) * 128, 128), 128)
        fc_shift[0:1, here] = shift[0:1, m * 128 : (m + 1) * 128]


def mlp_grads(second, grad_hidden, active, cot, proj, fk, fs, pk, ps, mine, left, right):
    for k in range(COLS):
        cols = slice(k * 256, (k + 1) * 256)
        value = dot(second[:, cols], grad_hidden[...], OVER_ROWS).astype(LOW)
        for m in range(PARTS):
            (fs if m % 2 else fk)[m // 2, cols, :] = value[:, m * 128 : (m + 1) * 128]
    for m in range(PARTS):
        value = dot(active[:, m * 128 : (m + 1) * 128], cot[...], OVER_ROWS).astype(LOW)
        for i in range(2 * COLS):
            rows = slice(i * 128, (i + 1) * 128)
            (ps if m // 2 else pk)[m % 2, rows, :] = value[:, rows]
    mine[...] = dot(active[0:256, :], proj[...])
    theirs = dot(active[256:512, :], proj[...]).astype(LOW)
    left[...] = theirs[:, 0:512]
    right[...] = theirs[:, 512:1024]


def first_add(ka, ra, kb, rb, ha, sa, hb, sb):
    for keep, got, have, send in ((ka, ra, ha, sa), (kb, rb, hb, sb)):
        have[...] = keep[0].astype(F32) + got[0].astype(F32)
        send[...] = (keep[1].astype(F32) + got[1].astype(F32)).astype(LOW)


def second_add_mlp(ha, ra, hb, rb, *outs):
    for k, out in enumerate(outs):
        rows = slice(k * 256, (k + 1) * 256)
        out[0:256, :] = (ha[rows, :] + ra[rows, :].astype(F32)).astype(LOW)
        out[256:512, :] = (hb[rows, :] + rb[rows, :].astype(F32)).astype(LOW)


def second_add_qkv(ha, ra, hb, rb, *outs):
    for k, out in enumerate(outs[:-1]):
        have, got = (ha, ra) if k < 2 else (hb, rb)
        rows = slice((k % 2) * 192, (k % 2) * 192 + 192)
        out[...] = (have[rows, :] + got[rows, :].astype(F32)).astype(LOW)
    for j, (have, got) in enumerate(((ha, ra), (hb, rb))):
        value = have[384:512, :] + got[384:512, :].astype(F32)
        outs[-1][j * 128 : (j + 1) * 128, :] = value.astype(LOW)


def split_sum(back, got, o0, o1, o2, o3):
    for k, out in enumerate((o0, o1, o2, o3)):
        cols = slice(k * 256, (k + 1) * 256)
        out[...] = (back[:, cols] + got[:, cols].astype(F32)).astype(out.dtype)


def middle_sum(cot, o0, g1, g2, g3, out, low):
    value = cot[...].astype(F32) + (
        o0[...] + g1[...].astype(F32) + g2[...].astype(F32) + g3[...].astype(F32)
    )
    out[...] = value
    low[...] = value.astype(LOW)


def mixed_sum(middle, o0, g1, g2, g3, b_proj, out):
    value = o0[...] + g1[...].astype(F32) + g2[...].astype(F32) + g3[...].astype(F32)
    out[...] = (middle[...] + value + b_proj[...]).astype(LOW)


def grad_out(own, other, w_out, o0, o1, o2, o3):
    c, d = place()
    for k, out in enumerate((o0, o1, o2, o3)):
        rows = pl.ds(pl.multiple_of((c ^ k) * 128, 128), 128)
        w = w_out[rows, :]
        out[0:256, :] = dot(own[...], w, OVER_COLS).astype(out.dtype)
        out[256:512, :] = dot(other[...], w, OVER_COLS).astype(out.dtype)


def out_weight(att, own, other, mix, left, right, out, shift, o0, o1, o2, o3):
    for k, part in enumerate((o0, o1, o2, o3)):
        cols = slice((k % 2) * 256, (k % 2 + 1) * 256)
        total = mix[:, k * 256 : (k + 1) * 256] + (left, right)[k // 2][:, cols].astype(F32)
        part[...] = total.astype(part.dtype)
    out[...] = (
        dot(att[0:256, :], own[...], OVER_ROWS) + dot(att[256:512, :], other[...], OVER_ROWS)
    ).astype(LOW)
    shift[...] = jnp.sum(own[...].astype(F32), 0, keepdims=True) + jnp.sum(
        other[...].astype(F32), 0, keepdims=True
    )


def sum_datt(o0, g1, g2, g3, out):
    value = o0[...] + g1[...].astype(F32) + g2[...].astype(F32) + g3[...].astype(F32)
    out[...] = value.astype(LOW)


def attention_back(*refs):
    datt, qkv, probs, wq, x_all, params, sums2 = refs[0:7]
    dqkv, back, send, qv_shift = refs[7:11]
    scores, lows, sums = refs[11:14]

    @pl.loop(0, 4)
    def _(i):
        rows = pl.ds(pl.multiple_of(i * 128, 128), 128)
        lanes = head_lanes((128, 128))
        keys = qkv[:, 128:256]
        values = qkv[:, 256:384]
        grad = datt[rows, :]
        outs = []
        for h in range(2):
            mine = jnp.where(lanes == (h == 0), grad, jnp.zeros_like(grad))
            gp = dot(mine, values, OVER_COLS)
            weights = probs[h, rows, :]
            centre = jnp.sum(weights * gp, -1, keepdims=True)
            score = (weights * (gp - centre)).astype(LOW)
            scores[h, rows, :] = score
            lows[h, rows, :] = weights.astype(LOW)
            outs.append(dot(score, keys))
        dqkv[rows, 0:128] = (jnp.where(lanes, outs[0], outs[1]) * FACTOR).astype(LOW)

    lanes = head_lanes((512, 128))
    gk = [dot(scores[h], qkv[:, 0:128], OVER_ROWS) for h in range(2)]
    dqkv[:, 128:256] = (jnp.where(lanes, gk[0], gk[1]) * FACTOR).astype(LOW)
    gv = [dot(lows[h], datt[...], OVER_ROWS) for h in range(2)]
    dqkv[:, 256:384] = jnp.where(lanes, gv[0], gv[1]).astype(LOW)
    qv_shift[...] = jnp.sum(dqkv[...].astype(F32), 0, keepdims=True)
    sums[...] = jnp.zeros_like(sums)

    def step(start):
        rows = pl.ds(pl.multiple_of(start, 128), 128)
        grad = dot(dqkv[rows, :], wq[...], OVER_COLS)
        x = x_all[rows, :].astype(F32)
        mean, factor = norm_parts([x])
        normed = (x - mean) * factor
        sums[0:1, :] += jnp.sum(grad * normed, 0, keepdims=True)
        sums[1:2, :] += jnp.sum(grad, 0, keepdims=True)
        scaled = grad * params[0:1, :]
        one = jnp.mean(scaled, -1, keepdims=True)
        two = jnp.mean(scaled * normed, -1, keepdims=True)
        return factor * (scaled - one - normed * two)

    @pl.loop(0, 2)
    def _(i):
        send[pl.ds(pl.multiple_of(i * 128, 128), 128), :] = step(256 + i * 128).astype(LOW)

    @pl.loop(0, 2)
    def _(i):
        back[pl.ds(pl.multiple_of(i * 128, 128), 128), :] = step(i * 128)

    rows = jnp.concatenate(
        [sums[0:1, :], sums2[0:1, :], sums[1:2, :], sums2[1:2, :], jnp.zeros((4, D), F32)], 0
    )
    back[256:264, :] = rows
    high = rows.astype(LOW).astype(F32)
    send[256:272, :] = jnp.concatenate([high, rows - high], 0).astype(LOW)


def split_last(back, got, o0, s0, o1, o2, o3):
    more = got[256:272, :].astype(F32)
    sums = back[256:264, :] + more[0:8] + more[8:16]
    high = sums.astype(LOW).astype(F32)
    both = jnp.concatenate([high, sums - high], 0).astype(LOW)
    o0[...] = back[0:256, 0:256] + got[0:256, 0:256].astype(F32)
    s0[...] = sums[:, 0:256]
    for k, out in ((1, o1), (2, o2), (3, o3)):
        cols = slice(k * 256, (k + 1) * 256)
        out[0:256, :] = (back[0:256, cols] + got[0:256, cols].astype(F32)).astype(LOW)
        out[256:272, :] = both[:, cols]


def last_sum(o0, s0, g1, g2, g3, middle, out, sums):
    out[...] = middle[...] + (
        o0[...]
        + g1[0:256, :].astype(F32)
        + g2[0:256, :].astype(F32)
        + g3[0:256, :].astype(F32)
    )
    value = s0[...]
    for g in (g1, g2, g3):
        more = g[256:272, :].astype(F32)
        value = value + more[0:8] + more[8:16]
    sums[...] = value


def qkv_weight(first, dqkv, w_out, ak, as_, bk, bs, full):
    c, d = place()

    @pl.loop(0, 4)
    def _(k):
        cols = pl.ds(pl.multiple_of(k * 256, 256), 256)
        full[cols, :] = dot(first[:, cols], dqkv[...], OVER_ROWS)

    for m in range(PARTS):
        outs = ((as_ if m % 2 else ak, m // 2), (bs if m // 2 else bk, m % 2))
        rows = pl.ds(pl.multiple_of((d ^ m) * 128, 128), 128)
        for j, (out, index) in enumerate(outs):
            out[index, 384:512, :] = w_out[rows, j * 128 : (j + 1) * 128]
        for k in range(COLS):
            out, index = outs[k // 2]
            start = pl.ds(pl.multiple_of(k * 256 + (d ^ m) * 64, 64), 64)
            for j in range(3):
                row = (k % 2) * 192 + j * 64
                out[index, row : row + 64, :] = full[start, j * 128 : (j + 1) * 128].astype(LOW)


def unpack_qkv(a0, a1, b0, b1, out, w_out, gain, shift, b_qv, b_out, b_fc, b_proj):
    c, d = place()
    lefts, rights = by_part(a0, a1, b0, b1)
    for m in range(PARTS):
        rows = pl.ds(pl.multiple_of((d ^ m) * 64, 64), 64)
        for k in range(COLS):
            src = (lefts if k < 2 else rights)[m]
            cols = pl.ds(pl.multiple_of((c ^ k) * 128, 128), 128)
            for j in range(3):
                start = (k % 2) * 192 + j * 64
                out[j, rows, cols] = src[start : start + 64, :].astype(F32)
        rows = pl.ds(pl.multiple_of((d ^ m) * 128, 128), 128)
        w_out[rows, 0:128] = lefts[m][384:512, :].astype(F32)
        w_out[rows, 128:256] = rights[m][384:512, :].astype(F32)
    total = sum(left[512:576, :].astype(F32) for left in lefts)
    total = total[0:32] + total[32:64]
    for j, rows in enumerate((total[0:16], total[16:32])):
        cols = slice(j * 128, (j + 1) * 128)
        gain[:, cols] = rows[0:2]
        shift[:, cols] = rows[2:4]
        b_out[:, cols] = rows[4:5]
        b_proj[:, cols] = rows[5:6]
        b_qv[j : j + 1, :] = rows[6:7]
        b_fc[0:1, j * 128 : (j + 1) * 128] = rows[7:8]
        b_fc[0:1, 256 + j * 128 : 256 + (j + 1) * 128] = rows[8:9]


def unpack_mlp(a0, a1, b0, b1, fc, proj):
    c, d = place()
    lefts, rights = by_part(a0, a1, b0, b1)
    for m in range(PARTS):
        for k in range(COLS):
            here = pl.ds(pl.multiple_of((c ^ k) * 512 + (d ^ m) * 128, 128), 128)
            fc[:, here] = lefts[m][k * 256 : (k + 1) * 256, :].astype(F32)
            for j in range(2):
                row = k * 256 + j * 128
                cols = slice(j * 128, (j + 1) * 128)
                proj[here, cols] = rights[m][row : row + 128, :].astype(F32)


def join_mlp(m0, m1, m2, m3, left, right):
    for k, part in enumerate((m0, m1, m2, m3)):
        rows = slice(k * 256, (k + 1) * 256)
        left[rows, :] = part[0:256, :]
        right[rows, :] = part[256:512, :]


def join_qkv(q0, q1, q2, q3, w_out, small, left, right):
    for j, (out, one, two) in enumerate(((left, q0, q1), (right, q2, q3))):
        out[0:192, :] = one[...]
        out[192:384, :] = two[...]
        out[384:512, :] = w_out[j * 128 : (j + 1) * 128, :]
    full = small[...]
    high = full.astype(LOW).astype(F32)
    low = full - high
    rows = [high[:, 0:128], high[:, 128:256], low[:, 0:128], low[:, 128:256]]
    left[512:576, :] = jnp.concatenate(rows, 0).astype(LOW)


def small_pack(sums, out_shift, cot_shift, qv, fc_shift, out):
    out[0:4, :] = sums[0:4, :]
    out[4:5, :] = out_shift[...]
    out[5:6, :] = cot_shift[...]
    out[6:7, 0:128] = qv[0:1, 0:128]
    out[6:7, 128:256] = qv[0:1, 256:384]
    out[7:8, :] = fc_shift[0:1, 0:256]
    out[8:9, :] = fc_shift[0:1, 256:512]
    out[9:16, :] = jnp.zeros((7, 256), F32)


def after(value, *others):
    return lax.optimization_barrier((value, others))[0]


def high_bits():
    return [1 << b for b in range(2, int(math.log2(lax.axis_size("dp"))))]


def over_high(parts):
    for k in high_bits():
        parts = [(o.astype(F32) + swap(o, "dp", k).astype(F32)).astype(LOW) for o in parts]
    return parts


def three(parts, axis="col"):
    return [swap(part, axis, k + 1) for k, part in enumerate(parts)]


def pair_arrays(left, right):
    return [arr((2,) + left.shape), arr((2,) + right.shape)]


def shards(
    tokens,
    segment,
    ln_gain,
    ln_bias,
    w_qkv,
    b_qv,
    w_out,
    b_out,
    w_fc,
    b_fc,
    w_proj,
    b_proj,
    cotangent,
):
    half, width = tokens.shape
    group = 2 * half
    dma = pltpu.SemaphoreType.DMA
    last = []
    v = types.SimpleNamespace(mixed=[])

    def run(body, outs, args, **keys):
        results = call(body, outs, after(list(args), last), **keys)
        last[:] = results[:1]
        return results

    def now(value):
        return after(value, last)

    def send_pair(left, right, one, two):
        left, right = now([left, right])
        return swap(left, "dp", one), swap(right, "dp", two)

    def join_pair(left, one, right, two):
        return run(pair, pair_arrays(left, right), [left, one, right, two])

    def first_sum(ka, kb, got):
        rows = ka.shape[1]
        outs = [arr((rows, 128), F32), arr((rows, 128))] * 2
        return run(first_add, outs, [ka, got[0], kb, got[1]])

    def split(back, got):
        outs = [arr((half, width), F32)] + [arr((half, width))] * 3
        return run(split_sum, outs, [back, got])

    def pack_all():
        *v.sent, v.head = run(
            pack,
            [arr((992, 128))] * 3 + [arr((32, 128))],
            [w_qkv, w_fc, w_proj, w_out, ln_gain, ln_bias, b_out.reshape(1, width)],
            hbm=range(7),
            scratch=[pltpu.VMEM((8, width), F32), dma((27,))],
            room=56 * 1024 * 1024,
        )

    def send_weights():
        v.f = three(now(v.sent))

    def split_weights():
        v.wa, v.wb = run(split_pack, [arr((3, 480, 128))] * 2, v.f)

    def send_tokens():
        v.x = three([now(tokens)] * 3)

    def send_weights_first():
        v.w1 = send_pair(v.wa, v.wb, 1, 2)

    def pair_weights_first():
        v.qa, v.wa, v.qb, v.wb = run(
            pair_first,
            [arr((2, 3, 96, 128)), arr((2, 3, 384, 128))] * 2,
            [v.wa, v.w1[0], v.wb, v.w1[1]],
        )

    def send_qkv_two():
        v.q2 = send_pair(v.qa, v.qb, 2, 1)

    def stack_tokens():
        outs = [arr((4, half, width))]
        v.x_own = run(stack, outs, [tokens, *v.x], us=50.0)[0]

    def swap_tokens():
        v.x_sib = swap(now(v.x_own), "row", 1)

    def send_cotangent():
        v.cot = three([now(cotangent)] * 3)

    def attend():
        (
            v.first,
            v.x_all,
            v.wq,
            v.params,
            v.qkv,
            v.probs,
            v.attended,
        ) = run(
            attention,
            [
                arr((group, D)),
                arr((group, D)),
                arr((D, 384)),
                arr((8, D), F32),
                arr((group, 384)),
                arr((2, group, group), F32),
                arr((group, 128)),
            ],
            [
                v.x_own,
                v.x_sib,
                v.head,
                *v.f,
                v.qa,
                v.q2[0],
                v.qb,
                v.q2[1],
                w_qkv,
                b_qv,
                segment.reshape(1, group),
            ],
            hbm=(10,),
            scratch=[pltpu.VMEM((group, group), F32), dma((3,))],
            us=50.0,
        )

    def send_weights_two():
        v.w2 = send_pair(v.wa, v.wb, 2, 1)

    def stack_cotangent():
        outs = [arr((4, half, width))]
        v.cot_own = run(stack, outs, [cotangent, *v.cot])[0]

    def swap_cotangent():
        v.cot_sib = swap(now(v.cot_own), "row", 1)

    def send_attended():
        v.att = three([now(v.attended)] * 3)

    def stack_attended():
        outs = [arr((4, group, 128))]
        v.att_four = run(stack, outs, [v.attended, *v.att])[0]

    def swap_attended():
        v.att_sib = swap(now(v.att_four), "row", 1)

    def join_all():
        v.w_own, v.fc, v.proj = run(
            join_weights,
            [arr((512, D)), arr((D, 512)), arr((512, D))],
            [w_out, w_fc, w_proj, v.wa, v.w2[0], v.wb, v.w2[1]],
            hbm=(0, 1, 2),
            scratch=[dma((9,))],
        )

    def swap_w_out():
        v.w_sib = swap(now(v.w_own), "row", 1)

    def feed_forward():
        v.att_own, v.middle, v.second, v.hidden, v.mid_own = run(
            forward,
            [
                arr((group, 512)),
                arr((group, D), F32),
                arr((group, D)),
                arr((group, 512), F32),
                arr((half, width), F32),
            ],
            [
                v.att_four,
                v.att_sib,
                v.w_own,
                v.w_sib,
                v.x_all,
                v.params,
                v.fc,
                b_fc.reshape(1, 512),
            ],
            scratch=[pltpu.VMEM((group, 512), LOW), pltpu.VMEM((8, 512), F32)],
        )

    def feed_back():
        (
            v.cot_all,
            v.active,
            v.grad_hidden,
            v.back,
            v.send,
            v.sums2,
            v.fc_shift,
            v.cot_shift,
        ) = run(
            backward,
            [
                arr((group, D)),
                arr((group, 512)),
                arr((group, 512)),
                arr((half, D), F32),
                arr((half, D)),
                arr((2, D), F32),
                arr((1, 512), F32),
                arr((1, width), F32),
            ],
            [v.cot_own, v.cot_sib, v.middle, v.hidden, v.fc, v.proj, v.params],
            scratch=[pltpu.VMEM((8, 512), F32)],
        )

    def swap_second():
        v.got = swap(now(v.send), "row", 1)

    def mlp_weights():
        v.fk, v.fs, v.pk, v.ps, v.mix, *v.mix_send = run(
            mlp_grads,
            [arr((2, 1024, 128))] * 4 + [arr((half, D), F32)] + [arr((half, D // 2))] * 2,
            [v.second, v.grad_hidden, v.active, v.cot_all, v.proj],
        )

    def send_mlp_one():
        v.m1 = send_pair(v.fs, v.ps, 1, 2)

    def split_second():
        v.own, *v.parts = split(v.back, v.got)

    def send_second():
        v.mid = three(now(v.parts))

    def sum_second():
        v.grad_middle, v.branch = run(
            middle_sum,
            [arr((half, width), F32), arr((half, width))],
            [cotangent, v.own, *v.mid],
            us=2.0,
        )

    def swap_branch():
        v.other = swap(now(v.branch), "row", 1)

    def swap_mixed():
        v.mix_got = [swap(part, "row", 1) for part in now(v.mix_send)]

    def back_out():
        v.att_sum, *v.att_parts = run(
            grad_out,
            [arr((group, 128), F32)] + [arr((group, 128))] * 3,
            [v.branch, v.other, w_out],
        )

    def send_back_out():
        v.datt = three(now(v.att_parts))

    def weigh_out():
        v.out_grad, v.out_shift, v.mix, *v.mix_parts = run(
            out_weight,
            [arr(w_out.shape), arr((1, width), F32), arr((half, width), F32)]
            + [arr((half, width))] * 3,
            [v.att_own, v.branch, v.other, v.mix, *v.mix_got],
        )

    def add_mlp_one():
        v.ha, v.sa, v.hb, v.sb = first_sum(v.fk, v.pk, v.m1)

    def send_mlp_two():
        v.m2 = send_pair(v.sa, v.sb, 2, 1)

    def sum_attended():
        v.att_sum = run(
            sum_datt, [arr((group, 128))], [v.att_sum, *v.datt], us=2.0
        )[0]

    def add_mlp_two():
        ms = run(
            second_add_mlp,
            [arr((512, 128))] * 4,
            [v.ha, v.m2[0], v.hb, v.m2[1]],
        )
        v.ms = over_high(ms)

    def send_mlp_cols():
        v.mz = three(now(v.ms[1:]))

    def attend_back():
        v.dqkv, v.back, v.send, v.qv_shift = run(
            attention_back,
            [
                arr((group, 384)),
                arr((half + 8, D), F32),
                arr((half + 16, D)),
                arr((1, 384), F32),
            ],
            [v.att_sum, v.qkv, v.probs, v.wq, v.x_all, v.params, v.sums2],
            scratch=[
                pltpu.VMEM((2, group, group), LOW),
                pltpu.VMEM((2, group, group), LOW),
                pltpu.VMEM((8, D), F32),
            ],
            us=50.0,
        )

    def swap_first():
        v.got = swap(now(v.send), "row", 1)

    def qkv_weights():
        v.ak, v.as_, v.bk, v.bs = run(
            qkv_weight,
            [arr((2, 512, 128))] * 4,
            [v.first, v.dqkv, v.out_grad],
            scratch=[pltpu.VMEM((D, 384), F32)],
        )

    def send_grad_one():
        v.g1 = send_pair(v.as_, v.bs, 1, 2)

    def add_grad_one():
        v.ga, v.gs, v.gb, v.gt = first_sum(v.ak, v.bk, v.g1)

    def send_grad_two():
        v.g2 = send_pair(v.gs, v.gt, 2, 1)

    def add_grad_two():
        outs = run(
            second_add_qkv,
            [arr((192, 128))] * 4 + [arr((256, 128))],
            [v.ga, v.g2[0], v.gb, v.g2[1]],
        )
        *v.qs, v.out_part = over_high(outs)

    def send_grad_cols():
        v.qz = three(now(v.qs[1:]))

    def join_grad():
        v.ga, v.gb = run(
            join_qkv,
            [arr((576, 128)), arr((512, 128))],
            [v.qs[0], *v.qz, v.out_part, v.small],
        )

    def send_grad_three():
        v.g3 = send_pair(v.ga, v.gb, 1, 2)

    def pair_grad():
        v.ga, v.gb = join_pair(v.ga, v.g3[0], v.gb, v.g3[1])

    def send_grad_four():
        v.g4 = send_pair(v.ga, v.gb, 2, 1)

    def join_mlp_cols():
        v.ma, v.mb = run(
            join_mlp, [arr((1024, 128))] * 2, [v.ms[0], *v.mz], us=50.0
        )

    def send_mlp_three():
        v.m3 = send_pair(v.ma, v.mb, 1, 2)

    def pair_mlp():
        v.ma, v.mb = join_pair(v.ma, v.m3[0], v.mb, v.m3[1])

    def send_mlp_four():
        v.m4 = send_pair(v.ma, v.mb, 2, 1)

    def split_first():
        v.last_own, v.last_sums, *v.last_parts = run(
            split_last,
            [arr((half, width), F32), arr((8, width), F32)] + [arr((half + 16, width))] * 3,
            [v.back, v.got],
        )

    def send_first():
        v.last = three(now(v.last_parts))

    def sum_first():
        v.grad_tokens, v.sums = run(
            last_sum,
            [arr((half, width), F32), arr((8, width), F32)],
            [v.last_own, v.last_sums, *v.last, v.grad_middle],
            us=50.0,
        )

    def send_mixed(k):
        part = now(v.mix_parts[k - 1])
        v.mixed = v.mixed + [swap(part, "col", k)]

    def send_mixed_one():
        send_mixed(1)

    def send_mixed_two():
        send_mixed(2)

    def send_mixed_three():
        send_mixed(3)

    def sum_mixed():
        v.mixed_out = run(
            mixed_sum,
            [arr((half, width))],
            [v.mid_own, v.mix, *v.mixed, b_proj.reshape(1, width)],
        )[0]

    def pack_small():
        v.small = run(
            small_pack,
            [arr((16, width), F32)],
            [v.sums, v.out_shift, v.cot_shift, v.qv_shift, v.fc_shift],
        )[0]
        for k in high_bits():
            v.small = v.small + swap(v.small, "dp", k)

    def unpack_mlp_all():
        v.fc_sum, v.proj_sum = run(
            unpack_mlp,
            [arr(w_fc.shape, F32), arr(w_proj.shape, F32)],
            [v.ma, v.m4[0], v.mb, v.m4[1]],
        )

    def unpack_grad():
        v.qkv_sum, v.out_sum, *v.outs = run(
            unpack_qkv,
            [
                arr(w_qkv.shape, F32),
                arr(w_out.shape, F32),
                arr((2, width), F32),
                arr((2, width), F32),
                arr(b_qv.shape, F32),
                arr((1, width), F32),
                arr((1, 512), F32),
                arr((1, width), F32),
            ],
            [v.ga, v.g4[0], v.gb, v.g4[1]],
        )

    order = (
        pack_all,
        send_weights,
        split_weights,
        send_tokens,
        send_weights_first,
        pair_weights_first,
        send_qkv_two,
        stack_tokens,
        swap_tokens,
        send_cotangent,
        send_weights_two,
        attend,
        stack_cotangent,
        send_attended,
        swap_cotangent,
        stack_attended,
        swap_attended,
        join_all,
        swap_w_out,
        feed_forward,
        feed_back,
        swap_second,
        mlp_weights,
        send_mlp_one,
        split_second,
        send_second,
        sum_second,
        swap_branch,
        swap_mixed,
        back_out,
        send_back_out,
        weigh_out,
        add_mlp_one,
        send_mlp_two,
        sum_attended,
        add_mlp_two,
        send_mlp_cols,
        attend_back,
        swap_first,
        qkv_weights,
        send_grad_one,
        join_mlp_cols,
        split_first,
        send_first,
        add_grad_one,
        send_grad_two,
        add_grad_two,
        send_mlp_three,
        sum_first,
        send_grad_cols,
        pack_small,
        pair_mlp,
        send_mlp_four,
        join_grad,
        send_grad_three,
        send_mixed_two,
        unpack_mlp_all,
        send_mixed_three,
        send_mixed_one,
        pair_grad,
        send_grad_four,
        unpack_grad,
        sum_mixed,
    )
    for step in order:
        step()
    gain, shift, qv, out_shift, fc_shift, proj_shift = v.outs
    return (
        v.mixed_out,
        v.grad_tokens,
        gain,
        shift,
        v.qkv_sum,
        qv,
        v.out_sum,
        out_shift.reshape(b_out.shape),
        v.fc_sum,
        fc_shift.reshape(b_fc.shape),
        v.proj_sum,
        proj_shift.reshape(b_proj.shape),
    )


def solution(mesh):
    in_specs = (
        P(("dp", "row"), "col"),
        P("dp"),
        P(None, "col"),
        P(None, "col"),
        P(None, "col", "row"),
        P(None, ("row", "col")),
        P("row", "col"),
        P("col"),
        P("col", "row"),
        P(("row", "col")),
        P("row", "col"),
        P("col"),
        P(("dp", "row"), "col"),
    )
    out_specs = (
        P(("dp", "row"), "col"),
        P(("dp", "row"), "col"),
        P(None, "col"),
        P(None, "col"),
        P(None, "col", "row"),
        P(None, ("row", "col")),
        P("row", "col"),
        P("col"),
        P("col", "row"),
        P(("row", "col")),
        P("row", "col"),
        P("col"),
    )
    return jax.shard_map(shards, mesh=mesh, in_specs=in_specs, out_specs=out_specs, check_vma=False)
```

```python
import math
import types

import jax
import jax.numpy as jnp
from jax import lax
from jax.experimental import pallas as pl
from jax.experimental.pallas import tpu as pltpu
from jax.sharding import PartitionSpec as P

D = 1024
HEAD_DIM = 64
EPS = 1e-05
NEGATIVE = -1e30
LOW = jnp.bfloat16
F32 = jnp.float32
FACTOR = 1.0 / math.sqrt(HEAD_DIM)
ROOT = math.sqrt(2.0 / math.pi)
CUBE = 0.044715
COLS = 4
PARTS = 4
OVER_ROWS = (((0,), (0,)), ((), ()))
OVER_COLS = (((1,), (1,)), ((), ()))
PLAIN = (((1,), (0,)), ((), ()))


def swap(value, axis, k):
    return lax.ppermute(value, axis, [(i, i ^ k) for i in range(lax.axis_size(axis))])


def dot(a, b, dims=PLAIN):
    return lax.dot_general(a, b, dims, preferred_element_type=F32)


def arr(shape, dtype=LOW):
    return jax.ShapeDtypeStruct(shape, dtype)


def place():
    return lax.axis_index("col"), lax.rem(lax.axis_index("dp"), PARTS)


def call(body, outs, args, hbm=(), scratch=(), room=None, us=0.001):
    whole = pl.BlockSpec(memory_space=pltpu.VMEM)
    anywhere = pl.BlockSpec(memory_space=pl.ANY)
    held = sum(math.prod(a.shape) * a.dtype.itemsize for a in list(args) + list(outs))
    held += sum(math.prod(a.shape) * 4 for a in scratch if len(a.shape) > 1)
    return pl.pallas_call(
        body,
        out_shape=list(outs),
        in_specs=[anywhere if i in hbm else whole for i in range(len(args))],
        out_specs=[whole] * len(outs),
        scratch_shapes=list(scratch),
        compiler_params=pltpu.CompilerParams(vmem_limit_bytes=room or held + 3 * 1024 * 1024),
        cost_estimate=pl.CostEstimate(
            flops=int(us * 1e9), bytes_accessed=1024, transcendentals=0
        ),
    )(*args)


def run_copies(copies, sems):
    copies = [pltpu.make_async_copy(a, b, sems.at[i]) for i, (a, b) in enumerate(copies)]
    for copy in copies:
        copy.start()
    for copy in copies:
        copy.wait()


def pack(w_qkv, w_fc, w_proj, w_out, gain, shift, b_out, f1, f2, f3, p0, full, sems):
    c, d = place()
    units = w_fc.shape[1] // COLS
    unit = units // PARTS
    quarter = w_out.shape[0] // PARTS
    piece = w_qkv.shape[1] // PARTS
    heads = w_qkv.shape[2] // COLS
    full[...] = jnp.zeros_like(full)
    copies = [(gain, full.at[0:2]), (shift, full.at[2:4]), (b_out, full.at[4:5])]
    for k, f in ((1, f1), (2, f2), (3, f3)):
        rows = pl.ds(pl.multiple_of(d * piece, piece), piece)
        cols = pl.ds(pl.multiple_of((c ^ k) * heads, heads), heads)
        for j in range(3):
            copies.append((w_qkv.at[j, rows, cols], f.at[pl.ds(j * piece, piece)]))
        start = pl.ds(pl.multiple_of((c ^ k) * units + d * unit, unit), unit)
        mine = pl.ds(pl.multiple_of(d * quarter, quarter), quarter)
        copies.append((w_fc.at[:, start], f.at[pl.ds(192, 256)]))
        for j in range(2):
            cols = pl.ds(j * 128, 128)
            copies.append((w_out.at[mine, cols], f.at[pl.ds(448 + j * 128, 128)]))
            copies.append((w_proj.at[start, cols], f.at[pl.ds(704 + j * 128, 128)]))
    run_copies(copies, sems)
    value = full[...]
    high = value.astype(LOW)
    low = (value - high.astype(F32)).astype(LOW).astype(F32)
    high = high.astype(F32)
    rows = jnp.concatenate([high[:, :128], high[:, 128:], low[:, :128], low[:, 128:]], 0)
    rows = rows.astype(LOW)
    p0[...] = rows
    for f in (f1, f2, f3):
        f[960:992, :] = rows


def split_pack(f1, f2, f3, left, right):
    for k, f in enumerate((f1, f2, f3)):
        left[k, 0:96, :] = f[0:96, :]
        right[k, 0:96, :] = f[96:192, :]
        right[k, 96:352, :] = f[192:448, :]
        left[k, 96:352, :] = f[448:704, :]
        left[k, 352:480, :] = f[704:832, :]
        right[k, 352:480, :] = f[832:960, :]


def pair_first(a, b, c, d, qa, wa, qb, wb):
    for i, ref in enumerate((a, b)):
        qa[i] = ref[:, 0:96, :]
        wa[i] = ref[:, 96:480, :]
    for i, ref in enumerate((c, d)):
        qb[i] = ref[:, 0:96, :]
        wb[i] = ref[:, 96:480, :]


def pair(a, b, c, d, left, right):
    left[0] = a[...]
    left[1] = b[...]
    right[0] = c[...]
    right[1] = d[...]


def stack(*refs):
    for i, ref in enumerate(refs[:-1]):
        refs[-1][i] = ref[...]


def norm_parts(blocks):
    total = sum(jnp.sum(b, -1, keepdims=True) for b in blocks)
    squares = sum(jnp.sum(b * b, -1, keepdims=True) for b in blocks)
    mean = total * (1.0 / D)
    factor = lax.rsqrt(squares * (1.0 / D) - mean * mean + EPS)
    return mean, factor


def head_lanes(shape):
    return lax.broadcasted_iota(jnp.int32, shape, 1) < HEAD_DIM


def attention(*refs):
    xo, xs = refs[0], refs[1]
    heads, (qa0, qa1, qb0, qb1, w, b_qv, segment) = refs[2:6], refs[6:13]
    first, x_all, wq, params, qkv, probs, attended, bias, sems = refs[13:22]
    c, d = place()
    piece = 64
    copies = []
    for j in range(3):
        copies.append(
            pltpu.make_async_copy(
                w.at[j, :, pl.ds(pl.multiple_of(c * 128, 128), 128)],
                wq.at[pl.ds(0, 256), pl.ds(j * 128, 128)],
                sems.at[j],
            )
        )
        copies[-1].start()
    for k in range(COLS):
        rows = (heads[k][...] if k == 0 else heads[k][960:992, :]).astype(F32)
        full = rows[0:16] + rows[16:32]
        params[:, k * 256 : k * 256 + 128] = full[0:8]
        params[:, k * 256 + 128 : (k + 1) * 256] = full[8:16]
    lefts = (qa0.at[0], qa0.at[1], qa1.at[0], qa1.at[1])
    rights = (qb0.at[0], qb1.at[0], qb0.at[1], qb1.at[1])
    for m in range(PARTS):
        for k in range(1, COLS):
            start = pl.multiple_of(k * 256 + (d ^ m) * piece, piece)
            both = jnp.concatenate([lefts[m][k - 1], rights[m][k - 1]], 0)
            for j in range(3):
                wq[pl.ds(start, piece), j * 128 : (j + 1) * 128] = both[
                    j * piece : (j + 1) * piece, :
                ]
    for half, srcs in enumerate((xo, xs)):

        @pl.loop(0, 8)
        def _(i):
            rows = pl.ds(pl.multiple_of(i * 32, 32), 32)
            into = pl.ds(pl.multiple_of(half * 256 + i * 32, 32), 32)
            low = [srcs[k, rows, :] for k in range(COLS)]
            blocks = [b.astype(F32) for b in low]
            mean, factor = norm_parts(blocks)
            for k in range(COLS):
                cols = slice(k * 256, (k + 1) * 256)
                out = (blocks[k] - mean) * factor * params[0:1, cols] + params[2:3, cols]
                first[into, cols] = out.astype(LOW)
                x_all[into, cols] = low[k]

    r = lax.axis_index("row")
    ids = segment[...].astype(F32)
    ids = jnp.where(r == 0, ids, jnp.concatenate([ids[:, 256:512], ids[:, 0:256]], 1))
    spot = lax.rem(lax.broadcasted_iota(jnp.int32, (1, 512), 1) + r * 256, 512).astype(F32)
    for i in range(4):
        cols = slice(i * 128, (i + 1) * 128)
        there = [
            jnp.concatenate([jnp.broadcast_to(v[:, cols], (128, 128)).T] * 4, 1)
            for v in (ids, spot)
        ]
        allowed = (there[0] == ids) & (there[1] >= spot)
        bias[cols, :] = jnp.where(allowed, 0.0, NEGATIVE)
    for copy in copies:
        copy.wait()
    added = jnp.concatenate([b_qv[0:1, :], jnp.zeros((1, 128), F32), b_qv[1:2, :]], 1)

    @pl.loop(0, 4)
    def _(i):
        rows = pl.ds(pl.multiple_of(i * 128, 128), 128)
        qkv[rows, :] = (dot(first[rows, :], wq[...]) + added).astype(LOW)

    @pl.loop(0, 4)
    def _(i):
        rows = pl.ds(pl.multiple_of(i * 128, 128), 128)
        lanes = head_lanes((128, 128))
        query = qkv[rows, 0:128]
        keys = qkv[:, 128:256]
        values = qkv[:, 256:384]
        outs = []
        for h in range(2):
            mine = jnp.where(lanes == (h == 0), query, jnp.zeros_like(query))
            score = dot(mine, keys, OVER_COLS) * FACTOR + bias[rows, :]
            expo = jnp.exp(score - jnp.max(score, -1, keepdims=True))
            weights = expo / jnp.sum(expo, -1, keepdims=True)
            probs[h, rows, :] = weights
            outs.append(dot(weights.astype(LOW), values))
        attended[rows, :] = jnp.where(lanes, outs[0], outs[1]).astype(LOW)


def by_part(a0, a1, b0, b1):
    return (
        (a0.at[0], a0.at[1], a1.at[0], a1.at[1]),
        (b0.at[0], b1.at[0], b0.at[1], b1.at[1]),
    )


def join_weights(w_out, w_fc, w_proj, a0, a1, b0, b1, out, fc, proj, sems):
    c, d = place()
    copies = [(w_out, out.at[:, pl.ds(0, 256)])]
    for m in range(PARTS):
        start = pl.ds(pl.multiple_of(c * 512 + (d ^ m) * 128, 128), 128)
        copies.append((w_fc.at[:, start], fc.at[pl.ds(0, 256), pl.ds(m * 128, 128)]))
        copies.append((w_proj.at[start], proj.at[pl.ds(m * 128, 128), pl.ds(0, 256)]))
    copies = [pltpu.make_async_copy(a, b, sems.at[i]) for i, (a, b) in enumerate(copies)]
    for copy in copies:
        copy.start()
    lefts, rights = by_part(a0, a1, b0, b1)
    for m in range(PARTS):
        rows = pl.ds(pl.multiple_of((d ^ m) * 128, 128), 128)
        mine = slice(m * 128, (m + 1) * 128)
        for k in range(1, COLS):
            one, two = slice(k * 256, k * 256 + 128), slice(k * 256 + 128, (k + 1) * 256)
            out[rows, one] = lefts[m][k - 1, 0:128, :]
            out[rows, two] = lefts[m][k - 1, 128:256, :]
            fc[k * 256 : (k + 1) * 256, mine] = rights[m][k - 1, 0:256, :]
            proj[mine, one] = lefts[m][k - 1, 256:384, :]
            proj[mine, two] = rights[m][k - 1, 256:384, :]
    for copy in copies:
        copy.wait()


def forward(*refs):
    mine, theirs = refs[0:2]
    w_own, w_sib, x_all, params, fc, b_fc = refs[2:8]
    att_own, middle, second, hidden, mid_own, att_sib, shift = refs[8:15]
    c, d = place()
    for m in range(PARTS):
        here = pl.ds(pl.multiple_of((d ^ m) * 128, 128), 128)
        shift[0:1, m * 128 : (m + 1) * 128] = b_fc[0:1, here]
    for k in range(COLS):
        cols = pl.ds(pl.multiple_of((c ^ k) * 128, 128), 128)
        att_own[:, cols] = mine[k]
        att_sib[0:256, cols] = theirs[k, 256:512, :]
        att_sib[256:512, cols] = theirs[k, 0:256, :]

    @pl.loop(0, 4)
    def _(i):
        rows = pl.ds(pl.multiple_of(i * 128, 128), 128)
        value = dot(att_own[rows, :], w_own[...]) + dot(att_sib[rows, :], w_sib[...])
        value = value + x_all[rows, :].astype(F32) + params[4:5, :]
        middle[rows, :] = value
        mean, factor = norm_parts([value])
        out = (value - mean) * factor * params[1:2, :] + params[3:4, :]
        second[rows, :] = out.astype(LOW)
        hidden[rows, :] = dot(second[rows, :], fc[...]) + shift[0:1, :]

    mid_own[...] = middle[0:256, 0:256]


def backward(*refs):
    co, cs = refs[0:2]
    middle, hidden, fc, proj, params = refs[2:7]
    cot, active, grad_hidden, back, send, sums, fc_shift, cot_shift, shift = refs[7:16]
    for k in range(COLS):
        cols = slice(k * 256, (k + 1) * 256)
        cot[0:256, cols] = co[k]
        cot[256:512, cols] = cs[k]
    sums[...] = jnp.zeros_like(sums)
    shift[...] = jnp.zeros_like(shift)
    cot_shift[...] = jnp.sum(cot[:, 0:256].astype(F32), 0, keepdims=True)

    def step(start):
        rows = pl.ds(pl.multiple_of(start, 128), 128)
        v = hidden[rows, :]
        t = jnp.tanh(ROOT * (v + CUBE * (v * v * v)))
        active[rows, :] = (0.5 * v * (1.0 + t)).astype(LOW)
        slope = 0.5 * (1.0 + t) + 0.5 * v * (1.0 - t * t) * (ROOT * (1.0 + 3.0 * CUBE * (v * v)))
        low = (dot(cot[rows, :], proj[...], OVER_COLS) * slope).astype(LOW)
        grad_hidden[rows, :] = low
        shift[0:1, :] += jnp.sum(low.astype(F32), 0, keepdims=True)
        grad = dot(low, fc[...], OVER_COLS)
        mean, factor = norm_parts([middle[rows, :]])
        normed = (middle[rows, :] - mean) * factor
        sums[0:1, :] += jnp.sum(grad * normed, 0, keepdims=True)
        sums[1:2, :] += jnp.sum(grad, 0, keepdims=True)
        scaled = grad * params[1:2, :]
        one = jnp.mean(scaled, -1, keepdims=True)
        two = jnp.mean(scaled * normed, -1, keepdims=True)
        return factor * (scaled - one - normed * two)

    @pl.loop(0, 2)
    def _(i):
        send[pl.ds(pl.multiple_of(i * 128, 128), 128), :] = step(256 + i * 128).astype(LOW)

    @pl.loop(0, 2)
    def _(i):
        back[pl.ds(pl.multiple_of(i * 128, 128), 128), :] = step(i * 128)

    c, d = place()
    for m in range(PARTS):
        here = pl.ds(pl.multiple_of((d ^ m) * 128, 128), 128)
        fc_shift[0:1, here] = shift[0:1, m * 128 : (m + 1) * 128]


def mlp_grads(second, grad_hidden, active, cot, proj, fk, fs, pk, ps, mine, left, right):
    for k in range(COLS):
        cols = slice(k * 256, (k + 1) * 256)
        value = dot(second[:, cols], grad_hidden[...], OVER_ROWS).astype(LOW)
        for m in range(PARTS):
            (fs if m % 2 else fk)[m // 2, cols, :] = value[:, m * 128 : (m + 1) * 128]
    for m in range(PARTS):
        value = dot(active[:, m * 128 : (m + 1) * 128], cot[...], OVER_ROWS).astype(LOW)
        for i in range(2 * COLS):
            rows = slice(i * 128, (i + 1) * 128)
            (ps if m // 2 else pk)[m % 2, rows, :] = value[:, rows]
    mine[...] = dot(active[0:256, :], proj[...])
    theirs = dot(active[256:512, :], proj[...]).astype(LOW)
    left[...] = theirs[:, 0:512]
    right[...] = theirs[:, 512:1024]


def first_add(ka, ra, kb, rb, ha, sa, hb, sb):
    for keep, got, have, send in ((ka, ra, ha, sa), (kb, rb, hb, sb)):
        have[...] = keep[0].astype(F32) + got[0].astype(F32)
        send[...] = (keep[1].astype(F32) + got[1].astype(F32)).astype(LOW)


def second_add_mlp(ha, ra, hb, rb, *outs):
    for k, out in enumerate(outs):
        rows = slice(k * 256, (k + 1) * 256)
        out[0:256, :] = (ha[rows, :] + ra[rows, :].astype(F32)).astype(LOW)
        out[256:512, :] = (hb[rows, :] + rb[rows, :].astype(F32)).astype(LOW)


def second_add_qkv(ha, ra, hb, rb, *outs):
    for k, out in enumerate(outs[:-1]):
        have, got = (ha, ra) if k < 2 else (hb, rb)
        rows = slice((k % 2) * 192, (k % 2) * 192 + 192)
        out[...] = (have[rows, :] + got[rows, :].astype(F32)).astype(LOW)
    for j, (have, got) in enumerate(((ha, ra), (hb, rb))):
        value = have[384:512, :] + got[384:512, :].astype(F32)
        outs[-1][j * 128 : (j + 1) * 128, :] = value.astype(LOW)


def split_sum(back, got, o0, o1, o2, o3):
    for k, out in enumerate((o0, o1, o2, o3)):
        cols = slice(k * 256, (k + 1) * 256)
        out[...] = (back[:, cols] + got[:, cols].astype(F32)).astype(out.dtype)


def middle_sum(cot, o0, g1, g2, g3, out, low):
    value = cot[...].astype(F32) + (
        o0[...] + g1[...].astype(F32) + g2[...].astype(F32) + g3[...].astype(F32)
    )
    out[...] = value
    low[...] = value.astype(LOW)


def mixed_sum(middle, o0, g1, g2, g3, b_proj, out):
    value = o0[...] + g1[...].astype(F32) + g2[...].astype(F32) + g3[...].astype(F32)
    out[...] = (middle[...] + value + b_proj[...]).astype(LOW)


def grad_out(own, other, w_out, o0, o1, o2, o3):
    c, d = place()
    for k, out in enumerate((o0, o1, o2, o3)):
        rows = pl.ds(pl.multiple_of((c ^ k) * 128, 128), 128)
        w = w_out[rows, :]
        out[0:256, :] = dot(own[...], w, OVER_COLS).astype(out.dtype)
        out[256:512, :] = dot(other[...], w, OVER_COLS).astype(out.dtype)


def out_weight(att, own, other, mix, left, right, out, shift, o0, o1, o2, o3):
    for k, part in enumerate((o0, o1, o2, o3)):
        cols = slice((k % 2) * 256, (k % 2 + 1) * 256)
        total = mix[:, k * 256 : (k + 1) * 256] + (left, right)[k // 2][:, cols].astype(F32)
        part[...] = total.astype(part.dtype)
    out[...] = (
        dot(att[0:256, :], own[...], OVER_ROWS) + dot(att[256:512, :], other[...], OVER_ROWS)
    ).astype(LOW)
    shift[...] = jnp.sum(own[...].astype(F32), 0, keepdims=True) + jnp.sum(
        other[...].astype(F32), 0, keepdims=True
    )


def sum_datt(o0, g1, g2, g3, out):
    value = o0[...] + g1[...].astype(F32) + g2[...].astype(F32) + g3[...].astype(F32)
    out[...] = value.astype(LOW)


def attention_back(*refs):
    datt, qkv, probs, wq, x_all, params, sums2 = refs[0:7]
    dqkv, back, send, qv_shift = refs[7:11]
    scores, lows, sums = refs[11:14]

    @pl.loop(0, 4)
    def _(i):
        rows = pl.ds(pl.multiple_of(i * 128, 128), 128)
        lanes = head_lanes((128, 128))
        keys = qkv[:, 128:256]
        values = qkv[:, 256:384]
        grad = datt[rows, :]
        outs = []
        for h in range(2):
            mine = jnp.where(lanes == (h == 0), grad, jnp.zeros_like(grad))
            gp = dot(mine, values, OVER_COLS)
            weights = probs[h, rows, :]
            centre = jnp.sum(weights * gp, -1, keepdims=True)
            score = (weights * (gp - centre)).astype(LOW)
            scores[h, rows, :] = score
            lows[h, rows, :] = weights.astype(LOW)
            outs.append(dot(score, keys))
        dqkv[rows, 0:128] = (jnp.where(lanes, outs[0], outs[1]) * FACTOR).astype(LOW)

    lanes = head_lanes((512, 128))
    gk = [dot(scores[h], qkv[:, 0:128], OVER_ROWS) for h in range(2)]
    dqkv[:, 128:256] = (jnp.where(lanes, gk[0], gk[1]) * FACTOR).astype(LOW)
    gv = [dot(lows[h], datt[...], OVER_ROWS) for h in range(2)]
    dqkv[:, 256:384] = jnp.where(lanes, gv[0], gv[1]).astype(LOW)
    qv_shift[...] = jnp.sum(dqkv[...].astype(F32), 0, keepdims=True)
    sums[...] = jnp.zeros_like(sums)

    def step(start):
        rows = pl.ds(pl.multiple_of(start, 128), 128)
        grad = dot(dqkv[rows, :], wq[...], OVER_COLS)
        x = x_all[rows, :].astype(F32)
        mean, factor = norm_parts([x])
        normed = (x - mean) * factor
        sums[0:1, :] += jnp.sum(grad * normed, 0, keepdims=True)
        sums[1:2, :] += jnp.sum(grad, 0, keepdims=True)
        scaled = grad * params[0:1, :]
        one = jnp.mean(scaled, -1, keepdims=True)
        two = jnp.mean(scaled * normed, -1, keepdims=True)
        return factor * (scaled - one - normed * two)

    @pl.loop(0, 2)
    def _(i):
        send[pl.ds(pl.multiple_of(i * 128, 128), 128), :] = step(256 + i * 128).astype(LOW)

    @pl.loop(0, 2)
    def _(i):
        back[pl.ds(pl.multiple_of(i * 128, 128), 128), :] = step(i * 128)

    rows = jnp.concatenate(
        [sums[0:1, :], sums2[0:1, :], sums[1:2, :], sums2[1:2, :], jnp.zeros((4, D), F32)], 0
    )
    back[256:264, :] = rows
    high = rows.astype(LOW).astype(F32)
    send[256:272, :] = jnp.concatenate([high, rows - high], 0).astype(LOW)


def split_last(back, got, o0, s0, o1, o2, o3):
    more = got[256:272, :].astype(F32)
    sums = back[256:264, :] + more[0:8] + more[8:16]
    high = sums.astype(LOW).astype(F32)
    both = jnp.concatenate([high, sums - high], 0).astype(LOW)
    o0[...] = back[0:256, 0:256] + got[0:256, 0:256].astype(F32)
    s0[...] = sums[:, 0:256]
    for k, out in ((1, o1), (2, o2), (3, o3)):
        cols = slice(k * 256, (k + 1) * 256)
        out[0:256, :] = (back[0:256, cols] + got[0:256, cols].astype(F32)).astype(LOW)
        out[256:272, :] = both[:, cols]


def last_sum(o0, s0, g1, g2, g3, middle, out, sums):
    out[...] = middle[...] + (
        o0[...]
        + g1[0:256, :].astype(F32)
        + g2[0:256, :].astype(F32)
        + g3[0:256, :].astype(F32)
    )
    value = s0[...]
    for g in (g1, g2, g3):
        more = g[256:272, :].astype(F32)
        value = value + more[0:8] + more[8:16]
    sums[...] = value


def qkv_weight(first, dqkv, w_out, ak, as_, bk, bs, full):
    c, d = place()

    @pl.loop(0, 4)
    def _(k):
        cols = pl.ds(pl.multiple_of(k * 256, 256), 256)
        full[cols, :] = dot(first[:, cols], dqkv[...], OVER_ROWS)

    for m in range(PARTS):
        outs = ((as_ if m % 2 else ak, m // 2), (bs if m // 2 else bk, m % 2))
        rows = pl.ds(pl.multiple_of((d ^ m) * 128, 128), 128)
        for j, (out, index) in enumerate(outs):
            out[index, 384:512, :] = w_out[rows, j * 128 : (j + 1) * 128]
        for k in range(COLS):
            out, index = outs[k // 2]
            start = pl.ds(pl.multiple_of(k * 256 + (d ^ m) * 64, 64), 64)
            for j in range(3):
                row = (k % 2) * 192 + j * 64
                out[index, row : row + 64, :] = full[start, j * 128 : (j + 1) * 128].astype(LOW)


def unpack_qkv(a0, a1, b0, b1, out, w_out, gain, shift, b_qv, b_out, b_fc, b_proj):
    c, d = place()
    lefts, rights = by_part(a0, a1, b0, b1)
    for m in range(PARTS):
        rows = pl.ds(pl.multiple_of((d ^ m) * 64, 64), 64)
        for k in range(COLS):
            src = (lefts if k < 2 else rights)[m]
            cols = pl.ds(pl.multiple_of((c ^ k) * 128, 128), 128)
            for j in range(3):
                start = (k % 2) * 192 + j * 64
                out[j, rows, cols] = src[start : start + 64, :].astype(F32)
        rows = pl.ds(pl.multiple_of((d ^ m) * 128, 128), 128)
        w_out[rows, 0:128] = lefts[m][384:512, :].astype(F32)
        w_out[rows, 128:256] = rights[m][384:512, :].astype(F32)
    total = sum(left[512:576, :].astype(F32) for left in lefts)
    total = total[0:32] + total[32:64]
    for j, rows in enumerate((total[0:16], total[16:32])):
        cols = slice(j * 128, (j + 1) * 128)
        gain[:, cols] = rows[0:2]
        shift[:, cols] = rows[2:4]
        b_out[:, cols] = rows[4:5]
        b_proj[:, cols] = rows[5:6]
        b_qv[j : j + 1, :] = rows[6:7]
        b_fc[0:1, j * 128 : (j + 1) * 128] = rows[7:8]
        b_fc[0:1, 256 + j * 128 : 256 + (j + 1) * 128] = rows[8:9]


def unpack_mlp(a0, a1, b0, b1, fc, proj):
    c, d = place()
    lefts, rights = by_part(a0, a1, b0, b1)
    for m in range(PARTS):
        for k in range(COLS):
            here = pl.ds(pl.multiple_of((c ^ k) * 512 + (d ^ m) * 128, 128), 128)
            fc[:, here] = lefts[m][k * 256 : (k + 1) * 256, :].astype(F32)
            for j in range(2):
                row = k * 256 + j * 128
                cols = slice(j * 128, (j + 1) * 128)
                proj[here, cols] = rights[m][row : row + 128, :].astype(F32)


def join_mlp(m0, m1, m2, m3, left, right):
    for k, part in enumerate((m0, m1, m2, m3)):
        rows = slice(k * 256, (k + 1) * 256)
        left[rows, :] = part[0:256, :]
        right[rows, :] = part[256:512, :]


def join_qkv(q0, q1, q2, q3, w_out, small, left, right):
    for j, (out, one, two) in enumerate(((left, q0, q1), (right, q2, q3))):
        out[0:192, :] = one[...]
        out[192:384, :] = two[...]
        out[384:512, :] = w_out[j * 128 : (j + 1) * 128, :]
    full = small[...]
    high = full.astype(LOW).astype(F32)
    low = full - high
    rows = [high[:, 0:128], high[:, 128:256], low[:, 0:128], low[:, 128:256]]
    left[512:576, :] = jnp.concatenate(rows, 0).astype(LOW)


def small_pack(sums, out_shift, cot_shift, qv, fc_shift, out):
    out[0:4, :] = sums[0:4, :]
    out[4:5, :] = out_shift[...]
    out[5:6, :] = cot_shift[...]
    out[6:7, 0:128] = qv[0:1, 0:128]
    out[6:7, 128:256] = qv[0:1, 256:384]
    out[7:8, :] = fc_shift[0:1, 0:256]
    out[8:9, :] = fc_shift[0:1, 256:512]
    out[9:16, :] = jnp.zeros((7, 256), F32)


def after(value, *others):
    return lax.optimization_barrier((value, others))[0]


def high_bits():
    return [1 << b for b in range(2, int(math.log2(lax.axis_size("dp"))))]


def over_high(parts):
    for k in high_bits():
        parts = [(o.astype(F32) + swap(o, "dp", k).astype(F32)).astype(LOW) for o in parts]
    return parts


def three(parts, axis="col"):
    return [swap(part, axis, k + 1) for k, part in enumerate(parts)]


def pair_arrays(left, right):
    return [arr((2,) + left.shape), arr((2,) + right.shape)]


def shards(
    tokens,
    segment,
    ln_gain,
    ln_bias,
    w_qkv,
    b_qv,
    w_out,
    b_out,
    w_fc,
    b_fc,
    w_proj,
    b_proj,
    cotangent,
):
    half, width = tokens.shape
    group = 2 * half
    dma = pltpu.SemaphoreType.DMA
    last = []
    v = types.SimpleNamespace(mixed=[])

    def run(body, outs, args, **keys):
        results = call(body, outs, after(list(args), last), **keys)
        last[:] = results[:1]
        return results

    def now(value):
        return after(value, last)

    def send_pair(left, right, one, two):
        left, right = now([left, right])
        return swap(left, "dp", one), swap(right, "dp", two)

    def join_pair(left, one, right, two):
        return run(pair, pair_arrays(left, right), [left, one, right, two])

    def first_sum(ka, kb, got):
        rows = ka.shape[1]
        outs = [arr((rows, 128), F32), arr((rows, 128))] * 2
        return run(first_add, outs, [ka, got[0], kb, got[1]])

    def split(back, got):
        outs = [arr((half, width), F32)] + [arr((half, width))] * 3
        return run(split_sum, outs, [back, got])

    def pack_all():
        *v.sent, v.head = run(
            pack,
            [arr((992, 128))] * 3 + [arr((32, 128))],
            [w_qkv, w_fc, w_proj, w_out, ln_gain, ln_bias, b_out.reshape(1, width)],
            hbm=range(7),
            scratch=[pltpu.VMEM((8, width), F32), dma((27,))],
            room=56 * 1024 * 1024,
        )

    def send_weights():
        v.f = three(now(v.sent))

    def split_weights():
        v.wa, v.wb = run(split_pack, [arr((3, 480, 128))] * 2, v.f)

    def send_tokens():
        v.x = three([now(tokens)] * 3)

    def send_weights_first():
        v.w1 = send_pair(v.wa, v.wb, 1, 2)

    def pair_weights_first():
        v.qa, v.wa, v.qb, v.wb = run(
            pair_first,
            [arr((2, 3, 96, 128)), arr((2, 3, 384, 128))] * 2,
            [v.wa, v.w1[0], v.wb, v.w1[1]],
        )

    def send_qkv_two():
        v.q2 = send_pair(v.qa, v.qb, 2, 1)

    def stack_tokens():
        outs = [arr((4, half, width))]
        v.x_own = run(stack, outs, [tokens, *v.x], us=50.0)[0]

    def swap_tokens():
        v.x_sib = swap(now(v.x_own), "row", 1)

    def send_cotangent():
        v.cot = three([now(cotangent)] * 3)

    def attend():
        (
            v.first,
            v.x_all,
            v.wq,
            v.params,
            v.qkv,
            v.probs,
            v.attended,
        ) = run(
            attention,
            [
                arr((group, D)),
                arr((group, D)),
                arr((D, 384)),
                arr((8, D), F32),
                arr((group, 384)),
                arr((2, group, group), F32),
                arr((group, 128)),
            ],
            [
                v.x_own,
                v.x_sib,
                v.head,
                *v.f,
                v.qa,
                v.q2[0],
                v.qb,
                v.q2[1],
                w_qkv,
                b_qv,
                segment.reshape(1, group),
            ],
            hbm=(10,),
            scratch=[pltpu.VMEM((group, group), F32), dma((3,))],
            us=50.0,
        )

    def send_weights_two():
        v.w2 = send_pair(v.wa, v.wb, 2, 1)

    def stack_cotangent():
        outs = [arr((4, half, width))]
        v.cot_own = run(stack, outs, [cotangent, *v.cot])[0]

    def swap_cotangent():
        v.cot_sib = swap(now(v.cot_own), "row", 1)

    def send_attended():
        v.att = three([now(v.attended)] * 3)

    def stack_attended():
        outs = [arr((4, group, 128))]
        v.att_four = run(stack, outs, [v.attended, *v.att])[0]

    def swap_attended():
        v.att_sib = swap(now(v.att_four), "row", 1)

    def join_all():
        v.w_own, v.fc, v.proj = run(
            join_weights,
            [arr((512, D)), arr((D, 512)), arr((512, D))],
            [w_out, w_fc, w_proj, v.wa, v.w2[0], v.wb, v.w2[1]],
            hbm=(0, 1, 2),
            scratch=[dma((9,))],
        )

    def swap_w_out():
        v.w_sib = swap(now(v.w_own), "row", 1)

    def feed_forward():
        v.att_own, v.middle, v.second, v.hidden, v.mid_own = run(
            forward,
            [
                arr((group, 512)),
                arr((group, D), F32),
                arr((group, D)),
                arr((group, 512), F32),
                arr((half, width), F32),
            ],
            [
                v.att_four,
                v.att_sib,
                v.w_own,
                v.w_sib,
                v.x_all,
                v.params,
                v.fc,
                b_fc.reshape(1, 512),
            ],
            scratch=[pltpu.VMEM((group, 512), LOW), pltpu.VMEM((8, 512), F32)],
        )

    def feed_back():
        (
            v.cot_all,
            v.active,
            v.grad_hidden,
            v.back,
            v.send,
            v.sums2,
            v.fc_shift,
            v.cot_shift,
        ) = run(
            backward,
            [
                arr((group, D)),
                arr((group, 512)),
                arr((group, 512)),
                arr((half, D), F32),
                arr((half, D)),
                arr((2, D), F32),
                arr((1, 512), F32),
                arr((1, width), F32),
            ],
            [v.cot_own, v.cot_sib, v.middle, v.hidden, v.fc, v.proj, v.params],
            scratch=[pltpu.VMEM((8, 512), F32)],
        )

    def swap_second():
        v.got = swap(now(v.send), "row", 1)

    def mlp_weights():
        v.fk, v.fs, v.pk, v.ps, v.mix, *v.mix_send = run(
            mlp_grads,
            [arr((2, 1024, 128))] * 4 + [arr((half, D), F32)] + [arr((half, D // 2))] * 2,
            [v.second, v.grad_hidden, v.active, v.cot_all, v.proj],
        )

    def send_mlp_one():
        v.m1 = send_pair(v.fs, v.ps, 1, 2)

    def split_second():
        v.own, *v.parts = split(v.back, v.got)

    def send_second():
        v.mid = three(now(v.parts))

    def sum_second():
        v.grad_middle, v.branch = run(
            middle_sum,
            [arr((half, width), F32), arr((half, width))],
            [cotangent, v.own, *v.mid],
            us=2.0,
        )

    def swap_branch():
        v.other = swap(now(v.branch), "row", 1)

    def swap_mixed():
        v.mix_got = [swap(part, "row", 1) for part in now(v.mix_send)]

    def back_out():
        v.att_sum, *v.att_parts = run(
            grad_out,
            [arr((group, 128), F32)] + [arr((group, 128))] * 3,
            [v.branch, v.other, w_out],
        )

    def send_back_out():
        v.datt = three(now(v.att_parts))

    def weigh_out():
        v.out_grad, v.out_shift, v.mix, *v.mix_parts = run(
            out_weight,
            [arr(w_out.shape), arr((1, width), F32), arr((half, width), F32)]
            + [arr((half, width))] * 3,
            [v.att_own, v.branch, v.other, v.mix, *v.mix_got],
        )

    def add_mlp_one():
        v.ha, v.sa, v.hb, v.sb = first_sum(v.fk, v.pk, v.m1)

    def send_mlp_two():
        v.m2 = send_pair(v.sa, v.sb, 2, 1)

    def sum_attended():
        v.att_sum = run(
            sum_datt, [arr((group, 128))], [v.att_sum, *v.datt], us=2.0
        )[0]

    def add_mlp_two():
        ms = run(
            second_add_mlp,
            [arr((512, 128))] * 4,
            [v.ha, v.m2[0], v.hb, v.m2[1]],
        )
        v.ms = over_high(ms)

    def send_mlp_cols():
        v.mz = three(now(v.ms[1:]))

    def attend_back():
        v.dqkv, v.back, v.send, v.qv_shift = run(
            attention_back,
            [
                arr((group, 384)),
                arr((half + 8, D), F32),
                arr((half + 16, D)),
                arr((1, 384), F32),
            ],
            [v.att_sum, v.qkv, v.probs, v.wq, v.x_all, v.params, v.sums2],
            scratch=[
                pltpu.VMEM((2, group, group), LOW),
                pltpu.VMEM((2, group, group), LOW),
                pltpu.VMEM((8, D), F32),
            ],
            us=50.0,
        )

    def swap_first():
        v.got = swap(now(v.send), "row", 1)

    def qkv_weights():
        v.ak, v.as_, v.bk, v.bs = run(
            qkv_weight,
            [arr((2, 512, 128))] * 4,
            [v.first, v.dqkv, v.out_grad],
            scratch=[pltpu.VMEM((D, 384), F32)],
        )

    def send_grad_one():
        v.g1 = send_pair(v.as_, v.bs, 1, 2)

    def add_grad_one():
        v.ga, v.gs, v.gb, v.gt = first_sum(v.ak, v.bk, v.g1)

    def send_grad_two():
        v.g2 = send_pair(v.gs, v.gt, 2, 1)

    def add_grad_two():
        outs = run(
            second_add_qkv,
            [arr((192, 128))] * 4 + [arr((256, 128))],
            [v.ga, v.g2[0], v.gb, v.g2[1]],
        )
        *v.qs, v.out_part = over_high(outs)

    def send_grad_cols():
        v.qz = three(now(v.qs[1:]))

    def join_grad():
        v.ga, v.gb = run(
            join_qkv,
            [arr((576, 128)), arr((512, 128))],
            [v.qs[0], *v.qz, v.out_part, v.small],
        )

    def send_grad_three():
        v.g3 = send_pair(v.ga, v.gb, 1, 2)

    def pair_grad():
        v.ga, v.gb = join_pair(v.ga, v.g3[0], v.gb, v.g3[1])

    def send_grad_four():
        v.g4 = send_pair(v.ga, v.gb, 2, 1)

    def join_mlp_cols():
        v.ma, v.mb = run(
            join_mlp, [arr((1024, 128))] * 2, [v.ms[0], *v.mz], us=50.0
        )

    def send_mlp_three():
        v.m3 = send_pair(v.ma, v.mb, 1, 2)

    def pair_mlp():
        v.ma, v.mb = join_pair(v.ma, v.m3[0], v.mb, v.m3[1])

    def send_mlp_four():
        v.m4 = send_pair(v.ma, v.mb, 2, 1)

    def split_first():
        v.last_own, v.last_sums, *v.last_parts = run(
            split_last,
            [arr((half, width), F32), arr((8, width), F32)] + [arr((half + 16, width))] * 3,
            [v.back, v.got],
        )

    def send_first():
        v.last = three(now(v.last_parts))

    def sum_first():
        v.grad_tokens, v.sums = run(
            last_sum,
            [arr((half, width), F32), arr((8, width), F32)],
            [v.last_own, v.last_sums, *v.last, v.grad_middle],
            us=50.0,
        )

    def send_mixed(k):
        part = now(v.mix_parts[k - 1])
        v.mixed = v.mixed + [swap(part, "col", k)]

    def send_mixed_one():
        send_mixed(1)

    def send_mixed_two():
        send_mixed(2)

    def send_mixed_three():
        send_mixed(3)

    def sum_mixed():
        v.mixed_out = run(
            mixed_sum,
            [arr((half, width))],
            [v.mid_own, v.mix, *v.mixed, b_proj.reshape(1, width)],
        )[0]

    def pack_small():
        v.small = run(
            small_pack,
            [arr((16, width), F32)],
            [v.sums, v.out_shift, v.cot_shift, v.qv_shift, v.fc_shift],
        )[0]
        for k in high_bits():
            v.small = v.small + swap(v.small, "dp", k)

    def unpack_mlp_all():
        v.fc_sum, v.proj_sum = run(
            unpack_mlp,
            [arr(w_fc.shape, F32), arr(w_proj.shape, F32)],
            [v.ma, v.m4[0], v.mb, v.m4[1]],
        )

    def unpack_grad():
        v.qkv_sum, v.out_sum, *v.outs = run(
            unpack_qkv,
            [
                arr(w_qkv.shape, F32),
                arr(w_out.shape, F32),
                arr((2, width), F32),
                arr((2, width), F32),
                arr(b_qv.shape, F32),
                arr((1, width), F32),
                arr((1, 512), F32),
                arr((1, width), F32),
            ],
            [v.ga, v.g4[0], v.gb, v.g4[1]],
        )

    order = (
        pack_all,
        send_weights,
        split_weights,
        send_tokens,
        send_weights_first,
        pair_weights_first,
        send_qkv_two,
        stack_tokens,
        swap_tokens,
        send_cotangent,
        send_weights_two,
        attend,
        send_attended,
        stack_cotangent,
        swap_cotangent,
        stack_attended,
        swap_attended,
        join_all,
        swap_w_out,
        feed_forward,
        feed_back,
        swap_second,
        mlp_weights,
        send_mlp_one,
        split_second,
        send_second,
        sum_second,
        swap_branch,
        swap_mixed,
        back_out,
        send_back_out,
        weigh_out,
        add_mlp_one,
        send_mlp_two,
        sum_attended,
        add_mlp_two,
        send_mlp_cols,
        attend_back,
        swap_first,
        qkv_weights,
        send_grad_one,
        join_mlp_cols,
        split_first,
        send_first,
        add_grad_one,
        send_grad_two,
        add_grad_two,
        send_mlp_three,
        sum_first,
        send_grad_cols,
        pack_small,
        pair_mlp,
        send_mlp_four,
        join_grad,
        send_grad_three,
        send_mixed_two,
        unpack_mlp_all,
        send_mixed_three,
        send_mixed_one,
        pair_grad,
        send_grad_four,
        unpack_grad,
        sum_mixed,
    )
    for step in order:
        step()
    gain, shift, qv, out_shift, fc_shift, proj_shift = v.outs
    return (
        v.mixed_out,
        v.grad_tokens,
        gain,
        shift,
        v.qkv_sum,
        qv,
        v.out_sum,
        out_shift.reshape(b_out.shape),
        v.fc_sum,
        fc_shift.reshape(b_fc.shape),
        v.proj_sum,
        proj_shift.reshape(b_proj.shape),
    )


def solution(mesh):
    in_specs = (
        P(("dp", "row"), "col"),
        P("dp"),
        P(None, "col"),
        P(None, "col"),
        P(None, "col", "row"),
        P(None, ("row", "col")),
        P("row", "col"),
        P("col"),
        P("col", "row"),
        P(("row", "col")),
        P("row", "col"),
        P("col"),
        P(("dp", "row"), "col"),
    )
    out_specs = (
        P(("dp", "row"), "col"),
        P(("dp", "row"), "col"),
        P(None, "col"),
        P(None, "col"),
        P(None, "col", "row"),
        P(None, ("row", "col")),
        P("row", "col"),
        P("col"),
        P("col", "row"),
        P(("row", "col")),
        P("row", "col"),
        P("col"),
    )
    return jax.shard_map(shards, mesh=mesh, in_specs=in_specs, out_specs=out_specs, check_vma=False)
```
